32 devices in a mesh: batch: 4 (over y, x), seq: 8 (over z, core).
Axes of the slice: x: 2, y: 2, z: 4, core: 2. Of those that a mesh axis runs over, the one named last changes fastest.
Arguments:
- layer_input: bfloat16 [4, 1024, 1024], P('batch', 'seq'), may hold values from -6 to 6
- segment_ids: int32 [4, 1024], P('batch', 'seq'), may hold values from 0 to 7, never falling along the last dimension, each value on 1 to 512 neighbouring positions
- out_cotangent: bfloat16 [4, 1024, 1024], P('batch', 'seq'), may hold values from -6 to 6
- key_weight: bfloat16 [1024, 1024], P(('batch', 'seq')), may hold values from -0.1875 to 0.1875
- value_weight: bfloat16 [1024, 1024], P(('batch', 'seq')), may hold values from -0.1875 to 0.1875
- recept_weight: bfloat16 [1024, 1024], P(('batch', 'seq')), may hold values from -0.1875 to 0.1875
- output_weight: bfloat16 [1024, 1024], P(('batch', 'seq')), may hold values from -0.75 to 0.75
- channel_key: bfloat16 [1024, 4096], P(('batch', 'seq')), may hold values from -0.1875 to 0.1875
- channel_value: bfloat16 [4096, 1024], P(('batch', 'seq')), may hold values from -0.09375 to 0.09375
- channel_recept: bfloat16 [1024, 1024], P(('batch', 'seq')), may hold values from -0.1875 to 0.1875
- norm_gains: bfloat16 [2, 1024], P(None, ('batch', 'seq')), may hold values from 0.5 to 1.5
- norm_offsets: bfloat16 [2, 1024], P(None, ('batch', 'seq')), may hold values from -1.5 to 1.5
- mix_coeffs: bfloat16 [5, 1024], P(None, ('batch', 'seq')), may hold values from 0.049804688 to 0.94921875
- time_decay: bfloat16 [1024], P(('batch', 'seq')), may hold values from -7.59375 to -2.296875
- time_first: bfloat16 [1024], P(('batch', 'seq')), may hold values from -1 to 1
Outputs:
- block_output: bfloat16 [4, 1024, 1024], P('batch', 'seq')
- input_grad: float32 [4, 1024, 1024], P('batch', 'seq')
- key_grad: float32 [1024, 1024], P(('batch', 'seq'))
- value_grad: float32 [1024, 1024], P(('batch', 'seq'))
- recept_grad: float32 [1024, 1024], P(('batch', 'seq'))
- output_grad: float32 [1024, 1024], P(('batch', 'seq'))
- channel_key_grad: float32 [1024, 4096], P(('batch', 'seq'))
- channel_value_grad: float32 [4096, 1024], P(('batch', 'seq'))
- channel_recept_grad: float32 [1024, 1024], P(('batch', 'seq'))
- gains_grad: float32 [2, 1024], P(None, ('batch', 'seq'))
- offsets_grad: float32 [2, 1024], P(None, ('batch', 'seq'))
- mixes_grad: float32 [5, 1024], P(None, ('batch', 'seq'))
- decay_grad: float32 [1024], P(('batch', 'seq'))
- first_grad: float32 [1024], P(('batch', 'seq'))
The draws below stay inside these ranges and needn't reach their ends.
Inputs may be any that keep to these rules, and one draw needn't show every extreme that they name: `segment_ids`: within a row the ids never fall and start at 0; each id marks one document of 1 to 512 positions, and one document has exactly 512.
All inputs are finite; a program needn't handle non-finite values.
Results may differ from the reference program's by a relative error of at most 0.008.
Values may be sent and summed in bfloat16 or wider, within the bound.
No kernel may reach another device: no remote copies, remote signals or barrier semaphores. Data moves between devices by JAX's collectives and lax.ppermute only.
A program may use at most 256 MiB of HBM per device.

```python
import math
import jax
import jax.numpy as jnp
import numpy as np
from jax import lax

D = 1024
FF = 4096
LENGTH = 1024
ROWS = 4
DOC_MOST = 512
SEGS = 8


def levels(key, shape, split, smallest, largest):
    level, own = 1.0, jax.random.fold_in(key, 6)
    for axis_at, shards_of in split:
        heights = jnp.exp(jax.random.uniform(jax.random.fold_in(own, axis_at), (shards_of,), jnp.float32, smallest / len(split), largest / len(split)))
        level = level * jnp.repeat(heights, shape[axis_at] // shards_of).reshape([-1 if axis == axis_at else 1 for axis in range(len(shape))])
    return level


def length_profile(amount, total, bound, lean):
    weights = [(1 << 20) // math.isqrt(grade ** lean) + 1 for grade in range(2, amount + 1)]
    surplus, counts = total - bound - (amount - 1), [1] * (amount - 1)
    while surplus > 0:
        movable = [i for i in range(amount - 1) if counts[i] < bound]
        whole, budget = sum([weights[i] for i in movable]), surplus
        for i in movable:
            more = min(bound - counts[i], max(1, budget * weights[i] // whole), surplus)
            counts[i] = counts[i] + more
            surplus = surplus - more
    return np.array([bound] + counts)


def ragged(rng, amount, total, bound, slope):
    if amount == 2:
        one = jax.random.randint(rng, (), max(1, total - bound), min(bound, total - 1) + 1)
        return jnp.stack([one, total - one])
    sizes = jnp.asarray(length_profile(amount, total, bound, slope), jnp.int32)
    pairs = (amount - 1) // 2
    giver, taker = sizes[1:1 + 2 * pairs:2], sizes[2:2 + 2 * pairs:2]
    room = jnp.minimum(giver - 1, bound - taker)
    moved = jax.random.randint(jax.random.fold_in(rng, 1), (pairs,), 0, 1 << 20) % (room + 1)
    sizes = sizes.at[1:1 + 2 * pairs:2].set(giver - moved).at[2:2 + 2 * pairs:2].set(taker + moved)
    return sizes[jax.random.permutation(jax.random.fold_in(rng, 2), amount)]


def bell_draw(stream_key, shape, deviation, reach, pieces=(), kind=jnp.bfloat16):
    factor_of = levels(stream_key, shape, pieces, -0.22, 0.18) if pieces else 1.0
    drawn = jax.random.normal(stream_key, shape, jnp.float32) * deviation * factor_of
    return jnp.minimum(jnp.maximum(drawn, -reach), reach).astype(kind)


def setup_inputs(seed: int = 0) -> dict:
    key_list = jax.random.split(jax.random.key(seed), 16)
    return {
        "layer_input": bell_draw(key_list[0], (ROWS, LENGTH, D), 1.0, 6.0, ((0, 4), (1, 8))),
        "segment_ids": jax.vmap(lambda own: jnp.searchsorted(jnp.cumsum(ragged(own, SEGS, LENGTH, DOC_MOST, 0)), jnp.arange(LENGTH), side="right"))(jax.random.split(key_list[1], ROWS)).reshape((ROWS, LENGTH)).astype(jnp.int32),
        "out_cotangent": bell_draw(key_list[2], (ROWS, LENGTH, D), 1.0, 6.0, ((0, 4), (1, 8))),
        "key_weight": bell_draw(key_list[3], (D, D), D ** -0.5, 0.1875, ((0, 32),)),
        "value_weight": bell_draw(key_list[4], (D, D), D ** -0.5, 0.1875, ((0, 32),)),
        "recept_weight": bell_draw(key_list[5], (D, D), D ** -0.5, 0.1875, ((0, 32),)),
        "output_weight": bell_draw(key_list[6], (D, D), (D // 16) ** -0.5, 0.75, ((0, 32),)),
        "channel_key": bell_draw(key_list[7], (D, FF), D ** -0.5, 0.1875, ((0, 32),)),
        "channel_value": bell_draw(key_list[8], (FF, D), FF ** -0.5, 0.09375, ((0, 32),)),
        "channel_recept": bell_draw(key_list[9], (D, D), D ** -0.5, 0.1875, ((0, 32),)),
        "norm_gains": jnp.clip(1.0 + 0.1 * jax.random.normal(key_list[10], (2, D), jnp.float32), 0.5, 1.5).astype(jnp.bfloat16),
        "norm_offsets": bell_draw(key_list[11], (2, D), 0.3, 1.5, ((1, 32),)),
        "mix_coeffs": jnp.clip(0.049804688 + 0.89941406 * jax.random.uniform(key_list[12], (5, D), jnp.float32) ** levels(key_list[12], (5, D), ((1, 32),), -0.2, 0.2), 0.049804688, 0.94921875).astype(jnp.bfloat16),
        "time_decay": jnp.clip(-7.59375 + 5.296875 * jax.random.uniform(key_list[13], (D,), jnp.float32) ** levels(key_list[13], (D,), ((0, 32),), -0.2, 0.2), -7.59375, -2.296875).astype(jnp.bfloat16),
        "time_first": jnp.clip(jax.random.uniform(key_list[14], (D,), jnp.float32, -1.0, 1.0) * levels(key_list[14], (D,), ((0, 32),), -0.4, 0.0), -1.0, 1.0).astype(jnp.bfloat16),
    }


EPS = 1e-05

@jax.custom_vjp
def low(v):
    return lax.optimization_barrier(v.astype(jnp.bfloat16)).astype(jnp.float32)

@jax.custom_vjp
def low_back(v):
    return v

def low_keep(v):
    return (low(v), None)

def low_pass(kept, grad):
    return (grad,)

def back_keep(v):
    return (v, None)

def back_low(kept, grad):
    return (low(grad),)
low.defvjp(low_keep, low_pass)
low_back.defvjp(back_keep, back_low)

def matmul(left, right):
    return jnp.dot(left, right, precision=lax.Precision.HIGHEST, preferred_element_type=jnp.float32)

def layer_norm(hidden, gain, offset):
    centred = hidden - lax.optimization_barrier(jnp.mean(hidden, axis=-1, keepdims=True))
    variance = lax.optimization_barrier(jnp.mean(centred * centred, axis=-1, keepdims=True))
    return centred * lax.rsqrt(variance + EPS) * gain + offset

def scaled_payload_line(lookup_squashed, payload_squashed, restart_markers, fading_pace, initial_reward):
    total_len = lookup_squashed.shape[0]
    span_len = math.gcd(total_len, 256)

    def step(state, item):
        present_lookup, present_payload, reset_now = item
        keep_now = 1.0 - reset_now
        cumulative_dividend = state[0] * keep_now
        cumulative_divisor = state[1] * keep_now
        leading_piece_reward = jnp.exp(initial_reward + present_lookup)
        tier_outcome = (cumulative_dividend + leading_piece_reward * present_payload) / (cumulative_divisor + leading_piece_reward)
        weight_now = jnp.exp(present_lookup)
        factor = jnp.exp(-fading_pace)
        return ((factor * cumulative_dividend + weight_now * present_payload, factor * cumulative_divisor + weight_now), tier_outcome)

    def block_steps(state, items):
        return lax.scan(step, state, items)
    start = (jnp.zeros_like(fading_pace), jnp.zeros_like(fading_pace))
    items = (lookup_squashed.reshape(-1, span_len, lookup_squashed.shape[1]), payload_squashed.reshape(-1, span_len, lookup_squashed.shape[1]), restart_markers.reshape(-1, span_len))
    ignored, results = lax.scan(jax.checkpoint(block_steps), start, items)
    return results.reshape(lookup_squashed.shape)

def row_forward(tier_settings, hidden, segment_row):
    lookup_weight_table, payload_weight_table, acceptor_table, emitted_weight_table, feature_blend_lookup, feature_blend_payload, feature_blend_acceptor, amplitude_lines, shifting_lines, blend_coefficient_lines, fading_exponent, initial_reward = tier_settings
    previous_ids = jnp.concatenate([jnp.full((1,), -1, jnp.int32), segment_row[:-1]])
    restart_markers = (segment_row != previous_ids).astype(hidden.dtype)
    keeps = (1.0 - restart_markers)[:, None]

    def shifted(normed):
        return jnp.concatenate([jnp.zeros_like(normed[:1]), normed[:-1]], axis=0) * keeps

    def mixed(normed, before, index):
        return low(normed * blend_coefficient_lines[index] + before * (1.0 - blend_coefficient_lines[index]))
    normed_one = layer_norm(hidden, amplitude_lines[0], shifting_lines[0])
    before_one = shifted(normed_one)
    lookup_squashed = low_back(matmul(mixed(normed_one, before_one, 0), lookup_weight_table))
    payload_squashed = low_back(matmul(mixed(normed_one, before_one, 1), payload_weight_table))
    recept = jax.nn.sigmoid(low_back(matmul(mixed(normed_one, before_one, 2), acceptor_table)))
    scaled_lookup_payloads = scaled_payload_line(lookup_squashed, payload_squashed, restart_markers, jnp.exp(fading_exponent), initial_reward)
    attended = low_back(matmul(low(recept * scaled_lookup_payloads), emitted_weight_table))
    middle = hidden + attended
    normed_two = layer_norm(middle, amplitude_lines[1], shifting_lines[1])
    before_two = shifted(normed_two)
    hidden_pre = low_back(matmul(mixed(normed_two, before_two, 3), feature_blend_lookup))
    squared = low(jnp.square(jax.nn.relu(hidden_pre)))
    channel_out = low_back(matmul(squared, feature_blend_payload))
    gate = jax.nn.sigmoid(low_back(matmul(mixed(normed_two, before_two, 4), feature_blend_acceptor)))
    return middle + gate * channel_out

def reference(layer_input, segment_ids, out_cotangent, key_weight, value_weight, recept_weight, output_weight, channel_key, channel_value, channel_recept, norm_gains, norm_offsets, mix_coeffs, time_decay, time_first):
    tier_settings = tuple((p.astype(jnp.float32) for p in (key_weight, value_weight, recept_weight, output_weight, channel_key, channel_value, channel_recept, norm_gains, norm_offsets, mix_coeffs, time_decay, time_first)))

    def forward(hidden_all, param_set):

        def each_row(carry, item):
            return (carry, row_forward(param_set, item[0], item[1]))
        ignored, outputs = lax.scan(jax.checkpoint(each_row), jnp.zeros((), jnp.float32), (hidden_all, segment_ids))
        return outputs
    tier_outcome, backward_function = jax.vjp(forward, layer_input.astype(jnp.float32), tier_settings)
    input_grad, grads = backward_function(out_cotangent.astype(jnp.float32))
    return (tier_outcome.astype(jnp.bfloat16), input_grad, grads[0], grads[1], grads[2], grads[3], grads[4], grads[5], grads[6], grads[7], grads[8], grads[9], grads[10], grads[11])
```

```python
import jax
import jax.numpy as jnp
from jax import lax
from jax.experimental import pallas as pl
from jax.experimental.pallas import tpu as pltpu
from jax.sharding import PartitionSpec as P

EPS = 1e-05
BOTH = ("batch", "seq")
LOW = jnp.bfloat16
FULL = jnp.float32
LANES = 128
SUBS = 8


def sizes():
    return lax.axis_size("batch"), lax.axis_size("seq")


def send(block, route):
    rows, cols = sizes()
    pairs = []
    for b in range(rows):
        for s in range(cols):
            target = route(b, s)
            if target is not None:
                pairs.append((b * cols + s, target[0] * cols + target[1]))
    return lax.ppermute(block, BOTH, pairs)


def send_next(block):
    cols = lax.axis_size("seq")
    return send(block, lambda b, s: (b, s + 1) if s + 1 < cols else None)


def send_back(block):
    return send(block, lambda b, s: (b, s - 1) if s > 0 else None)


def to_core(block):
    return send(block, lambda b, s: (b, s ^ 1))


def to_batch(block, k):
    return send(block, lambda b, s: (b ^ k, s))


def to_depth(block, k):
    return send(block, lambda b, s: (b, s ^ (2 * k)))


def share_rows(block):
    rows = lax.axis_size("batch")
    return jnp.concatenate([block] + [to_batch(block, k) for k in range(1, rows)], axis=0)


def return_rows(parts):
    rows = lax.axis_size("batch")
    count = parts.shape[0] // rows
    total = parts[:count]
    low = parts.astype(LOW)
    for k in range(1, rows):
        total = total + to_batch(low[k * count : (k + 1) * count], k).astype(FULL)
    return total


def scatter_sums(terms):
    rows, cols = sizes()
    b, s = lax.axis_index("batch"), lax.axis_index("seq")
    depth = cols // 2
    core, z = s % 2, s // 2
    count, height, width = terms.shape
    own = height // (rows * cols)

    def pick(x, at, axis):
        return lax.dynamic_index_in_dim(x, at, axis, keepdims=False)

    x = terms.astype(LOW).reshape(count, rows, depth, 2, own, width)
    got = to_core(pick(x, 1 - core, 3))
    y = (pick(x, core, 3).astype(FULL) + got.astype(FULL)).astype(LOW)
    total = pick(y, b, 1).astype(FULL)
    for k in range(1, rows):
        total = total + to_batch(pick(y, b ^ k, 1), k).astype(FULL)
    low = total.astype(LOW)
    result = pick(total, z, 1)
    for k in range(1, depth):
        result = result + to_depth(pick(low, z ^ k, 1), k).astype(FULL)
    return result


def sum_vectors(x):
    rows, cols = sizes()
    x = x + to_core(x)
    x = sum([to_batch(x, k) for k in range(1, rows)], x)
    return sum([to_depth(x, k) for k in range(1, cols // 2)], x)


def norm_forward(hidden, gain, offset):
    centred = hidden - jnp.mean(hidden, axis=-1, keepdims=True)
    scale = lax.rsqrt(jnp.mean(centred * centred, axis=-1, keepdims=True) + EPS)
    normed = centred * scale
    return normed * gain + offset, normed, scale


def norm_backward(grad, normed, scale, gain):
    gain_grad = jnp.sum(grad * normed, axis=0)
    offset_grad = jnp.sum(grad, axis=0)
    inner = grad * gain
    centred = inner - jnp.mean(inner, axis=-1, keepdims=True)
    input_part = scale * (centred - normed * jnp.mean(inner * normed, axis=-1, keepdims=True))
    return input_part, gain_grad, offset_grad


def mixing(normed, prior, coeff):
    return (normed * coeff + prior * (1.0 - coeff)).astype(LOW)


def project(active, weight):
    return jnp.einsum("td,de->te", active, weight, preferred_element_type=FULL)


def back_project(grad, weight):
    return jnp.einsum("te,de->td", grad, weight, preferred_element_type=FULL)


def weight_term(active, grad):
    return jnp.einsum("td,te->de", active, grad, preferred_element_type=FULL)


def to_tiles(x):
    count, width = x.shape
    blocks = width // LANES
    x = x.reshape(count // SUBS, SUBS, blocks, LANES).transpose(0, 2, 1, 3)
    return x.reshape(count * blocks, LANES)


def from_tiles(x, width):
    blocks = width // LANES
    count = x.shape[0] // blocks
    x = x.reshape(count // SUBS, blocks, SUBS, LANES).transpose(0, 2, 1, 3)
    return x.reshape(count, width)


def position(i, r, blocks):
    return pl.ds(i * (SUBS * blocks) + r, blocks, stride=SUBS)


def forward_scan(keep_ref, key_ref, value_ref, rates_ref, carry_ref, wkv_ref, inverse_ref, slope_ref):
    blocks = rates_ref.shape[1]
    fade, bonus = rates_ref[0], rates_ref[1]

    def eight(i, state):
        num, den, num_slope, den_slope = state
        for r in range(SUBS):
            at = position(i, r, blocks)
            key, value = key_ref[at, :], value_ref[at, :]
            keep = keep_ref[pl.ds(i * SUBS + r, 1), :]
            num, den, num_slope, den_slope = (
                num * keep,
                den * keep,
                num_slope * keep,
                den_slope * keep,
            )
            reward = jnp.exp(bonus + key)
            weight = jnp.exp(key)
            inverse = 1.0 / (den + reward)
            wkv = (num + reward * value) * inverse
            wkv_ref[at, :] = wkv
            inverse_ref[at, :] = inverse
            slope_ref[at, :] = (num_slope - wkv * den_slope) * inverse
            num_slope = fade * (num_slope + num)
            den_slope = fade * (den_slope + den)
            num = fade * num + weight * value
            den = fade * den + weight
        return num, den, num_slope, den_slope

    lax.fori_loop(
        0,
        keep_ref.shape[0] // SUBS,
        eight,
        (carry_ref[0], carry_ref[1], carry_ref[2], carry_ref[3]),
    )


def backward_scan(
    keep_ref, key_ref, value_ref, wkv_ref, share_ref, rates_ref, carry_ref, key_out, value_out, first_out
):
    blocks = rates_ref.shape[1]
    fade, bonus = rates_ref[0], rates_ref[1]
    groups = keep_ref.shape[0] // SUBS

    def eight(step, state):
        direct, scaled, first = state
        i = groups - 1 - step
        for r in reversed(range(SUBS)):
            at = position(i, r, blocks)
            key, value = key_ref[at, :], value_ref[at, :]
            wkv, share = wkv_ref[at, :], share_ref[at, :]
            keep = keep_ref[pl.ds(i * SUBS + r, 1), :]
            reward = share * jnp.exp(bonus + key)
            weight = jnp.exp(key)
            bonus_part = reward * (value - wkv)
            key_out[at, :] = weight * (direct * value - scaled) + bonus_part
            value_out[at, :] = weight * direct + reward
            first = first + bonus_part
            direct = (share + fade * direct) * keep
            scaled = (share * wkv + fade * scaled) * keep
        return direct, scaled, first

    first_out[...] = lax.fori_loop(
        0, groups, eight, (carry_ref[0], carry_ref[1], jnp.zeros_like(fade))
    )[2]


IN_VMEM = pl.BlockSpec(memory_space=pltpu.VMEM)
SMALL = pltpu.CompilerParams(vmem_limit_bytes=8 * 1024 * 1024)


def run_forward(keep, key, value, rates, carry):
    tiles = jax.ShapeDtypeStruct(key.shape, FULL)
    return pl.pallas_call(
        forward_scan,
        out_shape=(tiles, tiles, tiles),
        in_specs=[IN_VMEM] * 5,
        out_specs=(IN_VMEM,) * 3,
        compiler_params=SMALL,
        cost_estimate=pl.CostEstimate(
            flops=20 * key.size, bytes_accessed=20 * key.size, transcendentals=3 * key.size
        ),
    )(keep, key, value, rates, carry)


def run_backward(keep, key, value, wkv, share, rates, carry):
    tiles = jax.ShapeDtypeStruct(key.shape, FULL)
    return pl.pallas_call(
        backward_scan,
        out_shape=(tiles, tiles, jax.ShapeDtypeStruct(rates.shape[1:], FULL)),
        in_specs=[IN_VMEM] * 7,
        out_specs=(IN_VMEM,) * 3,
        compiler_params=SMALL,
        cost_estimate=pl.CostEstimate(
            flops=20 * key.size, bytes_accessed=24 * key.size, transcendentals=2 * key.size
        ),
    )(keep, key, value, wkv, share, rates, carry)


def per_device(
    layer_input,
    segment_ids,
    out_cotangent,
    key_weight,
    value_weight,
    recept_weight,
    output_weight,
    channel_key,
    channel_value,
    channel_recept,
    norm_gains,
    norm_offsets,
    mix_coeffs,
    time_decay,
    time_first,
):
    rows, cols = sizes()
    b, s = lax.axis_index("batch"), lax.axis_index("seq")
    device = b * cols + s
    length, width = layer_input.shape[1:]
    own = key_weight.shape[0]
    hidden_width = channel_key.shape[1]
    part_width = hidden_width // rows
    blocks = width // LANES

    raw = layer_input[0]
    ids = segment_ids[0].astype(FULL)
    edge = jnp.stack([raw[-1], jnp.full((width,), ids[-1]).astype(LOW)])
    edge = send_next(edge)
    before_id = jnp.where(s == 0, -1.0, edge[1, 0].astype(FULL))

    vectors = jnp.concatenate(
        [norm_gains, norm_offsets, mix_coeffs, time_decay[None], time_first[None]], axis=0
    )
    n_vectors = vectors.shape[0]
    vector_row = jnp.pad(vectors.reshape(1, -1), ((0, 15), (0, width - n_vectors * own)))
    packed = jnp.concatenate(
        [key_weight, value_weight, recept_weight, output_weight, channel_recept, vector_row], axis=0
    )
    gathered = lax.all_gather(packed, BOTH, axis=0)
    key_all, value_all, recept_all, output_all, gate_all = (
        gathered[:, i * own : (i + 1) * own].reshape(width, width) for i in range(5)
    )
    vectors = gathered[:, 5 * own, : n_vectors * own].reshape(rows * cols, n_vectors, own)
    vectors = vectors.transpose(1, 0, 2).reshape(n_vectors, width).astype(FULL)
    gains, offsets, coeffs = vectors[0:2], vectors[2:4], vectors[4:9]
    pace, bonus = jnp.exp(vectors[9]), vectors[10]

    crossed = channel_key.reshape(own, rows, part_width).transpose(1, 0, 2)
    crossed = lax.all_to_all(crossed, "batch", 0, 0)
    part_key = lax.all_gather(crossed, "seq", axis=1, tiled=True).reshape(width, part_width)
    part_value = lax.all_gather(channel_value, "seq", axis=0, tiled=True)

    hidden = raw.astype(FULL)
    normed_one, unit_one, scale_one = norm_forward(hidden, gains[0], offsets[0])
    edge_normed = norm_forward(edge[0:1].astype(FULL), gains[0], offsets[0])[0]
    previous_ids = jnp.concatenate([before_id[None], ids[:-1]])
    keep = (ids == previous_ids).astype(FULL)
    opened = (ids == before_id)[:, None]
    closing = (ids == ids[-1])[:, None]
    prior_one = jnp.concatenate([edge_normed, normed_one[:-1]], axis=0) * keep[:, None]
    mix_key = mixing(normed_one, prior_one, coeffs[0])
    mix_value = mixing(normed_one, prior_one, coeffs[1])
    mix_recept = mixing(normed_one, prior_one, coeffs[2])
    key_act = project(mix_key, key_all)
    value_act = project(mix_value, value_all)
    recept_act = jax.nn.sigmoid(project(mix_recept, recept_all))

    places = jnp.arange(length, dtype=FULL)[:, None]
    left = length - 1.0 - places
    sum_den = jnp.where(closing, jnp.exp(key_act - pace * left), 0.0)
    sum_num = sum_den * value_act
    local = jnp.stack(
        [
            jnp.sum(sum_num, axis=0),
            jnp.sum(sum_den, axis=0),
            jnp.sum(sum_num * left, axis=0),
            jnp.sum(sum_den * left, axis=0),
            jnp.full((width,), ids[-1]),
        ]
    )
    every = lax.all_gather(jnp.pad(local, ((0, 3), (0, 0))), "seq")
    order = jnp.arange(cols)
    span = (length * jnp.maximum(s - 1 - order, 0)).astype(FULL)[:, None]
    valid = ((order < s) & (every[:, 4, 0] == before_id))[:, None]
    reach = jnp.exp(-pace * span)
    carry = jnp.stack(
        [
            jnp.sum(jnp.where(valid, reach * every[:, 0], 0.0), axis=0),
            jnp.sum(jnp.where(valid, reach * every[:, 1], 0.0), axis=0),
            jnp.sum(jnp.where(valid, reach * (every[:, 2] + span * every[:, 0]), 0.0), axis=0),
            jnp.sum(jnp.where(valid, reach * (every[:, 3] + span * every[:, 1]), 0.0), axis=0),
        ]
    ).reshape(4, blocks, LANES)
    keep_lanes = jnp.broadcast_to(keep[:, None], (length, LANES))
    rates = jnp.stack([jnp.exp(-pace), bonus]).reshape(2, blocks, LANES)
    key_tiles, value_tiles = to_tiles(key_act), to_tiles(value_act)
    wkv_tiles, inverse_tiles, slope_tiles = run_forward(
        keep_lanes, key_tiles, value_tiles, rates, carry
    )
    wkv = from_tiles(wkv_tiles, width)
    inverse = from_tiles(inverse_tiles, width)
    slope = from_tiles(slope_tiles, width)
    gated = (recept_act * wkv).astype(LOW)
    middle = hidden + project(gated, output_all)

    normed_two, unit_two, scale_two = norm_forward(middle, gains[1], offsets[1])
    before_two = send_next(normed_two[-1:])
    prior_two = jnp.concatenate([before_two, normed_two[:-1]], axis=0) * keep[:, None]
    mix_hidden = mixing(normed_two, prior_two, coeffs[3])
    mix_gate = mixing(normed_two, prior_two, coeffs[4])
    shared = share_rows(mix_hidden)
    positive = jax.nn.relu(project(shared, part_key))
    squared = jnp.square(positive).astype(LOW)
    channel_out = return_rows(project(squared, part_value))
    gate = jax.nn.sigmoid(project(mix_gate, gate_all))
    block_output = (middle + gate * channel_out).astype(LOW)

    grad_out = out_cotangent[0].astype(FULL)
    grad_values = (grad_out * gate).astype(LOW)
    grad_gate = (grad_out * channel_out * gate * (1.0 - gate)).astype(LOW)
    shared_grad = share_rows(grad_values)
    grad_hidden = (back_project(shared_grad, part_value) * 2.0 * positive).astype(LOW)
    value_term = weight_term(squared, shared_grad).astype(LOW)
    hidden_term = weight_term(shared, grad_hidden).astype(LOW)
    grad_mix_hidden = return_rows(back_project(grad_hidden, part_key))
    grad_mix_gate = back_project(grad_gate, gate_all)
    channel_value_grad = lax.psum_scatter(value_term, "seq", scatter_dimension=0, tiled=True)
    hidden_term = hidden_term.reshape(rows, cols * own, part_width)
    hidden_sum = lax.psum_scatter(hidden_term, "seq", scatter_dimension=1, tiled=True)
    hidden_sum = lax.all_to_all(hidden_sum, "batch", 0, 0)
    channel_key_grad = hidden_sum.transpose(1, 0, 2).reshape(own, hidden_width).astype(FULL)

    own_two = grad_mix_hidden * coeffs[3] + grad_mix_gate * coeffs[4]
    passed_two = (
        grad_mix_hidden * (1.0 - coeffs[3]) + grad_mix_gate * (1.0 - coeffs[4])
    ) * keep[:, None]
    after_two = send_back(passed_two[:1])
    difference_two = normed_two - prior_two
    mix_three = jnp.sum(grad_mix_hidden * difference_two, axis=0)
    mix_four = jnp.sum(grad_mix_gate * difference_two, axis=0)
    grad_normed_two = own_two + jnp.concatenate([passed_two[1:], after_two], axis=0)
    middle_part, gain_two, offset_two = norm_backward(
        grad_normed_two, unit_two, scale_two, gains[1]
    )
    grad_middle = grad_out + middle_part

    grad_attended = grad_middle.astype(LOW)
    grad_gated = back_project(grad_attended, output_all)
    grad_wkv = grad_gated * recept_act
    grad_recept = (grad_gated * wkv * recept_act * (1.0 - recept_act)).astype(LOW)
    early = jnp.stack(
        [
            weight_term(gated, grad_attended).astype(LOW),
            weight_term(mix_gate, grad_gate).astype(LOW),
            weight_term(mix_recept, grad_recept).astype(LOW),
        ]
    )
    early_sums = scatter_sums(early)
    share = grad_wkv * inverse
    decay_term = -pace * jnp.sum(grad_wkv * slope, axis=0)
    head = jnp.where(opened, share * jnp.exp(-pace * places), 0.0)
    local_back = jnp.stack(
        [jnp.sum(head, axis=0), jnp.sum(head * wkv, axis=0), jnp.full((width,), before_id)]
    )
    every_back = lax.all_gather(jnp.pad(local_back, ((0, 5), (0, 0))), "seq")
    span_back = (length * jnp.maximum(order - 1 - s, 0)).astype(FULL)[:, None]
    valid_back = ((order > s) & (every_back[:, 2, 0] == ids[-1]))[:, None]
    reach_back = jnp.exp(-pace * span_back)
    carry_back = jnp.stack(
        [
            jnp.sum(jnp.where(valid_back, reach_back * every_back[:, 0], 0.0), axis=0),
            jnp.sum(jnp.where(valid_back, reach_back * every_back[:, 1], 0.0), axis=0),
        ]
    ).reshape(2, blocks, LANES)
    grad_key, grad_value, first_term = run_backward(
        keep_lanes, key_tiles, value_tiles, wkv_tiles, to_tiles(share), rates, carry_back
    )
    grad_key, grad_value = lax.optimization_barrier(
        (from_tiles(grad_key, width), from_tiles(grad_value, width))
    )
    grad_key, grad_value = grad_key.astype(LOW), grad_value.astype(LOW)
    late = jnp.stack(
        [weight_term(mix_key, grad_key).astype(LOW), weight_term(mix_value, grad_value).astype(LOW)]
    )
    late_sums = scatter_sums(late)
    grad_mix_key = back_project(grad_key, key_all)
    grad_mix_value = back_project(grad_value, value_all)
    grad_mix_recept = back_project(grad_recept, recept_all)
    own_one = (
        grad_mix_key * coeffs[0] + grad_mix_value * coeffs[1] + grad_mix_recept * coeffs[2]
    )
    passed_one = (
        grad_mix_key * (1.0 - coeffs[0])
        + grad_mix_value * (1.0 - coeffs[1])
        + grad_mix_recept * (1.0 - coeffs[2])
    ) * keep[:, None]
    after_one = send_back(passed_one[:1])
    difference_one = normed_one - prior_one
    grad_normed_one = own_one + jnp.concatenate([passed_one[1:], after_one], axis=0)
    input_part, gain_one, offset_one = norm_backward(
        grad_normed_one, unit_one, scale_one, gains[0]
    )
    input_grad = grad_middle + input_part

    sums = sum_vectors(
        jnp.stack(
            [
                gain_one,
                gain_two,
                offset_one,
                offset_two,
                jnp.sum(grad_mix_key * difference_one, axis=0),
                jnp.sum(grad_mix_value * difference_one, axis=0),
                jnp.sum(grad_mix_recept * difference_one, axis=0),
                mix_three,
                mix_four,
                decay_term,
                first_term.reshape(width),
            ]
        )
    )
    sums = lax.dynamic_slice(sums, (0, device * own), (n_vectors, own))
    return (
        block_output[None],
        input_grad[None],
        late_sums[0],
        late_sums[1],
        early_sums[2],
        early_sums[0],
        channel_key_grad,
        channel_value_grad.astype(FULL),
        early_sums[1],
        sums[0:2],
        sums[2:4],
        sums[4:9],
        sums[9],
        sums[10],
    )


def solution(mesh):
    tokens = P("batch", "seq", None)
    weight = P(BOTH, None)
    lines = P(None, BOTH)
    return jax.shard_map(
        per_device,
        mesh=mesh,
        in_specs=(tokens, P("batch", "seq"), tokens)
        + (weight,) * 7
        + (lines,) * 3
        + (P(BOTH),) * 2,
        out_specs=(tokens, tokens) + (weight,) * 7 + (lines,) * 3 + (P(BOTH),) * 2,
        check_vma=False,
    )
```

```python
import jax
import jax.numpy as jnp
from jax import lax
from jax.experimental import pallas as pl
from jax.experimental.pallas import tpu as pltpu
from jax.sharding import PartitionSpec as P

EPS = 1e-05
BOTH = ("batch", "seq")
LOW = jnp.bfloat16
FULL = jnp.float32
LANES = 128
SUBS = 8
MIB = 1024 * 1024
COST = 1024
IN_VMEM = pl.BlockSpec(memory_space=pltpu.VMEM)
ANYWHERE = pl.BlockSpec(memory_space=pl.ANY)
IN_HBM = pl.BlockSpec(memory_space=pltpu.HBM)


def sizes():
    return lax.axis_size("batch"), lax.axis_size("seq")


def places():
    s = lax.axis_index("seq")
    return lax.axis_index("batch"), s >> 1, s & 1


def send(block, route):
    rows, cols = sizes()
    pairs = []
    for b in range(rows):
        for s in range(cols):
            target = route(b, s)
            if target is not None:
                pairs.append((b * cols + s, target[0] * cols + target[1]))
    return lax.ppermute(block, BOTH, pairs)


def send_next(block):
    cols = lax.axis_size("seq")
    return send(block, lambda b, s: (b, s + 1) if s + 1 < cols else None)


def send_back(block):
    return send(block, lambda b, s: (b, s - 1) if s > 0 else None)


def to_core(block):
    return send(block, lambda b, s: (b, s ^ 1))


def to_batch(block, k):
    return send(block, lambda b, s: (b ^ k, s))


def to_depth(block, k):
    return send(block, lambda b, s: (b, s ^ (2 * k)))


def fuse(body, outs, *args, after=(), limit=16, flops=0, plain=False, fetch=False):
    if plain:
        return tuple(body(*args))
    count, held = len(args), len(args) + len(after)

    def kernel(*refs):
        taken = refs[:count]
        if fetch:
            taken, arrived = refs[held + len(outs) : -1], refs[-1]
            copies = [
                pltpu.make_async_copy(refs[i], taken[i], arrived.at[i]) for i in range(count)
            ]
            for copy in copies:
                copy.start()
            for copy in copies:
                copy.wait()
        results = body(*[ref[...] for ref in taken])
        for ref, value in zip(refs[held : held + len(outs)], results, strict=True):
            ref[...] = value

    return pl.pallas_call(
        kernel,
        out_shape=tuple(jax.ShapeDtypeStruct(shape, dtype) for shape, dtype in outs),
        in_specs=[IN_HBM if fetch else IN_VMEM] * count + [ANYWHERE] * len(after),
        out_specs=(IN_VMEM,) * len(outs),
        scratch_shapes=[pltpu.VMEM(x.shape, x.dtype) for x in args]
        + [pltpu.SemaphoreType.DMA((count,))]
        if fetch
        else [],
        compiler_params=pltpu.CompilerParams(vmem_limit_bytes=limit * MIB),
        cost_estimate=pl.CostEstimate(flops=COST, bytes_accessed=COST, transcendentals=0),
    )(*args, *after)


def dot(x, w):
    return lax.dot_general(x, w, (((1,), (0,)), ((), ())), preferred_element_type=FULL)


def dot_back(x, w):
    return lax.dot_general(x, w, (((1,), (1,)), ((), ())), preferred_element_type=FULL)


def dot_rows(x, y):
    return lax.dot_general(x, y, (((0,), (0,)), ((), ())), preferred_element_type=FULL)


def restore(x, order):
    high = x.astype(LOW)
    rest = (x - high.astype(FULL)).astype(LOW)
    return dot_back(high, order) + dot_back(rest, order)


def restore_in(x, order):
    high = x.astype(LOW)
    rest = (x - high.astype(FULL)).astype(LOW)
    return dot(high, order) + dot(rest, order)


def row_index(shape):
    return lax.broadcasted_iota(jnp.int32, shape, 0)


def stack_rows(rows, count=SUBS):
    width = rows[0].shape[1]
    index = row_index((count, width))
    out = jnp.zeros((count, width), FULL)
    for i, row in enumerate(rows):
        out = jnp.where(index == i, row, out)
    return out


def down(x, first, plain):
    rolled = jnp.roll(x, 1, 0) if plain else pltpu.roll(x, 1, 0)
    return jnp.where(row_index(x.shape) == 0, first, rolled)


def up(x, last, plain):
    count = x.shape[0]
    rolled = jnp.roll(x, -1, 0) if plain else pltpu.roll(x, count - 1, 0)
    return jnp.where(row_index(x.shape) == count - 1, last, rolled)


def column_sum(x):
    return jnp.sum(x, axis=0, keepdims=True)


def lane_mean(x):
    return jnp.mean(x, axis=-1, keepdims=True)


def unit_norm(hidden):
    centred = hidden - lane_mean(hidden)
    scale = lax.rsqrt(lane_mean(centred * centred) + EPS)
    return centred * scale, scale


def norm_backward(grad, unit, scale, gain):
    inner = grad * gain
    centred = inner - lane_mean(inner)
    return scale * (centred - unit * lane_mean(inner * unit))


def mixing(normed, prior, coeff):
    return (normed * coeff + prior * (1.0 - coeff)).astype(LOW)


def pick(values, index):
    out = values[0]
    for i in range(1, len(values)):
        out = jnp.where(index == i, values[i], out)
    return out


def log2(n):
    return n.bit_length() - 1


def untile(x, blocks):
    count = x.shape[0] // blocks
    x = x.reshape(count // SUBS, blocks, SUBS, LANES)
    return jnp.concatenate([x[:, i].reshape(count, LANES) for i in range(blocks)], axis=1)


def to_lanes(row):
    return jnp.concatenate(
        [row[:, i * LANES : (i + 1) * LANES] for i in range(row.shape[1] // LANES)], axis=0
    )


def from_lanes(x):
    return jnp.concatenate([x[i : i + 1] for i in range(x.shape[0])], axis=1)


def to_tiles(x):
    count, width = x.shape
    blocks = width // LANES
    x = x.reshape(count // SUBS, SUBS, blocks, LANES).transpose(0, 2, 1, 3)
    return x.reshape(count * blocks, LANES)


def from_tiles(x, width):
    blocks = width // LANES
    count = x.shape[0] // blocks
    x = x.reshape(count // SUBS, blocks, SUBS, LANES).transpose(0, 2, 1, 3)
    return x.reshape(count, width)


def position(i, r, blocks):
    return pl.ds(i * (SUBS * blocks) + r, blocks, stride=SUBS)


def forward_scan(keep_ref, key_ref, value_ref, rates_ref, carry_ref, out_ref):
    blocks = rates_ref.shape[1]
    fade, bonus = rates_ref[0], rates_ref[1]

    def eight(i, state):
        num, den, num_slope, den_slope = state
        for r in range(SUBS):
            at = position(i, r, blocks)
            key, value = key_ref[at, :], value_ref[at, :]
            keep = keep_ref[pl.ds(i * SUBS + r, 1), :]
            num, den, num_slope, den_slope = (
                num * keep,
                den * keep,
                num_slope * keep,
                den_slope * keep,
            )
            reward = jnp.exp(bonus + key)
            weight = jnp.exp(key)
            inverse = 1.0 / (den + reward)
            wkv = (num + reward * value) * inverse
            out_ref[0, at, :] = wkv
            out_ref[1, at, :] = inverse
            out_ref[2, at, :] = (num_slope - wkv * den_slope) * inverse
            num_slope = fade * (num_slope + num)
            den_slope = fade * (den_slope + den)
            num = fade * num + weight * value
            den = fade * den + weight
        return num, den, num_slope, den_slope

    lax.fori_loop(
        0,
        keep_ref.shape[0] // SUBS,
        eight,
        (carry_ref[0], carry_ref[1], carry_ref[2], carry_ref[3]),
    )


def backward_scan(
    keep_ref, key_ref, value_ref, scanned_ref, share_ref, rates_ref, carry_ref, key_out, value_out, first_out
):
    blocks = rates_ref.shape[1]
    fade, bonus = rates_ref[0], rates_ref[1]
    groups = keep_ref.shape[0] // SUBS

    def eight(step, state):
        direct, scaled, first = state
        i = groups - 1 - step
        for r in reversed(range(SUBS)):
            at = position(i, r, blocks)
            key, value = key_ref[at, :], value_ref[at, :]
            wkv, share = scanned_ref[0, at, :], share_ref[at, :]
            keep = keep_ref[pl.ds(i * SUBS + r, 1), :]
            reward = share * jnp.exp(bonus + key)
            weight = jnp.exp(key)
            bonus_part = reward * (value - wkv)
            key_out[at, :] = weight * (direct * value - scaled) + bonus_part
            value_out[at, :] = weight * direct + reward
            first = first + bonus_part
            direct = (share + fade * direct) * keep
            scaled = (share * wkv + fade * scaled) * keep
        return direct, scaled, first

    first_out[...] = lax.fori_loop(
        0, groups, eight, (carry_ref[0], carry_ref[1], jnp.zeros_like(fade))
    )[2]


def run_forward(keep, key, value, rates, carry):
    return pl.pallas_call(
        forward_scan,
        out_shape=jax.ShapeDtypeStruct((3,) + key.shape, FULL),
        in_specs=[IN_VMEM] * 5,
        out_specs=IN_VMEM,
        compiler_params=pltpu.CompilerParams(vmem_limit_bytes=8 * MIB),
        cost_estimate=pl.CostEstimate(
            flops=20 * key.size, bytes_accessed=20 * key.size, transcendentals=3 * key.size
        ),
    )(keep, key, value, rates, carry)


def run_backward(keep, key, value, wkv, share, rates, carry):
    tiles = jax.ShapeDtypeStruct(key.shape, FULL)
    return pl.pallas_call(
        backward_scan,
        out_shape=(tiles, tiles, jax.ShapeDtypeStruct(rates.shape[1:], FULL)),
        in_specs=[IN_VMEM] * 7,
        out_specs=(IN_VMEM,) * 3,
        compiler_params=pltpu.CompilerParams(vmem_limit_bytes=8 * MIB),
        cost_estimate=pl.CostEstimate(
            flops=20 * key.size, bytes_accessed=24 * key.size, transcendentals=2 * key.size
        ),
    )(keep, key, value, wkv, share, rates, carry)


def moved(sums, span, pace):
    fade = jnp.exp(-pace * span)
    if len(sums) == 4:
        num, den, num_slope, den_slope = sums
        return [
            fade * num,
            fade * den,
            fade * (num_slope + span * num),
            fade * (den_slope + span * den),
        ]
    return [fade * x for x in sums]


def split_message(message, count):
    return [message[i : i + 1] for i in range(count)], message[count : count + 1], message[count + 1 : count + 2]


def by_place(message, other):
    core = places()[2]
    return jnp.where(core == 0, message, other), jnp.where(core == 0, other, message)


def chip_sums(count, length, forward):
    def body(message, other, vectors):
        pace = jnp.exp(vectors[9:10])
        first, second = by_place(message, other)
        one, one_last, one_before = split_message(first, count)
        two, two_last, _ = split_message(second, count)
        near, far = (two, one) if forward else (one, two)
        through = (two_last == one_last) if forward else (one_last == one_before)
        far = moved(far, float(length), pace)
        sums = [n + jnp.where(through, f, 0.0) for n, f in zip(near, far, strict=True)]
        return (stack_rows(sums + [two_last, one_before]),)

    return body


def carried(count, length, forward):
    def body(message, other, vectors, *got):
        depth = len(got) + 1
        _, z, core = places()
        pace = jnp.exp(vectors[9:10])
        first, second = by_place(message, other)
        one, one_last, one_before = split_message(first, count)
        two, two_last, _ = split_message(second, count)
        total = [jnp.zeros_like(x) for x in one]
        for k in range(1, depth):
            sums, last, before = split_message(got[k - 1], count)
            if forward:
                valid = (last == one_before) & (z >= k)
            else:
                valid = (before == two_last) & (z < depth - k)
            sums = moved(sums, 2.0 * length * (k - 1), pace)
            total = [t + jnp.where(valid, x, 0.0) for t, x in zip(total, sums, strict=True)]
        inner, through = (one, one_last == one_before) if forward else (two, two_last == one_last)
        passed = moved(total, float(length), pace)
        passed = [x + jnp.where(through, y, 0.0) for x, y in zip(inner, passed, strict=True)]
        chosen = core == (1 if forward else 0)
        return (
            jnp.stack(
                [to_lanes(jnp.where(chosen, p, t)) for p, t in zip(passed, total, strict=True)]
            ),
        )

    return body


def carry_exchange(values, vectors, length, forward, plain, after=()):
    cols = lax.axis_size("seq")
    count = 4 if forward else 2
    width = values.shape[1]
    other = to_core(values)
    (chip,) = fuse(
        chip_sums(count, length, forward), [((SUBS, width), FULL)], values, other, vectors, plain=plain
    )
    step = 1 if forward else -1

    def route(k):
        def go(b, s):
            target = s + 2 * k * step
            return (b, target) if 0 <= target < cols else None

        return go

    got = [send(chip, route(k)) for k in range(1, cols // 2)]
    return fuse(
        carried(count, length, forward),
        [((count, width // LANES, LANES), FULL)],
        values,
        other,
        vectors,
        *got,
        after=after,
        plain=plain,
    )[0]


def add_batch(own, got, plain, after=()):
    count, height, width = own.shape
    depth = lax.axis_size("seq") // 2
    part = height // depth

    def body(own, *got):
        total = sum((x.astype(FULL) for x in got), own.astype(FULL))
        return [total[:, :part]] + [
            total[:, k * part : (k + 1) * part].astype(LOW) for k in range(1, depth)
        ]

    return fuse(
        body,
        [((count, part, width), FULL)] + [((count, part, width), LOW)] * (depth - 1),
        own,
        *got,
        after=after,
        plain=plain,
    )


def add_depth(pieces, plain, after=()):
    count, part, width = pieces[0].shape
    got = [to_depth(pieces[k], k) for k in range(1, len(pieces))]

    def body(own, *got):
        total = sum((x.astype(FULL) for x in got), own)
        return [total[i] for i in range(count)]

    return fuse(body, [((part, width), FULL)] * count, pieces[0], *got, after=after, plain=plain)


def per_device(
    layer_input,
    segment_ids,
    out_cotangent,
    key_weight,
    value_weight,
    recept_weight,
    output_weight,
    channel_key,
    channel_value,
    channel_recept,
    norm_gains,
    norm_offsets,
    mix_coeffs,
    time_decay,
    time_first,
):
    rows, cols = sizes()
    depth = cols // 2
    length, width = layer_input.shape[1:]
    own = key_weight.shape[0]
    hidden_width = channel_key.shape[1]
    part_width = hidden_width // rows
    half = width // 2
    plain = own % 16 != 0
    low_act, full_act = ((length, width), LOW), ((length, width), FULL)
    narrow = ((length, LANES), FULL)
    square = ((width, width), LOW)
    edge_row = ((SUBS, width), FULL)
    raw, cotangent = layer_input[0], out_cotangent[0]
    mac = 2 * length * width * width

    small = [norm_gains, norm_offsets, mix_coeffs, time_decay[None], time_first[None]]
    n_vectors = sum(x.shape[0] for x in small)

    def prepare(key, value, recept, output, gate, cross, raw, ids, *small):
        b, z, core = places()
        device = b * cols + z * 2 + core
        lane = lax.broadcasted_iota(jnp.int32, (own, width), 1)
        home = (lane == device * own + row_index((own, width))).astype(FULL).astype(LOW)
        placed = jnp.zeros((16, width), FULL)
        at = 0
        for x in small:
            x = dot(x, home)
            for i in range(x.shape[0]):
                placed = jnp.where(row_index(placed.shape) == at, x[i : i + 1], placed)
                at += 1
        blocks = [cross[:, j * part_width : (j + 1) * part_width] for j in range(rows)]
        ids = ids.astype(FULL)
        last = raw[length - 16 :].astype(FULL)[15:16]
        edge = stack_rows([last, jnp.broadcast_to(ids[:, length - 1 :], (1, width))], 16)
        return (
            [
                jnp.concatenate([key, value, placed.astype(LOW)], axis=0),
                jnp.concatenate([recept, output, gate], axis=0),
                edge,
                jnp.broadcast_to(ids, (LANES, length)).T,
            ]
            + [pick(blocks, b ^ k) for k in range(rows)]
        )

    first_pack, second_pack, edge, ids_lanes, *crossing = fuse(
        prepare,
        [((2 * own + 16, width), LOW), ((3 * own, width), LOW), ((16, width), FULL), narrow]
        + [((own, part_width), LOW)] * rows,
        key_weight,
        value_weight,
        recept_weight,
        output_weight,
        channel_recept,
        channel_key,
        raw,
        segment_ids,
        *small,
        plain=plain,
        fetch=True,
    )
    deep_got = [to_depth(first_pack, k) for k in range(1, depth)]
    cross_got = [to_batch(crossing[k], k) for k in range(1, rows)]
    edge = send_next(edge)

    def begin(raw, edge, ids):
        b, z, core = places()
        place = lax.broadcasted_iota(jnp.int32, (1, width), 1)
        block, row = place >> log2(own), place & (own - 1)
        k_core = block >> log2(rows * depth)
        k_batch = (block >> log2(depth)) & (rows - 1)
        k_depth = block & (depth - 1)
        target = ((k_batch ^ b) << log2(cols)) + ((k_depth ^ z) << 1) + (k_core ^ core)
        feature = (target << log2(own)) + row
        order = jnp.concatenate(
            [
                (row_index((LANES, width)) + i * LANES == feature).astype(FULL).astype(LOW)
                for i in range(width // LANES)
            ],
            axis=0,
        )
        unit, scale = unit_norm(dot(raw, order))
        edge_unit = unit_norm(dot(edge.astype(LOW), order))[0]
        before = jnp.where((z == 0) & (core == 0), -1.0, edge[1:2])
        before_lanes = before[:, :LANES]
        last = ids[length - 1 : length]
        keep = (ids == down(ids, before_lanes, plain)).astype(FULL)
        opened = (ids == before_lanes).astype(FULL)
        closing = (ids == last).astype(FULL)
        last = jnp.broadcast_to(last[:, :1], (1, width))
        scale = jnp.broadcast_to(scale, (length, LANES))
        return (
            order,
            unit,
            keep,
            jnp.concatenate([keep, opened, closing, scale], axis=1),
            stack_rows([edge_unit[0:1], last, before]),
        )

    order, unit_one, keep, statics, edges = fuse(
        begin,
        [square, full_act, narrow, ((length, 4 * LANES), FULL), edge_row],
        raw,
        edge,
        ids_lanes,
        plain=plain,
        flops=mac,
    )

    first_deep, second_pack = fuse(
        lambda second, *x: (jnp.stack(x), second),
        [((depth,) + first_pack.shape, LOW), (second_pack.shape, LOW)],
        second_pack,
        first_pack,
        *deep_got,
        after=(order, *cross_got),
        plain=plain,
    )
    first_wide = [to_batch(first_deep, k) for k in range(1, rows)]
    first_pieces = [first_deep] + first_wide
    first_pieces = first_pieces + [to_core(piece) for piece in first_pieces]
    second_got = [to_depth(second_pack, k) for k in range(1, depth)]

    cross_rows = rows * own * part_width // width
    packed_rows = cross_rows + channel_value.shape[0]

    def deepen(value, *x):
        b = places()[0]
        cross, x = x[:rows], x[rows:]
        cross = jnp.concatenate([pick(cross, j ^ b) for j in range(rows)], axis=0)
        return (
            jnp.stack([y[: 2 * own] for y in x]),
            jnp.stack([y[2 * own :] for y in x]),
            jnp.concatenate([cross.reshape(cross_rows, width), value], axis=0),
        )

    second_deep, third_deep, channel_pack = fuse(
        deepen,
        [
            ((depth, 2 * own, width), LOW),
            ((depth, own, width), LOW),
            ((packed_rows, width), LOW),
        ],
        channel_value,
        crossing[0],
        *cross_got,
        second_pack,
        *second_got,
        after=first_wide,
        plain=plain,
    )
    channel_pack = lax.all_gather(channel_pack, "seq", axis=0, tiled=True)

    def unpack_channel(x):
        x = x.reshape(cols, packed_rows, width)
        key = x[:, :cross_rows].reshape(cols, rows, own, part_width)
        key = jnp.concatenate(
            [key[j, i] for i in range(rows) for j in range(cols)], axis=0
        )
        return key, x[:, cross_rows:].reshape(part_width, width)

    part_key, part_value = fuse(
        unpack_channel,
        [((width, part_width), LOW), ((part_width, width), LOW)],
        channel_pack,
        plain=plain,
    )

    second_wide = [to_batch(second_deep, k) for k in range(1, rows)]
    (third_deep,) = fuse(
        lambda x: (x,), [(third_deep.shape, LOW)], third_deep, after=second_wide, plain=plain
    )
    third_wide = [to_batch(third_deep, k) for k in range(1, rows)]

    def joined(deep, wide, after):
        (mine,) = fuse(
            lambda *x: (jnp.concatenate(x, axis=0),),
            [((rows * depth,) + deep.shape[1:], LOW)],
            deep,
            *wide,
            after=after,
            plain=plain,
        )
        return mine, to_core(mine)


    def gathered(pieces, start):
        return jnp.concatenate(
            [piece[:, start : start + own].reshape(-1, width) for piece in pieces], axis=0
        )

    def front(unit, statics, edges, order, *pieces):
        vectors = sum(
            piece[k, 2 * own :].astype(FULL) for piece in pieces for k in range(depth)
        )
        lines = dot(vectors.astype(LOW), order)
        normed = unit * lines[0:1] + lines[2:3]
        edge_normed = edges[0:1] * lines[0:1] + lines[2:3]
        prior = down(normed, edge_normed, plain) * statics[:, :1]
        mix_key = mixing(normed, prior, lines[4:5])
        mix_value = mixing(normed, prior, lines[5:6])
        mix_recept = mixing(normed, prior, lines[6:7])
        key_all, value_all = gathered(pieces, 0), gathered(pieces, own)
        key, value = dot(mix_key, key_all), dot(mix_value, value_all)
        pace = jnp.exp(vectors[9:10])
        left = length - 1.0 - row_index((length, width)).astype(FULL)
        den = jnp.where(statics[:, 2 * LANES : 2 * LANES + 1] > 0.5, jnp.exp(key - pace * left), 0.0)
        num = den * value
        message = stack_rows(
            [column_sum(num), column_sum(den), column_sum(num * left), column_sum(den * left)]
            + [edges[1:2], edges[2:3]]
        )
        return (
            jnp.concatenate([vectors, lines], axis=0),
            normed - prior,
            jnp.stack([mix_key, mix_value, mix_recept]),
            jnp.stack([key_all, value_all]),
            key,
            value,
            message,
            jnp.stack([to_lanes(jnp.exp(-pace)), to_lanes(vectors[10:11])]),
        )

    (
        vectors,
        difference_one,
        mixes,
        first_all,
        key_act,
        value_act,
        message,
        rates,
    ) = fuse(
        front,
        [
            ((32, width), FULL),
            full_act,
            ((3, length, width), LOW),
            ((2, width, width), LOW),
            full_act,
            full_act,
            edge_row,
            ((2, width // LANES, LANES), FULL),
        ],
        unit_one,
        statics,
        edges,
        order,
        *first_pieces,
        plain=plain,
        limit=32,
        flops=2 * mac,
    )
    carry = carry_exchange(message, vectors, length, True, plain)
    mixes_got = to_core(mixes)

    def receptance(mixes, *pieces):
        recept_all, output_all = gathered(pieces, 0), gathered(pieces, own)
        return jax.nn.sigmoid(dot(mixes[2], recept_all)), jnp.stack([recept_all, output_all])

    recept_act, second_all = fuse(
        receptance,
        [full_act, ((2, width, width), LOW)],
        mixes,
        *joined(second_deep, second_wide, (message,)),
        plain=plain,
        limit=32,
        flops=mac,
    )
    key_tiles, value_tiles = to_tiles(key_act), to_tiles(value_act)
    scanned = run_forward(keep, key_tiles, value_tiles, rates, carry)

    def attend(scanned, recept, order, second_all, raw, vectors):
        gated = dot((recept * untile(scanned[0], width // LANES)).astype(LOW), order).astype(LOW)
        middle = raw.astype(FULL) + dot(gated, second_all[1])
        unit, scale = unit_norm(middle)
        normed = unit * vectors[1:2] + vectors[3:4]
        return (
            gated,
            middle,
            jnp.concatenate([unit, jnp.broadcast_to(scale, (length, LANES))], axis=1),
            stack_rows([normed[length - 1 :]]),
        )

    gated, middle, unit_two, edge_two = fuse(
        attend,
        [low_act, full_act, ((length, width + LANES), FULL), edge_row],
        scanned,
        recept_act,
        order,
        second_all,
        raw,
        vectors,
        plain=plain,
        flops=2 * mac,
    )
    edge_two = send_next(edge_two)

    def mix_two(unit, edge, statics, vectors):
        normed = unit[:, :width] * vectors[1:2] + vectors[3:4]
        prior = down(normed, edge[0:1], plain) * statics[:, :1]
        return (
            mixing(normed, prior, vectors[7:8]),
            mixing(normed, prior, vectors[8:9]),
            normed - prior,
        )

    mix_hidden, mix_gate, difference_two = fuse(
        mix_two, [low_act, low_act, full_act], unit_two, edge_two, statics, vectors, plain=plain
    )
    shared = [mix_hidden] + [to_batch(mix_hidden, k) for k in range(1, rows)]

    def channel(x, key, value):
        positive = jnp.maximum(dot(x, key), 0.0)
        squared = (positive * positive).astype(LOW)
        return squared, dot(squared, value)

    def channel_low(x, key, value):
        squared, out = channel(x, key, value)
        return squared, out.astype(LOW)

    hidden_act = ((length, part_width), LOW)
    squares, returned = [], []
    for k in range(rows):
        squared, out = fuse(
            channel_low if k else channel,
            [hidden_act, low_act if k else full_act],
            shared[k],
            part_key,
            part_value,
            plain=plain,
            flops=2 * mac,
        )
        squares.append(squared)
        returned.append(to_batch(out, k) if k else out)

    def gating(mix, order, *pieces):
        gate_all = gathered(pieces, 0)
        mix = dot(mix, order).astype(LOW)
        return jax.nn.sigmoid(dot(mix, gate_all)), mix, gate_all

    gate, mix_gate, gate_all = fuse(
        gating,
        [full_act, low_act, square],
        mix_gate,
        order,
        *joined(third_deep, third_wide, (gated,)),
        plain=plain,
        flops=2 * mac,
    )

    def finish(own_part, gate, middle, grad_out, *got):
        out = sum((x.astype(FULL) for x in got), own_part)
        grad_out = grad_out.astype(FULL)
        return (
            (middle + gate * out).astype(LOW),
            (grad_out * gate).astype(LOW),
            (grad_out * out * gate * (1.0 - gate)).astype(LOW),
        )

    block_output, grad_values, grad_gate = fuse(
        finish,
        [low_act, low_act, low_act],
        returned[0],
        gate,
        middle,
        cotangent,
        *returned[1:],
        plain=plain,
    )

    shared_grad = [grad_values] + [to_batch(grad_values, k) for k in range(1, rows)]

    def channel_back(grad, squared, key, value):
        positive = jnp.sqrt(squared.astype(FULL))
        hidden = (dot_back(grad, value) * 2.0 * positive).astype(LOW)
        return hidden, dot_back(hidden, key)

    def channel_back_low(grad, squared, key, value):
        hidden, out = channel_back(grad, squared, key, value)
        return hidden, out.astype(LOW)

    hiddens, returned = [], []
    for k in range(rows):
        hidden, out = fuse(
            channel_back_low if k else channel_back,
            [hidden_act, low_act if k else full_act],
            shared_grad[k],
            squares[k],
            part_key,
            part_value,
            plain=plain,
            flops=2 * mac,
        )
        hiddens.append(hidden)
        returned.append(to_batch(out, k) if k else out)

    def channel_terms(*x):
        shared, hiddens, squares, grads = (
            jnp.concatenate(x[i * rows : (i + 1) * rows], axis=0) for i in range(4)
        )
        key = dot_rows(shared, hiddens).astype(LOW)
        value = dot_rows(squares, grads).astype(LOW)
        key = key.reshape(rows, cols, own, part_width)
        value_rows = part_width // cols
        parts = []
        for j in range(cols):
            block = jnp.concatenate([key[i, j] for i in range(rows)], axis=0)
            parts += [
                block.reshape(cross_rows, width),
                value[j * value_rows : (j + 1) * value_rows],
            ]
        return (jnp.concatenate(parts, axis=0),)

    (channel_term,) = fuse(
        channel_terms,
        [((cols * packed_rows, width), LOW)],
        *shared,
        *hiddens,
        *squares,
        *shared_grad,
        after=returned[1:],
        plain=plain,
        limit=32,
        flops=2 * rows * mac,
    )
    channel_sum = lax.psum_scatter(channel_term, "seq", scatter_dimension=0, tiled=True)

    def gating_back(grad, gate_all, order):
        return (restore(dot_back(grad, gate_all), order),)

    (grad_mix_gate,) = fuse(
        gating_back, [full_act], grad_gate, gate_all, order, plain=plain, flops=3 * mac
    )

    def paired(active, active_got, grad, grad_got):
        return dot_rows(
            jnp.concatenate([active[:, :half], active_got[:, half:]], axis=0),
            jnp.concatenate([grad, grad_got], axis=0),
        ).astype(LOW)

    def cut(terms):
        part = half // rows
        return [
            jnp.stack([term[k * part : (k + 1) * part] for term in terms]) for k in range(rows)
        ]

    def gate_terms(mix_gate, mix_gate_got, grad_gate, grad_gate_got):
        return cut([paired(mix_gate, mix_gate_got, grad_gate, grad_gate_got)])

    def early_terms(gated, gated_got, mixes, mixes_got, grads, grads_got):
        return cut(
            [
                paired(gated, gated_got, grads[0], grads_got[0]),
                paired(mixes[2], mixes_got[2], grads[1], grads_got[1]),
            ]
        )

    mix_gate_got, grad_gate_got = to_core(mix_gate), to_core(grad_gate)
    gated_got = to_core(gated)
    gate_term = fuse(
        gate_terms,
        [((1, half // rows, width), LOW)] * rows,
        mix_gate,
        mix_gate_got,
        grad_gate,
        grad_gate_got,
        after=returned[1:],
        plain=plain,
        flops=mac,
    )
    gate_got = [to_batch(gate_term[k], k) for k in range(1, rows)]
    gate_pieces = add_batch(gate_term[0], gate_got, plain)

    def unmix_two(own_part, grad_gate, difference, statics, vectors, *got):
        grad_hidden = sum((x.astype(FULL) for x in got), own_part)
        mix_h, mix_g = vectors[7:8], vectors[8:9]
        passed = (grad_hidden * (1.0 - mix_h) + grad_gate * (1.0 - mix_g)) * statics[:, :1]
        return (
            grad_hidden * mix_h + grad_gate * mix_g,
            passed,
            stack_rows([passed[0:1]]),
            stack_rows([column_sum(grad_hidden * difference), column_sum(grad_gate * difference)]),
        )

    own_two, passed_two, after_two, mix_sums_two = fuse(
        unmix_two,
        [full_act, full_act, edge_row, edge_row],
        returned[0],
        grad_mix_gate,
        difference_two,
        statics,
        vectors,
        *returned[1:],
        plain=plain,
    )
    after_two = send_back(after_two)

    def middle_back(
        own_part, passed, after, unit, grad_out, vectors, mix_sums, recept, scanned,
        second_all, order, statics, edges,
    ):
        wkv, inverse, slope = (untile(scanned[i], width // LANES) for i in range(3))
        unit, scale = unit[:, :width], unit[:, width : width + 1]
        grad_normed = own_part + up(passed, after[0:1], plain)
        part = norm_backward(grad_normed, unit, scale, vectors[1:2])
        grad_middle = grad_out.astype(FULL) + part
        grad_low = grad_middle.astype(LOW)
        grad_gated = restore(dot_back(grad_low, second_all[1]), order)
        grad_wkv = grad_gated * recept
        grad_recept = (grad_wkv * wkv * (1.0 - recept)).astype(LOW)
        share = grad_wkv * inverse
        pace = jnp.exp(vectors[9:10])
        step = row_index((length, width)).astype(FULL)
        head = jnp.where(statics[:, LANES : LANES + 1] > 0.5, share * jnp.exp(-pace * step), 0.0)
        return (
            grad_middle,
            jnp.stack([grad_low, grad_recept]),
            share,
            stack_rows([column_sum(head), column_sum(head * wkv), edges[1:2], edges[2:3]]),
            stack_rows(
                [
                    column_sum(grad_normed * unit),
                    column_sum(grad_normed),
                    mix_sums[0:1],
                    mix_sums[1:2],
                    -pace * column_sum(grad_wkv * slope),
                ]
            ),
        )

    grad_middle, grad_pair, share, message, sums_two = fuse(
        middle_back,
        [full_act, ((2, length, width), LOW), full_act, edge_row, edge_row],
        own_two,
        passed_two,
        after_two,
        unit_two,
        cotangent,
        vectors,
        mix_sums_two,
        recept_act,
        scanned,
        second_all,
        order,
        statics,
        edges,
        after=(channel_term, gate_term[0]),
        plain=plain,
        limit=24,
        flops=3 * mac,
    )

    early = fuse(
        early_terms,
        [((2, half // rows, width), LOW)] * rows,
        gated,
        gated_got,
        mixes,
        mixes_got,
        grad_pair,
        to_core(grad_pair),
        plain=plain,
        limit=24,
        flops=2 * mac,
    )
    early_got = [to_batch(early[k], k) for k in range(1, rows)]

    carry_back = carry_exchange(message, vectors, length, False, plain, after=early)
    grad_key, grad_value, first_term = run_backward(
        keep, key_tiles, value_tiles, scanned, to_tiles(share), rates, carry_back
    )

    def lower(key, value):
        return (jnp.stack([key.astype(LOW), value.astype(LOW)]),)

    (grad_late,) = fuse(
        lower,
        [((2, length, width), LOW)],
        *lax.optimization_barrier((from_tiles(grad_key, width), from_tiles(grad_value, width))),
        plain=plain,
    )

    def late_terms(mixes, mixes_got, grads, grads_got):
        return cut([paired(mixes[i], mixes_got[i], grads[i], grads_got[i]) for i in range(2)])

    late = fuse(
        late_terms,
        [((2, half // rows, width), LOW)] * rows,
        mixes,
        mixes_got,
        grad_late,
        to_core(grad_late),
        after=gate_pieces,
        plain=plain,
        flops=2 * mac,
    )
    late_got = [to_batch(late[k], k) for k in range(1, rows)]
    early_pieces = add_batch(early[0], early_got, plain)
    output_grad, recept_grad = add_depth(early_pieces, plain)
    (gate_grad,) = add_depth(gate_pieces, plain)
    late_pieces = add_batch(late[0], late_got, plain, (output_grad, gate_grad))
    key_grad, value_grad = add_depth(late_pieces, plain)

    def unmix_one(grads, grad_pair, first_all, second_all, vectors, statics, difference, order):
        lines = vectors[16:]
        grad_key = dot_back(grads[0], first_all[0])
        grad_value = dot_back(grads[1], first_all[1])
        grad_recept = dot_back(grad_pair[1], second_all[0])
        m_key, m_value, m_recept = lines[4:5], lines[5:6], lines[6:7]
        passed = (
            grad_key * (1.0 - m_key) + grad_value * (1.0 - m_value) + grad_recept * (1.0 - m_recept)
        ) * statics[:, :1]
        return (
            grad_key * m_key + grad_value * m_value + grad_recept * m_recept,
            passed,
            restore(passed[:16], order)[:SUBS],
            stack_rows([column_sum(x * difference) for x in (grad_key, grad_value, grad_recept)]),
        )

    own_one, passed_one, after_one, mix_sums_one = fuse(
        unmix_one,
        [full_act, full_act, edge_row, edge_row],
        grad_late,
        grad_pair,
        first_all,
        second_all,
        vectors,
        statics,
        difference_one,
        order,
        plain=plain,
        limit=24,
        flops=3 * mac,
    )
    after_one = send_back(after_one)

    def input_back(
        own_part, passed, after, unit, statics, vectors, order, grad_middle, mix_sums, sums_two, first
    ):
        lines, scale = vectors[16:], statics[:, 3 * LANES : 3 * LANES + 1]
        after = jnp.where(row_index((16, width)) == 0, after[0:1], 0.0)
        grad_normed = own_part + up(passed, restore_in(after, order)[0:1], plain)
        part = norm_backward(grad_normed, unit, scale, lines[0:1])
        ordered = stack_rows(
            [
                column_sum(grad_normed * unit),
                column_sum(grad_normed),
                mix_sums[0:1],
                mix_sums[1:2],
                mix_sums[2:3],
            ],
            16,
        )
        ordered = restore(ordered, order)
        total = [ordered[0:1], sums_two[0:1], ordered[1:2], sums_two[1:2]]
        total += [ordered[2:3], ordered[3:4], ordered[4:5], sums_two[2:3], sums_two[3:4]]
        total += [sums_two[4:5], from_lanes(first)]
        return grad_middle + restore(part, order), stack_rows(total, 16)

    input_grad, sums = fuse(
        input_back,
        [full_act, ((16, width), FULL)],
        own_one,
        passed_one,
        after_one,
        unit_one,
        statics,
        vectors,
        order,
        grad_middle,
        mix_sums_one,
        sums_two,
        first_term,
        plain=plain,
        limit=24,
        flops=2 * mac,
    )
    sums = sums + to_core(sums)
    (sums,) = fuse(
        lambda *x: (sum(x[1:], x[0]),),
        [((16, width), FULL)],
        sums,
        *[to_batch(sums, k) for k in range(1, rows)],
        after=late_pieces,
        plain=plain,
    )

    def own_columns(*got):
        b, z, core = places()
        total = sum(got[1:], got[0])
        device = b * cols + z * 2 + core
        if plain:
            total = lax.dynamic_slice(total, (0, device * own), (16, own))
        else:
            total = pltpu.roll(total, (width - device * own) & (width - 1), 1)[:, :own]
        return total[0:2], total[2:4], total[4:9], total[9:10], total[10:11]

    gains_grad, offsets_grad, mixes_grad, decay_grad, first_grad = fuse(
        own_columns,
        [((2, own), FULL), ((2, own), FULL), ((5, own), FULL), ((1, own), FULL), ((1, own), FULL)],
        sums,
        *[to_depth(sums, k) for k in range(1, depth)],
        after=(key_grad,),
        plain=plain,
    )

    def uncross(x):
        b = places()[0]
        blocks = x[:cross_rows].reshape(rows, own, part_width)
        return [pick([blocks[j] for j in range(rows)], b ^ k) for k in range(rows)]

    leaving = fuse(uncross, [((own, part_width), LOW)] * rows, channel_sum, plain=plain)

    def assemble(x, *blocks):
        b = places()[0]
        blocks = [block.astype(FULL) for block in blocks]
        return (
            jnp.concatenate([pick(blocks, j ^ b) for j in range(rows)], axis=1),
            x[cross_rows:].astype(FULL),
        )

    channel_key_grad, channel_value_grad = fuse(
        assemble,
        [((own, hidden_width), FULL), (channel_value.shape, FULL)],
        channel_sum,
        leaving[0],
        *[to_batch(leaving[k], k) for k in range(1, rows)],
        plain=plain,
    )
    return (
        block_output[None],
        input_grad[None],
        key_grad,
        value_grad,
        recept_grad,
        output_grad,
        channel_key_grad,
        channel_value_grad,
        gate_grad,
        gains_grad,
        offsets_grad,
        mixes_grad,
        decay_grad[0],
        first_grad[0],
    )


def solution(mesh):
    tokens = P("batch", "seq", None)
    weight = P(BOTH, None)
    lines = P(None, BOTH)
    return jax.shard_map(
        per_device,
        mesh=mesh,
        in_specs=(tokens, P("batch", "seq"), tokens)
        + (weight,) * 7
        + (lines,) * 3
        + (P(BOTH),) * 2,
        out_specs=(tokens, tokens) + (weight,) * 7 + (lines,) * 3 + (P(BOTH),) * 2,
        check_vma=False,
    )
```

```python
import jax
import jax.numpy as jnp
from jax import lax
from jax.experimental import pallas as pl
from jax.experimental.pallas import tpu as pltpu
from jax.sharding import PartitionSpec as P

EPS = 1e-05
BOTH = ("batch", "seq")
LOW = jnp.bfloat16
FULL = jnp.float32
LANES = 128
SUBS = 8
MIB = 1024 * 1024
COST = 1024
IN_VMEM = pl.BlockSpec(memory_space=pltpu.VMEM)
IN_HBM = pl.BlockSpec(memory_space=pltpu.HBM)


def sizes():
    return lax.axis_size("batch"), lax.axis_size("seq")


def places():
    s = lax.axis_index("seq")
    return lax.axis_index("batch"), s >> 1, s & 1


def send(block, route):
    rows, cols = sizes()
    pairs = []
    for b in range(rows):
        for s in range(cols):
            target = route(b, s)
            if target is not None:
                pairs.append((b * cols + s, target[0] * cols + target[1]))
    return lax.ppermute(block, BOTH, pairs)


def send_next(block):
    cols = lax.axis_size("seq")
    return send(block, lambda b, s: (b, s + 1) if s + 1 < cols else None)


def send_back(block):
    return send(block, lambda b, s: (b, s - 1) if s > 0 else None)


def to_core(block):
    return send(block, lambda b, s: (b, s ^ 1))


def to_batch(block, k):
    return send(block, lambda b, s: (b ^ k, s))


def to_depth(block, k):
    return send(block, lambda b, s: (b, s ^ (2 * k)))


def fuse(body, outs, *args, after=(), limit=16, plain=False, fetch=False, token=False):
    if plain:
        return tuple(body(*args)) + (None,) * token
    after = [x for x in after if x is not None]
    count, held = len(args), len(args) + len(after)
    outs = [*outs, ((SUBS, LANES), FULL)] if token else outs

    def kernel(*refs):
        taken = refs[:count]
        if fetch:
            taken, arrived = refs[held + len(outs) : -1], refs[-1]
            copies = [
                pltpu.make_async_copy(refs[i], taken[i], arrived.at[i]) for i in range(count)
            ]
            for copy in copies:
                copy.start()
            for copy in copies:
                copy.wait()
        results = body(*[ref[...] for ref in taken])
        if token:
            results = [*results, jnp.zeros((SUBS, LANES), FULL)]
        for ref, value in zip(refs[held : held + len(outs)], results, strict=True):
            ref[...] = value


    return pl.pallas_call(
        kernel,
        out_shape=tuple(jax.ShapeDtypeStruct(shape, dtype) for shape, dtype in outs),
        in_specs=[IN_HBM if fetch else IN_VMEM] * count + [IN_VMEM] * len(after),
        out_specs=(IN_VMEM,) * len(outs),
        scratch_shapes=[pltpu.VMEM(x.shape, x.dtype) for x in args]
        + [pltpu.SemaphoreType.DMA((count,))]
        if fetch
        else [],
        compiler_params=pltpu.CompilerParams(vmem_limit_bytes=limit * MIB),
        cost_estimate=pl.CostEstimate(flops=COST, bytes_accessed=COST, transcendentals=0),
    )(*args, *after)


def dot(x, w):
    return lax.dot_general(x, w, (((1,), (0,)), ((), ())), preferred_element_type=FULL)


def dot_back(x, w):
    return lax.dot_general(x, w, (((1,), (1,)), ((), ())), preferred_element_type=FULL)


def dot_rows(x, y):
    return lax.dot_general(x, y, (((0,), (0,)), ((), ())), preferred_element_type=FULL)


def restore(x, order):
    high = x.astype(LOW)
    rest = (x - high.astype(FULL)).astype(LOW)
    return dot_back(high, order) + dot_back(rest, order)


def restore_in(x, order):
    high = x.astype(LOW)
    rest = (x - high.astype(FULL)).astype(LOW)
    return dot(high, order) + dot(rest, order)


def row_index(shape):
    return lax.broadcasted_iota(jnp.int32, shape, 0)


def stack_rows(rows, count=SUBS):
    width = rows[0].shape[1]
    index = row_index((count, width))
    out = jnp.zeros((count, width), FULL)
    for i, row in enumerate(rows):
        out = jnp.where(index == i, row, out)
    return out


def down(x, first, plain):
    rolled = jnp.roll(x, 1, 0) if plain else pltpu.roll(x, 1, 0)
    return jnp.where(row_index(x.shape) == 0, first, rolled)


def up(x, last, plain):
    count = x.shape[0]
    rolled = jnp.roll(x, -1, 0) if plain else pltpu.roll(x, count - 1, 0)
    return jnp.where(row_index(x.shape) == count - 1, last, rolled)


def column_sum(x):
    return jnp.sum(x, axis=0, keepdims=True)


def lane_mean(x):
    return jnp.mean(x, axis=-1, keepdims=True)


def unit_norm(hidden):
    centred = hidden - lane_mean(hidden)
    scale = lax.rsqrt(lane_mean(centred * centred) + EPS)
    return centred * scale, scale


def norm_backward(grad, unit, scale, gain):
    inner = grad * gain
    centred = inner - lane_mean(inner)
    return scale * (centred - unit * lane_mean(inner * unit))


def mixing(normed, prior, coeff):
    return (normed * coeff + prior * (1.0 - coeff)).astype(LOW)


def pick(values, index):
    out = values[0]
    for i in range(1, len(values)):
        out = jnp.where(index == i, values[i], out)
    return out


def log2(n):
    return n.bit_length() - 1


def untile(x, blocks):
    count = x.shape[0] // blocks
    x = x.reshape(count // SUBS, blocks, SUBS, LANES)
    return jnp.concatenate([x[:, i].reshape(count, LANES) for i in range(blocks)], axis=1)


def to_lanes(row):
    return jnp.concatenate(
        [row[:, i * LANES : (i + 1) * LANES] for i in range(row.shape[1] // LANES)], axis=0
    )


def from_lanes(x):
    return jnp.concatenate([x[i : i + 1] for i in range(x.shape[0])], axis=1)


def to_tiles(x):
    count, width = x.shape
    blocks = width // LANES
    x = x.reshape(count // SUBS, SUBS, blocks, LANES).transpose(0, 2, 1, 3)
    return x.reshape(count * blocks, LANES)


def from_tiles(x, width):
    blocks = width // LANES
    count = x.shape[0] // blocks
    x = x.reshape(count // SUBS, blocks, SUBS, LANES).transpose(0, 2, 1, 3)
    return x.reshape(count, width)


def position(i, r, blocks):
    return pl.ds(i * (SUBS * blocks) + r, blocks, stride=SUBS)


def forward_scan(keep_ref, key_ref, value_ref, rates_ref, carry_ref, out_ref):
    blocks = rates_ref.shape[1]
    fade, bonus = rates_ref[0], rates_ref[1]

    def eight(i, state):
        num, den, num_slope, den_slope = state
        for r in range(SUBS):
            at = position(i, r, blocks)
            key, value = key_ref[at, :], value_ref[at, :]
            keep = keep_ref[pl.ds(i * SUBS + r, 1), :]
            num, den, num_slope, den_slope = (
                num * keep,
                den * keep,
                num_slope * keep,
                den_slope * keep,
            )
            reward = jnp.exp(bonus + key)
            weight = jnp.exp(key)
            inverse = 1.0 / (den + reward)
            wkv = (num + reward * value) * inverse
            out_ref[0, at, :] = wkv
            out_ref[1, at, :] = inverse
            out_ref[2, at, :] = (num_slope - wkv * den_slope) * inverse
            num_slope = fade * (num_slope + num)
            den_slope = fade * (den_slope + den)
            num = fade * num + weight * value
            den = fade * den + weight
        return num, den, num_slope, den_slope

    lax.fori_loop(
        0,
        keep_ref.shape[0] // SUBS,
        eight,
        (carry_ref[0], carry_ref[1], carry_ref[2], carry_ref[3]),
    )


def backward_scan(
    keep_ref, key_ref, value_ref, scanned_ref, share_ref, rates_ref, carry_ref, key_out, value_out, first_out
):
    blocks = rates_ref.shape[1]
    fade, bonus = rates_ref[0], rates_ref[1]
    groups = keep_ref.shape[0] // SUBS

    def eight(step, state):
        direct, scaled, first = state
        i = groups - 1 - step
        for r in reversed(range(SUBS)):
            at = position(i, r, blocks)
            key, value = key_ref[at, :], value_ref[at, :]
            wkv, share = scanned_ref[0, at, :], share_ref[at, :]
            keep = keep_ref[pl.ds(i * SUBS + r, 1), :]
            reward = share * jnp.exp(bonus + key)
            weight = jnp.exp(key)
            bonus_part = reward * (value - wkv)
            key_out[at, :] = weight * (direct * value - scaled) + bonus_part
            value_out[at, :] = weight * direct + reward
            first = first + bonus_part
            direct = (share + fade * direct) * keep
            scaled = (share * wkv + fade * scaled) * keep
        return direct, scaled, first

    first_out[...] = lax.fori_loop(
        0, groups, eight, (carry_ref[0], carry_ref[1], jnp.zeros_like(fade))
    )[2]


def run_forward(keep, key, value, rates, carry):
    return pl.pallas_call(
        forward_scan,
        out_shape=jax.ShapeDtypeStruct((3,) + key.shape, FULL),
        in_specs=[IN_VMEM] * 5,
        out_specs=IN_VMEM,
        compiler_params=pltpu.CompilerParams(vmem_limit_bytes=8 * MIB),
        cost_estimate=pl.CostEstimate(
            flops=20 * key.size, bytes_accessed=20 * key.size, transcendentals=3 * key.size
        ),
    )(keep, key, value, rates, carry)


def run_backward(keep, key, value, wkv, share, rates, carry):
    tiles = jax.ShapeDtypeStruct(key.shape, FULL)
    return pl.pallas_call(
        backward_scan,
        out_shape=(tiles, tiles, jax.ShapeDtypeStruct(rates.shape[1:], FULL)),
        in_specs=[IN_VMEM] * 7,
        out_specs=(IN_VMEM,) * 3,
        compiler_params=pltpu.CompilerParams(vmem_limit_bytes=8 * MIB),
        cost_estimate=pl.CostEstimate(
            flops=20 * key.size, bytes_accessed=24 * key.size, transcendentals=2 * key.size
        ),
    )(keep, key, value, wkv, share, rates, carry)


def moved(sums, span, pace):
    fade = jnp.exp(-pace * span)
    if len(sums) == 4:
        num, den, num_slope, den_slope = sums
        return [
            fade * num,
            fade * den,
            fade * (num_slope + span * num),
            fade * (den_slope + span * den),
        ]
    return [fade * x for x in sums]


def split_message(message, count):
    return [message[i : i + 1] for i in range(count)], message[count : count + 1], message[count + 1 : count + 2]


def by_place(message, other):
    core = places()[2]
    return jnp.where(core == 0, message, other), jnp.where(core == 0, other, message)


def chip_sums(count, length, forward):
    def body(message, other, vectors):
        pace = jnp.exp(vectors[9:10])
        first, second = by_place(message, other)
        one, one_last, one_before = split_message(first, count)
        two, two_last, _ = split_message(second, count)
        near, far = (two, one) if forward else (one, two)
        through = (two_last == one_last) if forward else (one_last == one_before)
        far = moved(far, float(length), pace)
        sums = [n + jnp.where(through, f, 0.0) for n, f in zip(near, far, strict=True)]
        return (stack_rows(sums + [two_last, one_before]),)

    return body


def carried(count, length, forward):
    def body(message, other, vectors, *got):
        depth = len(got) + 1
        _, z, core = places()
        pace = jnp.exp(vectors[9:10])
        first, second = by_place(message, other)
        one, one_last, one_before = split_message(first, count)
        two, two_last, _ = split_message(second, count)
        total = [jnp.zeros_like(x) for x in one]
        for k in range(1, depth):
            sums, last, before = split_message(got[k - 1], count)
            if forward:
                valid = (last == one_before) & (z >= k)
            else:
                valid = (before == two_last) & (z < depth - k)
            sums = moved(sums, 2.0 * length * (k - 1), pace)
            total = [t + jnp.where(valid, x, 0.0) for t, x in zip(total, sums, strict=True)]
        inner, through = (one, one_last == one_before) if forward else (two, two_last == one_last)
        passed = moved(total, float(length), pace)
        passed = [x + jnp.where(through, y, 0.0) for x, y in zip(inner, passed, strict=True)]
        chosen = core == (1 if forward else 0)
        return (
            jnp.stack(
                [to_lanes(jnp.where(chosen, p, t)) for p, t in zip(passed, total, strict=True)]
            ),
        )

    return body


def carry_start(values, vectors, length, forward, plain):
    cols = lax.axis_size("seq")
    count = 4 if forward else 2
    other = to_core(values)
    (chip,) = fuse(
        chip_sums(count, length, forward),
        [((SUBS, values.shape[1]), FULL)],
        values,
        other,
        vectors,
        plain=plain,
    )
    step = 1 if forward else -1

    def route(k):
        def go(b, s):
            target = s + 2 * k * step
            return (b, target) if 0 <= target < cols else None

        return go

    return chip, [values, other, vectors] + [send(chip, route(k)) for k in range(1, cols // 2)]


def carry_end(parts, length, forward, plain, after=()):
    count = 4 if forward else 2
    return fuse(
        carried(count, length, forward),
        [((count, parts[0].shape[1] // LANES, LANES), FULL)],
        *parts,
        after=after,
        plain=plain,
    )[0]


def split_parts(x):
    high = x.astype(LOW)
    return [high, (x - high.astype(FULL)).astype(LOW)]


def add_batch(own, got, count, plain, after=(), vectors=None):
    depth = lax.axis_size("seq") // 2
    height, width = own.shape
    extra = 32 if vectors is not None else 0
    height -= extra
    part = height // (count * depth)
    inputs = [own, *got] + ([vectors] if extra else [])

    def body(own, *got):
        got, sums = (got[:-1], got[-1]) if extra else (got, None)
        got = [x.astype(FULL) for x in got]
        total = sum((x[:height] for x in got), own[:height].astype(FULL))
        blocks = [
            [total[(i * depth + k) * part : (i * depth + k + 1) * part] for i in range(count)]
            for k in range(depth)
        ]
        first, rest = blocks[0], [[x.astype(LOW) for x in block] for block in blocks[1:]]
        if extra:
            sums = sum((x[height : height + 16] + x[height + 16 :] for x in got), sums)
            first, rest = first + [sums], [block + split_parts(sums) for block in rest]
        return [jnp.concatenate(x, axis=0) for x in [first, *rest]]

    return fuse(
        body,
        [((count * part + extra // 2, width), FULL)]
        + [((count * part + extra, width), LOW)] * (depth - 1),
        *inputs,
        after=after,
        plain=plain,
        token=True,
    )


def add_depth(pieces, count, part, outs, last, plain, after=()):
    width = pieces[0].shape[1]
    height = count * part
    got = [to_depth(pieces[k], k) for k in range(1, len(pieces))]

    def body(own, *got):
        got = [x.astype(FULL) for x in got]
        total = sum((x[:height] for x in got), own[:height])
        results = [total[i * part : (i + 1) * part] for i in range(count)]
        if last is not None:
            sums = sum((x[height : height + 16] + x[height + 16 :] for x in got), own[height:])
            results += last(sums)
        return results

    return fuse(
        body, [((part, width), FULL)] * count + outs, pieces[0], *got, after=after, plain=plain
    )


def halve_depth(pieces, plain):
    half = len(pieces) // 2
    height, width = pieces[0].shape
    joined = fuse(
        lambda *x: (jnp.concatenate(x, axis=0),),
        [((half * height, width), LOW)],
        *pieces[half:],
        plain=plain,
    )[0]
    got = to_depth(joined, half)

    def body(own, *rest):
        rest, got = rest[:-1], rest[-1].astype(FULL)
        blocks = [got[i * height : (i + 1) * height] for i in range(half)]
        return [own + blocks[0]] + [
            (x.astype(FULL) + y).astype(LOW) for x, y in zip(rest, blocks[1:], strict=True)
        ]

    return fuse(
        body,
        [((height, width), FULL)] + [((height, width), LOW)] * (half - 1),
        *pieces[:half],
        got,
        plain=plain,
        token=True,
    )


def per_device(
    layer_input,
    segment_ids,
    out_cotangent,
    key_weight,
    value_weight,
    recept_weight,
    output_weight,
    channel_key,
    channel_value,
    channel_recept,
    norm_gains,
    norm_offsets,
    mix_coeffs,
    time_decay,
    time_first,
):
    rows, cols = sizes()
    depth = cols // 2
    length, width = layer_input.shape[1:]
    own = key_weight.shape[0]
    hidden_width = channel_key.shape[1]
    part_width = hidden_width // rows
    half = width // 2
    plain = own % 16 != 0
    low_act, full_act = ((length, width), LOW), ((length, width), FULL)
    narrow = ((length, LANES), FULL)
    square = ((width, width), LOW)
    edge_row = ((SUBS, width), FULL)
    raw, cotangent = layer_input[0], out_cotangent[0]
    mac = 2 * length * width * width

    small = [norm_gains, norm_offsets, mix_coeffs, time_decay[None], time_first[None]]
    n_vectors = sum(x.shape[0] for x in small)

    def prepare(key, value, recept, output, gate, cross, raw, ids, *small):
        b, z, core = places()
        device = b * cols + z * 2 + core
        lane = lax.broadcasted_iota(jnp.int32, (own, width), 1)
        home = (lane == device * own + row_index((own, width))).astype(FULL).astype(LOW)
        placed = jnp.zeros((16, width), FULL)
        at = 0
        for x in small:
            x = dot(x, home)
            for i in range(x.shape[0]):
                placed = jnp.where(row_index(placed.shape) == at, x[i : i + 1], placed)
                at += 1
        blocks = [cross[:, j * part_width : (j + 1) * part_width] for j in range(rows)]
        ids = ids.astype(FULL)
        last = raw[length - 16 :].astype(FULL)[15:16]
        edge = stack_rows([last, jnp.broadcast_to(ids[:, length - 1 :], (1, width))], 16)
        return (
            [
                jnp.concatenate([key, value, placed.astype(LOW)], axis=0),
                jnp.concatenate([recept, output, gate], axis=0),
                edge,
                jnp.broadcast_to(ids, (LANES, length)).T,
            ]
            + [pick(blocks, b ^ k) for k in range(rows)]
        )

    first_pack, second_pack, edge, ids_lanes, *crossing = fuse(
        prepare,
        [((2 * own + 16, width), LOW), ((3 * own, width), LOW), ((16, width), FULL), narrow]
        + [((own, part_width), LOW)] * rows,
        key_weight,
        value_weight,
        recept_weight,
        output_weight,
        channel_recept,
        channel_key,
        raw,
        segment_ids,
        *small,
        plain=plain,
        fetch=True,
        limit=58,
    )
    deep_got = [to_depth(first_pack, k) for k in range(1, depth)]
    cross_got = [to_batch(crossing[k], k) for k in range(1, rows)]
    edge = send_next(edge)

    def begin(raw, edge, ids):
        b, z, core = places()
        place = lax.broadcasted_iota(jnp.int32, (1, width), 1)
        block, row = place >> log2(own), place & (own - 1)
        k_core = block >> log2(rows * depth)
        k_batch = (block >> log2(depth)) & (rows - 1)
        k_depth = block & (depth - 1)
        target = ((k_batch ^ b) << log2(cols)) + ((k_depth ^ z) << 1) + (k_core ^ core)
        feature = (target << log2(own)) + row
        order = jnp.concatenate(
            [
                (row_index((LANES, width)) + i * LANES == feature).astype(FULL).astype(LOW)
                for i in range(width // LANES)
            ],
            axis=0,
        )
        unit, scale = unit_norm(dot(raw, order))
        edge_unit = unit_norm(dot(edge.astype(LOW), order))[0]
        before = jnp.where((z == 0) & (core == 0), -1.0, edge[1:2])
        before_lanes = before[:, :LANES]
        last = ids[length - 1 : length]
        keep = (ids == down(ids, before_lanes, plain)).astype(FULL)
        opened = (ids == before_lanes).astype(FULL)
        closing = (ids == last).astype(FULL)
        last = jnp.broadcast_to(last[:, :1], (1, width))
        scale = jnp.broadcast_to(scale, (length, LANES))
        return (
            order,
            unit,
            keep,
            jnp.concatenate([keep, opened, closing, scale], axis=1),
            stack_rows([edge_unit[0:1], last, before]),
        )

    order, unit_one, keep, statics, edges = fuse(
        begin,
        [square, full_act, narrow, ((length, 4 * LANES), FULL), edge_row],
        raw,
        edge,
        ids_lanes,
        plain=plain,
    )

    first_deep, second_pack = fuse(
        lambda second, *x: (jnp.stack(x), second),
        [((depth,) + first_pack.shape, LOW), (second_pack.shape, LOW)],
        second_pack,
        first_pack,
        *deep_got,
        after=(order, *cross_got),
        plain=plain,
    )
    first_wide = [to_batch(first_deep, k) for k in range(1, rows)]
    first_pieces = [first_deep] + first_wide
    first_pieces = first_pieces + [to_core(piece) for piece in first_pieces]
    second_got = [to_depth(second_pack, k) for k in range(1, depth)]

    cross_rows = rows * own * part_width // width
    packed_rows = cross_rows + channel_value.shape[0]

    def deepen(value, *x):
        b = places()[0]
        cross, x = x[:rows], x[rows:]
        cross = jnp.concatenate([pick(cross, j ^ b) for j in range(rows)], axis=0)
        return (
            jnp.stack([y[: 2 * own] for y in x]),
            jnp.stack([y[2 * own :] for y in x]),
            jnp.concatenate([cross.reshape(cross_rows, width), value], axis=0),
        )

    second_deep, third_deep, channel_pack = fuse(
        deepen,
        [
            ((depth, 2 * own, width), LOW),
            ((depth, own, width), LOW),
            ((packed_rows, width), LOW),
        ],
        channel_value,
        crossing[0],
        *cross_got,
        second_pack,
        *second_got,
        after=first_wide,
        plain=plain,
    )
    channel_pack = lax.all_gather(channel_pack, "seq", axis=0, tiled=True)

    def unpack_channel(x):
        x = x.reshape(cols, packed_rows, width)
        key = x[:, :cross_rows].reshape(cols, rows, own, part_width)
        key = jnp.concatenate(
            [key[j, i] for i in range(rows) for j in range(cols)], axis=0
        )
        return key, x[:, cross_rows:].reshape(part_width, width)

    part_key, part_value = fuse(
        unpack_channel,
        [((width, part_width), LOW), ((part_width, width), LOW)],
        channel_pack,
        plain=plain,
    )

    second_wide = [to_batch(second_deep, k) for k in range(1, rows)]
    (third_deep,) = fuse(
        lambda x: (x,), [(third_deep.shape, LOW)], third_deep, after=second_wide, plain=plain
    )
    third_wide = [to_batch(third_deep, k) for k in range(1, rows)]

    def joined(deep, wide, after):
        (mine,) = fuse(
            lambda *x: (jnp.concatenate(x, axis=0),),
            [((rows * depth,) + deep.shape[1:], LOW)],
            deep,
            *wide,
            after=after,
            plain=plain,
        )
        return mine, to_core(mine)


    def gathered(pieces, start):
        return jnp.concatenate(
            [piece[:, start : start + own].reshape(-1, width) for piece in pieces], axis=0
        )

    def front(unit, statics, edges, order, *pieces):
        vectors = sum(
            piece[k, 2 * own :].astype(FULL) for piece in pieces for k in range(depth)
        )
        lines = dot(vectors.astype(LOW), order)
        normed = unit * lines[0:1] + lines[2:3]
        edge_normed = edges[0:1] * lines[0:1] + lines[2:3]
        prior = down(normed, edge_normed, plain) * statics[:, :1]
        mix_key = mixing(normed, prior, lines[4:5])
        mix_value = mixing(normed, prior, lines[5:6])
        mix_recept = mixing(normed, prior, lines[6:7])
        key_all, value_all = gathered(pieces, 0), gathered(pieces, own)
        key, value = dot(mix_key, key_all), dot(mix_value, value_all)
        pace = jnp.exp(vectors[9:10])
        left = length - 1.0 - row_index((length, width)).astype(FULL)
        den = jnp.where(statics[:, 2 * LANES : 2 * LANES + 1] > 0.5, jnp.exp(key - pace * left), 0.0)
        num = den * value
        message = stack_rows(
            [column_sum(num), column_sum(den), column_sum(num * left), column_sum(den * left)]
            + [edges[1:2], edges[2:3]]
        )
        return (
            jnp.concatenate([vectors, lines], axis=0),
            normed - prior,
            jnp.stack([mix_key, mix_value, mix_recept]),
            jnp.stack([key_all, value_all]),
            key,
            value,
            message,
            jnp.stack([to_lanes(jnp.exp(-pace)), to_lanes(vectors[10:11])]),
        )

    (
        vectors,
        difference_one,
        mixes,
        first_all,
        key_act,
        value_act,
        message,
        rates,
    ) = fuse(
        front,
        [
            ((32, width), FULL),
            full_act,
            ((3, length, width), LOW),
            ((2, width, width), LOW),
            full_act,
            full_act,
            edge_row,
            ((2, width // LANES, LANES), FULL),
        ],
        unit_one,
        statics,
        edges,
        order,
        *first_pieces,
        plain=plain,
        limit=32,
    )
    carry = carry_end(carry_start(message, vectors, length, True, plain)[1], length, True, plain)

    def receptance(mixes, *pieces):
        recept_all = gathered(pieces, 0)
        return jax.nn.sigmoid(dot(mixes[2], recept_all)), recept_all, gathered(pieces, own)

    recept_act, recept_all, output_all = fuse(
        receptance,
        [full_act, square, square],
        mixes,
        *joined(second_deep, second_wide, (carry,)),
        plain=plain,
        limit=32,
    )
    key_tiles, value_tiles = to_tiles(key_act), to_tiles(value_act)
    scanned = run_forward(keep, key_tiles, value_tiles, rates, carry)

    def attend(scanned, recept, order, output_all, raw, vectors):
        gated = dot((recept * untile(scanned[0], width // LANES)).astype(LOW), order).astype(LOW)
        middle = raw.astype(FULL) + dot(gated, output_all)
        unit, scale = unit_norm(middle)
        normed = unit * vectors[1:2] + vectors[3:4]
        return (
            gated,
            middle,
            jnp.concatenate([unit, jnp.broadcast_to(scale, (length, LANES))], axis=1),
            stack_rows([normed[length - 1 :]]),
        )

    gated, middle, unit_two, edge_two = fuse(
        attend,
        [low_act, full_act, ((length, width + LANES), FULL), edge_row],
        scanned,
        recept_act,
        order,
        output_all,
        raw,
        vectors,
        plain=plain,
    )
    edge_two = send_next(edge_two)

    def mix_two(unit, edge, statics, vectors):
        normed = unit[:, :width] * vectors[1:2] + vectors[3:4]
        prior = down(normed, edge[0:1], plain) * statics[:, :1]
        return (
            mixing(normed, prior, vectors[7:8]),
            mixing(normed, prior, vectors[8:9]),
            normed - prior,
        )

    mix_hidden, mix_gate, difference_two = fuse(
        mix_two, [low_act, low_act, full_act], unit_two, edge_two, statics, vectors, plain=plain
    )
    shared = [mix_hidden] + [to_batch(mix_hidden, k) for k in range(1, rows)]

    def channel(x, key, value):
        positive = jnp.maximum(dot(x, key), 0.0)
        squared = (positive * positive).astype(LOW)
        return squared, dot(squared, value)

    def channel_low(x, key, value):
        squared, out = channel(x, key, value)
        return squared, out.astype(LOW)

    hidden_act = ((length, part_width), LOW)
    squares, returned = [], []
    for k in range(rows):
        squared, out = fuse(
            channel_low if k else channel,
            [hidden_act, low_act if k else full_act],
            shared[k],
            part_key,
            part_value,
            plain=plain,
        )
        squares.append(squared)
        returned.append(to_batch(out, k) if k else out)

    def gating(mix, order, gated, mixes, *pieces):
        gate_all = gathered(pieces, 0)
        mix = dot(mix, order).astype(LOW)
        sides = jnp.stack([mixes[0], mixes[1], mixes[2], gated, mix])
        return jax.nn.sigmoid(dot(mix, gate_all)), sides, gate_all

    gate, sides, gate_all = fuse(
        gating,
        [full_act, ((5, length, width), LOW), square],
        mix_gate,
        order,
        gated,
        mixes,
        *joined(third_deep, third_wide, (edge_two,)),
        plain=plain,
    )

    def finish(own_part, gate, middle, grad_out, *got):
        out = sum((x.astype(FULL) for x in got), own_part)
        grad_out = grad_out.astype(FULL)
        return (
            (middle + gate * out).astype(LOW),
            (grad_out * gate).astype(LOW),
            (grad_out * out * gate * (1.0 - gate)).astype(LOW),
        )

    block_output, grad_values, grad_gate = fuse(
        finish,
        [low_act, low_act, low_act],
        returned[0],
        gate,
        middle,
        cotangent,
        *returned[1:],
        plain=plain,
    )

    shared_grad = [grad_values] + [to_batch(grad_values, k) for k in range(1, rows)]

    def channel_back(grad, squared, key, value):
        positive = jnp.sqrt(squared.astype(FULL))
        hidden = (dot_back(grad, value) * 2.0 * positive).astype(LOW)
        return hidden, dot_back(hidden, key)

    def channel_back_low(grad, squared, key, value):
        hidden, out = channel_back(grad, squared, key, value)
        return hidden, out.astype(LOW)

    def channel_back_own(grad, squared, key, value, grad_gate, gate_all, order):
        hidden, out = channel_back(grad, squared, key, value)
        return hidden, out, restore(dot_back(grad_gate, gate_all), order)

    hidden, out, grad_mix_gate = fuse(
        channel_back_own,
        [hidden_act, full_act, full_act],
        shared_grad[0],
        squares[0],
        part_key,
        part_value,
        grad_gate,
        gate_all,
        order,
        plain=plain,
    )
    hiddens, returned = [hidden], [out]
    for k in range(1, rows):
        hidden, out = fuse(
            channel_back_low,
            [hidden_act, low_act],
            shared_grad[k],
            squares[k],
            part_key,
            part_value,
            plain=plain,
        )
        hiddens.append(hidden)
        returned.append(to_batch(out, k))

    def paired(active, active_got, grad, grad_got):
        return dot_rows(
            jnp.concatenate([active[:, :half], active_got[:, half:]], axis=0),
            jnp.concatenate([grad, grad_got], axis=0),
        ).astype(LOW)

    def cut(terms, *more):
        part = half // rows
        return [
            jnp.concatenate([term[k * part : (k + 1) * part] for term in terms] + list(more), axis=0)
            for k in range(rows)
        ]

    def early_terms(sides, sides_got, grads, grads_got):
        return cut(
            [
                paired(sides[side], sides_got[side], grads[i], grads_got[i])
                for i, side in enumerate((3, 2, 4))
            ]
        )

    sides_got = to_core(sides)

    def unmix_two(own_part, grad_gate, difference, statics, vectors, *got):
        grad_hidden = sum((x.astype(FULL) for x in got), own_part)
        mix_h, mix_g = vectors[7:8], vectors[8:9]
        passed = (grad_hidden * (1.0 - mix_h) + grad_gate * (1.0 - mix_g)) * statics[:, :1]
        return (
            grad_hidden * mix_h + grad_gate * mix_g,
            passed,
            stack_rows([passed[0:1]]),
            stack_rows([column_sum(grad_hidden * difference), column_sum(grad_gate * difference)]),
        )

    own_two, passed_two, after_two, mix_sums_two = fuse(
        unmix_two,
        [full_act, full_act, edge_row, edge_row],
        returned[0],
        grad_mix_gate,
        difference_two,
        statics,
        vectors,
        *returned[1:],
        plain=plain,
    )
    after_two = send_back(after_two)

    def middle_back(
        own_part, passed, after, unit, grad_out, vectors, mix_sums, recept, scanned,
        output_all, order, statics, edges, grad_gate,
    ):
        wkv, inverse, slope = (untile(scanned[i], width // LANES) for i in range(3))
        unit, scale = unit[:, :width], unit[:, width : width + 1]
        grad_normed = own_part + up(passed, after[0:1], plain)
        part = norm_backward(grad_normed, unit, scale, vectors[1:2])
        grad_middle = grad_out.astype(FULL) + part
        grad_low = grad_middle.astype(LOW)
        grad_gated = restore(dot_back(grad_low, output_all), order)
        grad_wkv = grad_gated * recept
        grad_recept = (grad_wkv * wkv * (1.0 - recept)).astype(LOW)
        share = grad_wkv * inverse
        pace = jnp.exp(vectors[9:10])
        step = row_index((length, width)).astype(FULL)
        head = jnp.where(statics[:, LANES : LANES + 1] > 0.5, share * jnp.exp(-pace * step), 0.0)
        return (
            grad_middle,
            jnp.stack([grad_low, grad_recept, grad_gate]),
            share,
            stack_rows([column_sum(head), column_sum(head * wkv), edges[1:2], edges[2:3]]),
            stack_rows(
                [
                    column_sum(grad_normed * unit),
                    column_sum(grad_normed),
                    mix_sums[0:1],
                    mix_sums[1:2],
                    -pace * column_sum(grad_wkv * slope),
                ]
            ),
        )

    grad_middle, grad_three, share, message, sums_two = fuse(
        middle_back,
        [full_act, ((3, length, width), LOW), full_act, edge_row, edge_row],
        own_two,
        passed_two,
        after_two,
        unit_two,
        cotangent,
        vectors,
        mix_sums_two,
        recept_act,
        scanned,
        output_all,
        order,
        statics,
        edges,
        grad_gate,
        plain=plain,
        limit=24,
    )

    chip_back, carry_parts = carry_start(message, vectors, length, False, plain)

    *early, early_token = fuse(
        early_terms,
        [((3 * half // rows, width), LOW)] * rows,
        sides,
        sides_got,
        grad_three,
        to_core(grad_three),
        after=(chip_back,),
        plain=plain,
        token=True,
    )
    def channel_terms(*x):
        shared, hiddens, squares, grads = (
            jnp.concatenate(x[i * rows : (i + 1) * rows], axis=0) for i in range(4)
        )
        key = dot_rows(shared, hiddens).astype(LOW)
        value = dot_rows(squares, grads).astype(LOW)
        key = key.reshape(rows, cols, own, part_width)
        value_rows = part_width // cols
        parts = []
        for j in range(cols):
            block = jnp.concatenate([key[i, j] for i in range(rows)], axis=0)
            parts += [
                block.reshape(cross_rows, width),
                value[j * value_rows : (j + 1) * value_rows],
            ]
        return (jnp.concatenate(parts, axis=0),)

    channel_term, channel_token = fuse(
        channel_terms,
        [((cols * packed_rows, width), LOW)],
        *shared,
        *hiddens,
        *squares,
        *shared_grad,
        after=(early_token,),
        plain=plain,
        token=True,
        limit=32,
    )
    channel_sum = lax.psum_scatter(channel_term, "seq", scatter_dimension=0, tiled=True)
    carry_back = carry_end(carry_parts, length, False, plain, (channel_token, early_token))
    grad_key, grad_value, first_term = run_backward(
        keep, key_tiles, value_tiles, scanned, to_tiles(share), rates, carry_back
    )

    def lower(key, value):
        return (jnp.stack([key.astype(LOW), value.astype(LOW)]),)

    (grad_late,) = fuse(
        lower,
        [((2, length, width), LOW)],
        *lax.optimization_barrier((from_tiles(grad_key, width), from_tiles(grad_value, width))),
        plain=plain,
    )

    def unmix_one(grads, grad_three, first_all, recept_all, vectors, statics, difference, order):
        lines = vectors[16:]
        grad_key = dot_back(grads[0], first_all[0])
        grad_value = dot_back(grads[1], first_all[1])
        grad_recept = dot_back(grad_three[1], recept_all)
        m_key, m_value, m_recept = lines[4:5], lines[5:6], lines[6:7]
        passed = (
            grad_key * (1.0 - m_key) + grad_value * (1.0 - m_value) + grad_recept * (1.0 - m_recept)
        ) * statics[:, :1]
        return (
            grad_key * m_key + grad_value * m_value + grad_recept * m_recept,
            passed,
            restore(passed[:16], order)[:SUBS],
            stack_rows([column_sum(x * difference) for x in (grad_key, grad_value, grad_recept)]),
        )

    own_one, passed_one, after_one, mix_sums_one = fuse(
        unmix_one,
        [full_act, full_act, edge_row, edge_row],
        grad_late,
        grad_three,
        first_all,
        recept_all,
        vectors,
        statics,
        difference_one,
        order,
        plain=plain,
        limit=24,
    )
    after_one = send_back(after_one)

    def input_back(
        own_part, passed, after, unit, statics, vectors, order, grad_middle, mix_sums, sums_two, first
    ):
        lines, scale = vectors[16:], statics[:, 3 * LANES : 3 * LANES + 1]
        after = jnp.where(row_index((16, width)) == 0, after[0:1], 0.0)
        grad_normed = own_part + up(passed, restore_in(after, order)[0:1], plain)
        part = norm_backward(grad_normed, unit, scale, lines[0:1])
        ordered = stack_rows(
            [
                column_sum(grad_normed * unit),
                column_sum(grad_normed),
                mix_sums[0:1],
                mix_sums[1:2],
                mix_sums[2:3],
            ],
            16,
        )
        ordered = restore(ordered, order)
        total = [ordered[0:1], sums_two[0:1], ordered[1:2], sums_two[1:2]]
        total += [ordered[2:3], ordered[3:4], ordered[4:5], sums_two[2:3], sums_two[3:4]]
        total += [sums_two[4:5], from_lanes(first)]
        return grad_middle + restore(part, order), stack_rows(total, 16)

    input_grad, sums = fuse(
        input_back,
        [full_act, ((16, width), FULL)],
        own_one,
        passed_one,
        after_one,
        unit_one,
        statics,
        vectors,
        order,
        grad_middle,
        mix_sums_one,
        sums_two,
        first_term,
        plain=plain,
        limit=24,
    )
    sums = sums + to_core(sums)
    early_got = [to_batch(early[k], k) for k in range(1, rows)]
    *early_pieces, early_wide_token = add_batch(early[0], early_got, 3, plain, (sums,))
    early_half = None
    if depth == 4:
        *early_pieces, early_half = halve_depth(early_pieces, plain)

    def late_terms(sides, sides_got, grads, grads_got, sums):
        terms = [paired(sides[i], sides_got[i], grads[i], grads_got[i]) for i in range(2)]
        return cut(terms, *split_parts(sums))

    late = fuse(
        late_terms,
        [((2 * half // rows + 32, width), LOW)] * rows,
        sides,
        sides_got,
        grad_late,
        to_core(grad_late),
        sums,
        after=(early_wide_token,),
        plain=plain,
    )
    late_got = [to_batch(late[k], k) for k in range(1, rows)]
    def own_columns(total):
        b, z, core = places()
        device = b * cols + z * 2 + core
        if plain:
            total = lax.dynamic_slice(total, (0, device * own), (16, own))
        else:
            total = pltpu.roll(total, (width - device * own) & (width - 1), 1)[:, :own]
        return [total[0:2], total[2:4], total[4:9], total[9:10], total[10:11]]

    *late_pieces, _ = add_batch(late[0], late_got, 2, plain, (early_half,), vectors=sums)
    output_grad, recept_grad, gate_grad = add_depth(early_pieces, 3, own, [], None, plain)
    key_grad, value_grad, gains_grad, offsets_grad, mixes_grad, decay_grad, first_grad = add_depth(
        late_pieces,
        2,
        own,
        [((2, own), FULL), ((2, own), FULL), ((5, own), FULL), ((1, own), FULL), ((1, own), FULL)],
        own_columns,
        plain,
    )

    crossed = channel_sum[:cross_rows].reshape(rows, own, part_width)
    crossed = lax.all_to_all(crossed, "batch", 0, 0)

    def assemble(x, crossed):
        return (
            jnp.concatenate([crossed[j].astype(FULL) for j in range(rows)], axis=1),
            x[cross_rows:].astype(FULL),
        )

    channel_key_grad, channel_value_grad = fuse(
        assemble,
        [((own, hidden_width), FULL), (channel_value.shape, FULL)],
        channel_sum,
        crossed,
        plain=plain,
    )
    return (
        block_output[None],
        input_grad[None],
        key_grad,
        value_grad,
        recept_grad,
        output_grad,
        channel_key_grad,
        channel_value_grad,
        gate_grad,
        gains_grad,
        offsets_grad,
        mixes_grad,
        decay_grad[0],
        first_grad[0],
    )


def solution(mesh):
    tokens = P("batch", "seq", None)
    weight = P(BOTH, None)
    lines = P(None, BOTH)
    return jax.shard_map(
        per_device,
        mesh=mesh,
        in_specs=(tokens, P("batch", "seq"), tokens)
        + (weight,) * 7
        + (lines,) * 3
        + (P(BOTH),) * 2,
        out_specs=(tokens, tokens) + (weight,) * 7 + (lines,) * 3 + (P(BOTH),) * 2,
        check_vma=False,
    )
```

```python
import jax
import jax.numpy as jnp
from jax import lax
from jax.experimental import pallas as pl
from jax.experimental.pallas import tpu as pltpu
from jax.sharding import PartitionSpec as P

EPS = 1e-05
BOTH = ("batch", "seq")
LOW = jnp.bfloat16
FULL = jnp.float32
LANES = 128
SUBS = 8
MIB = 1024 * 1024
COST = 1024
IN_VMEM = pl.BlockSpec(memory_space=pltpu.VMEM)
IN_HBM = pl.BlockSpec(memory_space=pltpu.HBM)


def sizes():
    return lax.axis_size("batch"), lax.axis_size("seq")


def places():
    s = lax.axis_index("seq")
    return lax.axis_index("batch"), s >> 1, s & 1


def send(block, route):
    rows, cols = sizes()
    pairs = []
    for b in range(rows):
        for s in range(cols):
            target = route(b, s)
            if target is not None:
                pairs.append((b * cols + s, target[0] * cols + target[1]))
    return lax.ppermute(block, BOTH, pairs)


def send_next(block):
    cols = lax.axis_size("seq")
    return send(block, lambda b, s: (b, s + 1) if s + 1 < cols else None)


def send_back(block):
    return send(block, lambda b, s: (b, s - 1) if s > 0 else None)


def to_core(block):
    return send(block, lambda b, s: (b, s ^ 1))


def to_batch(block, k):
    return send(block, lambda b, s: (b ^ k, s))


def to_depth(block, k):
    return send(block, lambda b, s: (b, s ^ (2 * k)))


def fuse(body, outs, *args, after=(), limit=16, plain=False, fetch=False, token=False):
    if plain:
        return tuple(body(*args)) + (None,) * token
    after = [x for x in after if x is not None]
    count, held = len(args), len(args) + len(after)
    outs = [*outs, ((SUBS, LANES), FULL)] if token else outs

    def kernel(*refs):
        taken = refs[:count]
        if fetch:
            taken, arrived = refs[held + len(outs) : -1], refs[-1]
            copies = [
                pltpu.make_async_copy(refs[i], taken[i], arrived.at[i]) for i in range(count)
            ]
            for copy in copies:
                copy.start()
            for copy in copies:
                copy.wait()
        results = body(*[ref[...] for ref in taken])
        if token:
            results = [*results, jnp.zeros((SUBS, LANES), FULL)]
        for ref, value in zip(refs[held : held + len(outs)], results, strict=True):
            ref[...] = value


    return pl.pallas_call(
        kernel,
        out_shape=tuple(jax.ShapeDtypeStruct(shape, dtype) for shape, dtype in outs),
        in_specs=[IN_HBM if fetch else IN_VMEM] * count + [IN_VMEM] * len(after),
        out_specs=(IN_VMEM,) * len(outs),
        scratch_shapes=[pltpu.VMEM(x.shape, x.dtype) for x in args]
        + [pltpu.SemaphoreType.DMA((count,))]
        if fetch
        else [],
        compiler_params=pltpu.CompilerParams(vmem_limit_bytes=limit * MIB),
        cost_estimate=pl.CostEstimate(flops=COST, bytes_accessed=COST, transcendentals=0),
    )(*args, *after)


def dot(x, w):
    return lax.dot_general(x, w, (((1,), (0,)), ((), ())), preferred_element_type=FULL)


def dot_back(x, w):
    return lax.dot_general(x, w, (((1,), (1,)), ((), ())), preferred_element_type=FULL)


def dot_rows(x, y):
    return lax.dot_general(x, y, (((0,), (0,)), ((), ())), preferred_element_type=FULL)


def restore(x, order):
    high = x.astype(LOW)
    rest = (x - high.astype(FULL)).astype(LOW)
    return dot_back(high, order) + dot_back(rest, order)


def restore_in(x, order):
    high = x.astype(LOW)
    rest = (x - high.astype(FULL)).astype(LOW)
    return dot(high, order) + dot(rest, order)


def row_index(shape):
    return lax.broadcasted_iota(jnp.int32, shape, 0)


def stack_rows(rows, count=SUBS):
    width = rows[0].shape[1]
    index = row_index((count, width))
    out = jnp.zeros((count, width), FULL)
    for i, row in enumerate(rows):
        out = jnp.where(index == i, row, out)
    return out


def down(x, first, plain):
    rolled = jnp.roll(x, 1, 0) if plain else pltpu.roll(x, 1, 0)
    return jnp.where(row_index(x.shape) == 0, first, rolled)


def up(x, last, plain):
    count = x.shape[0]
    rolled = jnp.roll(x, -1, 0) if plain else pltpu.roll(x, count - 1, 0)
    return jnp.where(row_index(x.shape) == count - 1, last, rolled)


def column_sum(x):
    return jnp.sum(x, axis=0, keepdims=True)


def lane_mean(x):
    return jnp.mean(x, axis=-1, keepdims=True)


def unit_norm(hidden):
    centred = hidden - lane_mean(hidden)
    scale = lax.rsqrt(lane_mean(centred * centred) + EPS)
    return centred * scale, scale


def norm_backward(grad, unit, scale, gain):
    inner = grad * gain
    centred = inner - lane_mean(inner)
    return scale * (centred - unit * lane_mean(inner * unit))


def mixing(normed, prior, coeff):
    return (normed * coeff + prior * (1.0 - coeff)).astype(LOW)


def pick(values, index):
    out = values[0]
    for i in range(1, len(values)):
        out = jnp.where(index == i, values[i], out)
    return out


def log2(n):
    return n.bit_length() - 1


def untile(x, blocks):
    count = x.shape[0] // blocks
    x = x.reshape(count // SUBS, blocks, SUBS, LANES)
    return jnp.concatenate([x[:, i].reshape(count, LANES) for i in range(blocks)], axis=1)


def to_lanes(row):
    return jnp.concatenate(
        [row[:, i * LANES : (i + 1) * LANES] for i in range(row.shape[1] // LANES)], axis=0
    )


def from_lanes(x):
    return jnp.concatenate([x[i : i + 1] for i in range(x.shape[0])], axis=1)


def to_tiles(x):
    count, width = x.shape
    blocks = width // LANES
    x = x.reshape(count // SUBS, SUBS, blocks, LANES).transpose(0, 2, 1, 3)
    return x.reshape(count * blocks, LANES)


def from_tiles(x, width):
    blocks = width // LANES
    count = x.shape[0] // blocks
    x = x.reshape(count // SUBS, blocks, SUBS, LANES).transpose(0, 2, 1, 3)
    return x.reshape(count, width)


def position(i, r, blocks):
    return pl.ds(i * (SUBS * blocks) + r, blocks, stride=SUBS)


def forward_scan(keep_ref, key_ref, value_ref, rates_ref, carry_ref, out_ref):
    blocks = rates_ref.shape[1]
    fade, bonus = rates_ref[0], rates_ref[1]

    def eight(i, state):
        num, den, num_slope, den_slope = state
        for r in range(SUBS):
            at = position(i, r, blocks)
            key, value = key_ref[at, :], value_ref[at, :]
            keep = keep_ref[pl.ds(i * SUBS + r, 1), :]
            num, den, num_slope, den_slope = (
                num * keep,
                den * keep,
                num_slope * keep,
                den_slope * keep,
            )
            reward = jnp.exp(bonus + key)
            weight = jnp.exp(key)
            inverse = 1.0 / (den + reward)
            wkv = (num + reward * value) * inverse
            out_ref[0, at, :] = wkv
            out_ref[1, at, :] = inverse
            out_ref[2, at, :] = (num_slope - wkv * den_slope) * inverse
            num_slope = fade * (num_slope + num)
            den_slope = fade * (den_slope + den)
            num = fade * num + weight * value
            den = fade * den + weight
        return num, den, num_slope, den_slope

    lax.fori_loop(
        0,
        keep_ref.shape[0] // SUBS,
        eight,
        (carry_ref[0], carry_ref[1], carry_ref[2], carry_ref[3]),
    )


def backward_scan(
    keep_ref, key_ref, value_ref, scanned_ref, share_ref, rates_ref, carry_ref, key_out, value_out, first_out
):
    blocks = rates_ref.shape[1]
    fade, bonus = rates_ref[0], rates_ref[1]
    groups = keep_ref.shape[0] // SUBS

    def eight(step, state):
        direct, scaled, first = state
        i = groups - 1 - step
        for r in reversed(range(SUBS)):
            at = position(i, r, blocks)
            key, value = key_ref[at, :], value_ref[at, :]
            wkv, share = scanned_ref[0, at, :], share_ref[at, :]
            keep = keep_ref[pl.ds(i * SUBS + r, 1), :]
            reward = share * jnp.exp(bonus + key)
            weight = jnp.exp(key)
            bonus_part = reward * (value - wkv)
            key_out[at, :] = weight * (direct * value - scaled) + bonus_part
            value_out[at, :] = weight * direct + reward
            first = first + bonus_part
            direct = (share + fade * direct) * keep
            scaled = (share * wkv + fade * scaled) * keep
        return direct, scaled, first

    first_out[...] = lax.fori_loop(
        0, groups, eight, (carry_ref[0], carry_ref[1], jnp.zeros_like(fade))
    )[2]


def run_forward(keep, key, value, rates, carry):
    return pl.pallas_call(
        forward_scan,
        out_shape=jax.ShapeDtypeStruct((3,) + key.shape, FULL),
        in_specs=[IN_VMEM] * 5,
        out_specs=IN_VMEM,
        compiler_params=pltpu.CompilerParams(vmem_limit_bytes=8 * MIB),
        cost_estimate=pl.CostEstimate(
            flops=20 * key.size, bytes_accessed=20 * key.size, transcendentals=3 * key.size
        ),
    )(keep, key, value, rates, carry)


def run_backward(keep, key, value, wkv, share, rates, carry):
    tiles = jax.ShapeDtypeStruct(key.shape, FULL)
    return pl.pallas_call(
        backward_scan,
        out_shape=(tiles, tiles, jax.ShapeDtypeStruct(rates.shape[1:], FULL)),
        in_specs=[IN_VMEM] * 7,
        out_specs=(IN_VMEM,) * 3,
        compiler_params=pltpu.CompilerParams(vmem_limit_bytes=8 * MIB),
        cost_estimate=pl.CostEstimate(
            flops=20 * key.size, bytes_accessed=24 * key.size, transcendentals=2 * key.size
        ),
    )(keep, key, value, wkv, share, rates, carry)


def moved(sums, span, pace):
    fade = jnp.exp(-pace * span)
    if len(sums) == 4:
        num, den, num_slope, den_slope = sums
        return [
            fade * num,
            fade * den,
            fade * (num_slope + span * num),
            fade * (den_slope + span * den),
        ]
    return [fade * x for x in sums]


def split_message(message, count):
    return [message[i : i + 1] for i in range(count)], message[count : count + 1], message[count + 1 : count + 2]


def by_place(message, other):
    core = places()[2]
    return jnp.where(core == 0, message, other), jnp.where(core == 0, other, message)


def chip_sums(count, length, forward):
    def body(message, other, vectors):
        pace = jnp.exp(vectors[9:10])
        first, second = by_place(message, other)
        one, one_last, one_before = split_message(first, count)
        two, two_last, _ = split_message(second, count)
        near, far = (two, one) if forward else (one, two)
        through = (two_last == one_last) if forward else (one_last == one_before)
        far = moved(far, float(length), pace)
        sums = [n + jnp.where(through, f, 0.0) for n, f in zip(near, far, strict=True)]
        return (stack_rows(sums + [two_last, one_before]),)

    return body


def joined_sums(count, length, chips):
    def body(near, far, vectors):
        pace = jnp.exp(vectors[9:10])
        sums, last, before = split_message(near, count)
        more, far_last, far_before = split_message(far, count)
        more = moved(more, 2.0 * length * chips, pace)
        sums = [x + jnp.where(last == before, y, 0.0) for x, y in zip(sums, more, strict=True)]
        ids = [last, far_before] if count == 4 else [far_last, before]
        return (stack_rows(sums + ids),)

    return body


def carried(count, length, forward):
    def body(message, other, vectors, *got):
        core = places()[2]
        pace = jnp.exp(vectors[9:10])
        first, second = by_place(message, other)
        one, one_last, one_before = split_message(first, count)
        two, two_last, _ = split_message(second, count)
        total, last, before = split_message(got[0], count)
        through, chips = last == before, 1
        for i, message in enumerate(got[1:]):
            sums, last, before = split_message(message, count)
            sums = moved(sums, 2.0 * length * chips, pace)
            total = [t + jnp.where(through, x, 0.0) for t, x in zip(total, sums, strict=True)]
            through, chips = through & (last == before), chips + 2 ** (i + 1)
        inner, through = (one, one_last == one_before) if forward else (two, two_last == one_last)
        passed = moved(total, float(length), pace)
        passed = [x + jnp.where(through, y, 0.0) for x, y in zip(inner, passed, strict=True)]
        chosen = core == (1 if forward else 0)
        return (
            jnp.stack(
                [to_lanes(jnp.where(chosen, p, t)) for p, t in zip(passed, total, strict=True)]
            ),
        )

    return body


def carry_chip(values, vectors, length, forward, plain):
    count = 4 if forward else 2
    width = values.shape[1]
    other = to_core(values)
    (chip,) = fuse(
        chip_sums(count, length, forward), [((SUBS, width), FULL)], values, other, vectors, plain=plain
    )
    return other, chip


def carry_steps(chip, vectors, length, forward, plain, after=()):
    cols = lax.axis_size("seq")
    count = 4 if forward else 2
    width = chip.shape[1]

    def route(step):
        def go(b, s):
            target = s + 2 * step * (1 if forward else -1)
            return (b, target) if 0 <= target < cols else None

        return go

    got, sums, step = [], chip, 1
    while step < cols // 2:
        got.append(send(sums, route(step)))
        if 2 * step < cols // 2:
            (sums,) = fuse(
                joined_sums(count, length, step),
                [((SUBS, width), FULL)],
                sums,
                got[-1],
                vectors,
                after=after,
                plain=plain,
            )
        step *= 2
    return got


def carry_end(parts, length, forward, plain, after=()):
    count = 4 if forward else 2
    return fuse(
        carried(count, length, forward),
        [((count, parts[0].shape[1] // LANES, LANES), FULL)],
        *parts,
        after=after,
        plain=plain,
    )[0]


def split_parts(x):
    high = x.astype(LOW)
    return [high, (x - high.astype(FULL)).astype(LOW)]


def add_batch(own, got, count, plain, after=(), vectors=None):
    depth = lax.axis_size("seq") // 2
    height, width = own.shape
    extra = 32 if vectors is not None else 0
    height -= extra
    part = height // (count * depth)
    inputs = [own, *got] + ([vectors] if extra else [])

    def body(own, *got):
        got, sums = (got[:-1], got[-1]) if extra else (got, None)
        got = [x.astype(FULL) for x in got]
        total = sum((x[:height] for x in got), own[:height].astype(FULL))
        blocks = [
            [total[(i * depth + k) * part : (i * depth + k + 1) * part] for i in range(count)]
            for k in range(depth)
        ]
        first, rest = blocks[0], [[x.astype(LOW) for x in block] for block in blocks[1:]]
        if extra:
            sums = sum((x[height : height + 16] + x[height + 16 :] for x in got), sums)
            first, rest = first + [sums], [block + split_parts(sums) for block in rest]
        return [jnp.concatenate(x, axis=0) for x in [first, *rest]]

    return fuse(
        body,
        [((count * part + extra // 2, width), FULL)]
        + [((count * part + extra, width), LOW)] * (depth - 1),
        *inputs,
        after=after,
        plain=plain,
        token=True,
    )


def add_depth(pieces, count, part, outs, last, plain, after=()):
    width = pieces[0].shape[1]
    height = count * part
    got = [to_depth(pieces[k], k) for k in range(1, len(pieces))]

    def body(own, *got):
        got = [x.astype(FULL) for x in got]
        total = sum((x[:height] for x in got), own[:height])
        results = [total[i * part : (i + 1) * part] for i in range(count)]
        if last is not None:
            sums = sum((x[height : height + 16] + x[height + 16 :] for x in got), own[height:])
            results += last(sums)
        return results

    return fuse(
        body, [((part, width), FULL)] * count + outs, pieces[0], *got, after=after, plain=plain
    )


def halve_depth(pieces, plain):
    half = len(pieces) // 2
    height, width = pieces[0].shape
    joined = fuse(
        lambda *x: (jnp.concatenate(x, axis=0),),
        [((half * height, width), LOW)],
        *pieces[half:],
        plain=plain,
    )[0]
    got = to_depth(joined, half)

    def body(own, *rest):
        rest, got = rest[:-1], rest[-1].astype(FULL)
        blocks = [got[i * height : (i + 1) * height] for i in range(half)]
        return [own + blocks[0]] + [
            (x.astype(FULL) + y).astype(LOW) for x, y in zip(rest, blocks[1:], strict=True)
        ]

    return fuse(
        body,
        [((height, width), FULL)] + [((height, width), LOW)] * (half - 1),
        *pieces[:half],
        got,
        plain=plain,
        token=True,
    )


def per_device(
    layer_input,
    segment_ids,
    out_cotangent,
    key_weight,
    value_weight,
    recept_weight,
    output_weight,
    channel_key,
    channel_value,
    channel_recept,
    norm_gains,
    norm_offsets,
    mix_coeffs,
    time_decay,
    time_first,
):
    rows, cols = sizes()
    depth = cols // 2
    length, width = layer_input.shape[1:]
    own = key_weight.shape[0]
    hidden_width = channel_key.shape[1]
    part_width = hidden_width // rows
    half = width // 2
    plain = own % 16 != 0
    low_act, full_act = ((length, width), LOW), ((length, width), FULL)
    narrow = ((length, LANES), FULL)
    square = ((width, width), LOW)
    edge_row = ((SUBS, width), FULL)
    raw, cotangent = layer_input[0], out_cotangent[0]
    mac = 2 * length * width * width

    small = [norm_gains, norm_offsets, mix_coeffs, time_decay[None], time_first[None]]
    n_vectors = sum(x.shape[0] for x in small)

    def prepare(key, value, recept, output, gate, cross, raw, ids, *small):
        b, z, core = places()
        device = b * cols + z * 2 + core
        lane = lax.broadcasted_iota(jnp.int32, (own, width), 1)
        home = (lane == device * own + row_index((own, width))).astype(FULL).astype(LOW)
        placed = jnp.zeros((16, width), FULL)
        at = 0
        for x in small:
            x = dot(x, home)
            for i in range(x.shape[0]):
                placed = jnp.where(row_index(placed.shape) == at, x[i : i + 1], placed)
                at += 1
        blocks = [cross[:, j * part_width : (j + 1) * part_width] for j in range(rows)]
        ids = ids.astype(FULL)
        last = raw[length - 16 :].astype(FULL)[15:16]
        edge = stack_rows([last, jnp.broadcast_to(ids[:, length - 1 :], (1, width))], 16)
        return (
            [
                jnp.concatenate([key, value, placed.astype(LOW)], axis=0),
                jnp.concatenate([recept, output, gate], axis=0),
                edge,
                jnp.broadcast_to(ids, (LANES, length)).T,
            ]
            + [pick(blocks, b ^ k) for k in range(rows)]
        )

    first_pack, second_pack, edge, ids_lanes, *crossing = fuse(
        prepare,
        [((2 * own + 16, width), LOW), ((3 * own, width), LOW), ((16, width), FULL), narrow]
        + [((own, part_width), LOW)] * rows,
        key_weight,
        value_weight,
        recept_weight,
        output_weight,
        channel_recept,
        channel_key,
        raw,
        segment_ids,
        *small,
        plain=plain,
        fetch=True,
        limit=58,
    )
    deep_got = [to_depth(first_pack, k) for k in range(1, depth)]
    cross_got = [to_batch(crossing[k], k) for k in range(1, rows)]
    edge = send_next(edge)

    def begin(raw, edge, ids):
        b, z, core = places()
        place = lax.broadcasted_iota(jnp.int32, (1, width), 1)
        block, row = place >> log2(own), place & (own - 1)
        k_core = block >> log2(rows * depth)
        k_batch = (block >> log2(depth)) & (rows - 1)
        k_depth = block & (depth - 1)
        target = ((k_batch ^ b) << log2(cols)) + ((k_depth ^ z) << 1) + (k_core ^ core)
        feature = (target << log2(own)) + row
        order = jnp.concatenate(
            [
                (row_index((LANES, width)) + i * LANES == feature).astype(FULL).astype(LOW)
                for i in range(width // LANES)
            ],
            axis=0,
        )
        unit, scale = unit_norm(dot(raw, order))
        edge_unit = unit_norm(dot(edge.astype(LOW), order))[0]
        before = jnp.where((z == 0) & (core == 0), -1.0, edge[1:2])
        before_lanes = before[:, :LANES]
        last = ids[length - 1 : length]
        keep = (ids == down(ids, before_lanes, plain)).astype(FULL)
        opened = (ids == before_lanes).astype(FULL)
        closing = (ids == last).astype(FULL)
        last = jnp.broadcast_to(last[:, :1], (1, width))
        scale = jnp.broadcast_to(scale, (length, LANES))
        return (
            order,
            unit,
            keep,
            jnp.concatenate([keep, opened, closing, scale], axis=1),
            stack_rows([edge_unit[0:1], last, before]),
        )

    order, unit_one, keep, statics, edges = fuse(
        begin,
        [square, full_act, narrow, ((length, 4 * LANES), FULL), edge_row],
        raw,
        edge,
        ids_lanes,
        plain=plain,
    )

    def deepen_first(second, *x):
        vectors = sum(y[2 * own :].astype(FULL) for y in x).astype(LOW)
        parts = [y[i * own : (i + 1) * own] for i in range(2) for y in x]
        return jnp.concatenate(parts + [vectors], axis=0), second

    first_deep, second_pack = fuse(
        deepen_first,
        [((2 * depth * own + 16, width), LOW), (second_pack.shape, LOW)],
        second_pack,
        first_pack,
        *deep_got,
        after=(order, *cross_got),
        plain=plain,
    )
    first_wide = [to_batch(first_deep, k) for k in range(1, rows)]
    first_pieces = [first_deep] + first_wide
    first_pieces = first_pieces + [to_core(piece) for piece in first_pieces]
    second_got = [to_depth(second_pack, k) for k in range(1, depth)]

    cross_rows = rows * own * part_width // width
    packed_rows = cross_rows + channel_value.shape[0]

    def deepen(value, *x):
        b = places()[0]
        cross, x = x[:rows], x[rows:]
        cross = jnp.concatenate([pick(cross, j ^ b) for j in range(rows)], axis=0)
        return (
            jnp.stack([y[: 2 * own] for y in x]),
            jnp.stack([y[2 * own :] for y in x]),
            jnp.concatenate([cross.reshape(cross_rows, width), value], axis=0),
        )

    second_deep, third_deep, channel_pack = fuse(
        deepen,
        [
            ((depth, 2 * own, width), LOW),
            ((depth, own, width), LOW),
            ((packed_rows, width), LOW),
        ],
        channel_value,
        crossing[0],
        *cross_got,
        second_pack,
        *second_got,
        after=first_wide,
        plain=plain,
    )
    channel_pack = lax.all_gather(channel_pack, "seq", axis=0, tiled=True)

    def unpack_channel(x):
        x = x.reshape(cols, packed_rows, width)
        key = x[:, :cross_rows].reshape(cols, rows, own, part_width)
        key = jnp.concatenate(
            [key[j, i] for i in range(rows) for j in range(cols)], axis=0
        )
        return key, x[:, cross_rows:].reshape(part_width, width)

    part_key, part_value = fuse(
        unpack_channel,
        [((width, part_width), LOW), ((part_width, width), LOW)],
        channel_pack,
        plain=plain,
    )

    second_wide = [to_batch(second_deep, k) for k in range(1, rows)]
    (third_deep,) = fuse(
        lambda x: (x,), [(third_deep.shape, LOW)], third_deep, after=second_wide, plain=plain
    )
    third_wide = [to_batch(third_deep, k) for k in range(1, rows)]

    def joined(deep, wide, after):
        (mine,) = fuse(
            lambda *x: (jnp.concatenate(x, axis=0),),
            [((rows * depth,) + deep.shape[1:], LOW)],
            deep,
            *wide,
            after=after,
            plain=plain,
        )
        return mine, to_core(mine)


    def gathered(pieces, start):
        return jnp.concatenate(
            [piece[:, start : start + own].reshape(-1, width) for piece in pieces], axis=0
        )

    def front(unit, statics, edges, order, *pieces):
        height = depth * own
        vectors = sum(piece[2 * height :].astype(FULL) for piece in pieces)
        lines = dot(vectors.astype(LOW), order)
        normed = unit * lines[0:1] + lines[2:3]
        edge_normed = edges[0:1] * lines[0:1] + lines[2:3]
        prior = down(normed, edge_normed, plain) * statics[:, :1]
        mix_key = mixing(normed, prior, lines[4:5])
        mix_value = mixing(normed, prior, lines[5:6])
        mix_recept = mixing(normed, prior, lines[6:7])
        key_all = jnp.concatenate([piece[:height] for piece in pieces], axis=0)
        value_all = jnp.concatenate([piece[height : 2 * height] for piece in pieces], axis=0)
        key, value = dot(mix_key, key_all), dot(mix_value, value_all)
        pace = jnp.exp(vectors[9:10])
        left = length - 1.0 - row_index((length, width)).astype(FULL)
        den = jnp.where(statics[:, 2 * LANES : 2 * LANES + 1] > 0.5, jnp.exp(key - pace * left), 0.0)
        num = den * value
        message = stack_rows(
            [column_sum(num), column_sum(den), column_sum(num * left), column_sum(den * left)]
            + [edges[1:2], edges[2:3]]
        )
        return (
            jnp.concatenate([vectors, lines], axis=0),
            normed - prior,
            jnp.stack([mix_key, mix_value, mix_recept]),
            jnp.stack([key_all, value_all]),
            key,
            value,
            message,
            jnp.stack([to_lanes(jnp.exp(-pace)), to_lanes(vectors[10:11])]),
        )

    (
        vectors,
        difference_one,
        mixes,
        first_all,
        key_act,
        value_act,
        message,
        rates,
    ) = fuse(
        front,
        [
            ((32, width), FULL),
            full_act,
            ((3, length, width), LOW),
            ((2, width, width), LOW),
            full_act,
            full_act,
            edge_row,
            ((2, width // LANES, LANES), FULL),
        ],
        unit_one,
        statics,
        edges,
        order,
        *first_pieces,
        plain=plain,
        limit=32,
    )
    other, chip = carry_chip(message, vectors, length, True, plain)
    got = carry_steps(chip, vectors, length, True, plain)
    carry = carry_end([message, other, vectors] + got, length, True, plain)

    def receptance(mixes, *pieces):
        recept_all = gathered(pieces, 0)
        return jax.nn.sigmoid(dot(mixes[2], recept_all)), recept_all, gathered(pieces, own)

    recept_act, recept_all, output_all = fuse(
        receptance,
        [full_act, square, square],
        mixes,
        *joined(second_deep, second_wide, (carry,)),
        plain=plain,
        limit=32,
    )
    key_tiles, value_tiles = to_tiles(key_act), to_tiles(value_act)
    scanned = run_forward(keep, key_tiles, value_tiles, rates, carry)

    def attend(scanned, recept, order, output_all, raw, vectors):
        gated = dot((recept * untile(scanned[0], width // LANES)).astype(LOW), order).astype(LOW)
        middle = raw.astype(FULL) + dot(gated, output_all)
        unit, scale = unit_norm(middle)
        normed = unit * vectors[1:2] + vectors[3:4]
        return (
            gated,
            middle,
            jnp.concatenate([unit, jnp.broadcast_to(scale, (length, LANES))], axis=1),
            stack_rows([normed[length - 1 :]]),
        )

    gated, middle, unit_two, edge_two = fuse(
        attend,
        [low_act, full_act, ((length, width + LANES), FULL), edge_row],
        scanned,
        recept_act,
        order,
        output_all,
        raw,
        vectors,
        plain=plain,
    )
    edge_two = send_next(edge_two)

    def mix_two(unit, edge, statics, vectors):
        normed = unit[:, :width] * vectors[1:2] + vectors[3:4]
        prior = down(normed, edge[0:1], plain) * statics[:, :1]
        return (
            mixing(normed, prior, vectors[7:8]),
            mixing(normed, prior, vectors[8:9]),
            normed - prior,
        )

    mix_hidden, mix_gate, difference_two, mixed_token = fuse(
        mix_two, [low_act, low_act, full_act], unit_two, edge_two, statics, vectors, plain=plain, token=True
    )
    shared = [mix_hidden] + [to_batch(mix_hidden, k) for k in range(1, rows)]

    def channel(x, key, value):
        positive = jnp.maximum(dot(x, key), 0.0)
        squared = (positive * positive).astype(LOW)
        return squared, dot(squared, value)

    def channel_low(x, key, value):
        squared, out = channel(x, key, value)
        return squared, out.astype(LOW)

    hidden_act = ((length, part_width), LOW)
    squares, returned = [], []
    for k in range(rows):
        squared, out = fuse(
            channel_low if k else channel,
            [hidden_act, low_act if k else full_act],
            shared[k],
            part_key,
            part_value,
            plain=plain,
        )
        squares.append(squared)
        returned.append(to_batch(out, k) if k else out)

    def gating(mix, order, gated, mixes, *pieces):
        gate_all = gathered(pieces, 0)
        mix = dot(mix, order).astype(LOW)
        sides = jnp.stack([mixes[0], mixes[1], mixes[2], gated, mix])
        return jax.nn.sigmoid(dot(mix, gate_all)), sides, gate_all

    gate, sides, gate_all = fuse(
        gating,
        [full_act, ((5, length, width), LOW), square],
        mix_gate,
        order,
        gated,
        mixes,
        *joined(third_deep, third_wide, (mixed_token,)),
        plain=plain,
    )

    def finish(own_part, gate, middle, grad_out, *got):
        out = sum((x.astype(FULL) for x in got), own_part)
        grad_out = grad_out.astype(FULL)
        return (
            (middle + gate * out).astype(LOW),
            (grad_out * gate).astype(LOW),
            (grad_out * out * gate * (1.0 - gate)).astype(LOW),
        )

    block_output, grad_values, grad_gate = fuse(
        finish,
        [low_act, low_act, low_act],
        returned[0],
        gate,
        middle,
        cotangent,
        *returned[1:],
        plain=plain,
    )

    shared_grad = [grad_values] + [to_batch(grad_values, k) for k in range(1, rows)]

    def channel_back(grad, squared, key, value):
        positive = jnp.sqrt(squared.astype(FULL))
        hidden = (dot_back(grad, value) * 2.0 * positive).astype(LOW)
        return hidden, dot_back(hidden, key)

    def channel_back_low(grad, squared, key, value):
        hidden, out = channel_back(grad, squared, key, value)
        return hidden, out.astype(LOW)

    def channel_back_own(grad, squared, key, value, grad_gate, gate_all, order):
        hidden, out = channel_back(grad, squared, key, value)
        return hidden, out, restore(dot_back(grad_gate, gate_all), order)

    hidden, out, grad_mix_gate = fuse(
        channel_back_own,
        [hidden_act, full_act, full_act],
        shared_grad[0],
        squares[0],
        part_key,
        part_value,
        grad_gate,
        gate_all,
        order,
        plain=plain,
    )
    hiddens, returned = [hidden], [out]
    for k in range(1, rows):
        hidden, out = fuse(
            channel_back_low,
            [hidden_act, low_act],
            shared_grad[k],
            squares[k],
            part_key,
            part_value,
            plain=plain,
        )
        hiddens.append(hidden)
        returned.append(to_batch(out, k))

    def paired(active, active_got, grad, grad_got):
        return dot_rows(
            jnp.concatenate([active[:, :half], active_got[:, half:]], axis=0),
            jnp.concatenate([grad, grad_got], axis=0),
        ).astype(LOW)

    def cut(terms, *more):
        part = half // rows
        return [
            jnp.concatenate([term[k * part : (k + 1) * part] for term in terms] + list(more), axis=0)
            for k in range(rows)
        ]

    def early_terms(sides, sides_got, grads, grads_got):
        return cut(
            [
                paired(sides[side], sides_got[side], grads[i], grads_got[i])
                for i, side in enumerate((3, 2, 4))
            ]
        )

    sides_got = to_core(sides)

    def unmix_two(own_part, grad_gate, difference, statics, vectors, *got):
        grad_hidden = sum((x.astype(FULL) for x in got), own_part)
        mix_h, mix_g = vectors[7:8], vectors[8:9]
        passed = (grad_hidden * (1.0 - mix_h) + grad_gate * (1.0 - mix_g)) * statics[:, :1]
        return (
            grad_hidden * mix_h + grad_gate * mix_g,
            passed,
            stack_rows([passed[0:1]]),
            stack_rows([column_sum(grad_hidden * difference), column_sum(grad_gate * difference)]),
        )

    own_two, passed_two, after_two, mix_sums_two = fuse(
        unmix_two,
        [full_act, full_act, edge_row, edge_row],
        returned[0],
        grad_mix_gate,
        difference_two,
        statics,
        vectors,
        *returned[1:],
        plain=plain,
    )
    after_two = send_back(after_two)

    def middle_back(
        own_part, passed, after, unit, grad_out, vectors, mix_sums, recept, scanned,
        output_all, order, statics, edges, grad_gate,
    ):
        wkv, inverse, slope = (untile(scanned[i], width // LANES) for i in range(3))
        unit, scale = unit[:, :width], unit[:, width : width + 1]
        grad_normed = own_part + up(passed, after[0:1], plain)
        part = norm_backward(grad_normed, unit, scale, vectors[1:2])
        grad_middle = grad_out.astype(FULL) + part
        grad_low = grad_middle.astype(LOW)
        grad_gated = restore(dot_back(grad_low, output_all), order)
        grad_wkv = grad_gated * recept
        grad_recept = (grad_wkv * wkv * (1.0 - recept)).astype(LOW)
        share = grad_wkv * inverse
        pace = jnp.exp(vectors[9:10])
        step = row_index((length, width)).astype(FULL)
        head = jnp.where(statics[:, LANES : LANES + 1] > 0.5, share * jnp.exp(-pace * step), 0.0)
        return (
            grad_middle,
            jnp.stack([grad_low, grad_recept, grad_gate]),
            share,
            stack_rows([column_sum(head), column_sum(head * wkv), edges[1:2], edges[2:3]]),
            stack_rows(
                [
                    column_sum(grad_normed * unit),
                    column_sum(grad_normed),
                    mix_sums[0:1],
                    mix_sums[1:2],
                    -pace * column_sum(grad_wkv * slope),
                ]
            ),
        )

    grad_middle, grad_three, share, message, sums_two = fuse(
        middle_back,
        [full_act, ((3, length, width), LOW), full_act, edge_row, edge_row],
        own_two,
        passed_two,
        after_two,
        unit_two,
        cotangent,
        vectors,
        mix_sums_two,
        recept_act,
        scanned,
        output_all,
        order,
        statics,
        edges,
        grad_gate,
        plain=plain,
        limit=24,
    )

    other, chip_back = carry_chip(message, vectors, length, False, plain)

    *early, early_token = fuse(
        early_terms,
        [((3 * half // rows, width), LOW)] * rows,
        sides,
        sides_got,
        grad_three,
        to_core(grad_three),
        after=(chip_back,),
        plain=plain,
        token=True,
    )
    carry_parts = [message, other, vectors] + carry_steps(
        chip_back, vectors, length, False, plain, (early_token,)
    )
    early_got = [to_batch(early[k], k) for k in range(1, rows)]
    def channel_terms(*x):
        shared, hiddens, squares, grads = (
            jnp.concatenate(x[i * rows : (i + 1) * rows], axis=0) for i in range(4)
        )
        key = dot_rows(shared, hiddens).astype(LOW)
        value = dot_rows(squares, grads).astype(LOW)
        key = key.reshape(rows, cols, own, part_width)
        value_rows = part_width // cols
        parts = []
        for j in range(cols):
            block = jnp.concatenate([key[i, j] for i in range(rows)], axis=0)
            parts += [
                block.reshape(cross_rows, width),
                value[j * value_rows : (j + 1) * value_rows],
            ]
        return (jnp.concatenate(parts, axis=0),)

    channel_term, channel_token = fuse(
        channel_terms,
        [((cols * packed_rows, width), LOW)],
        *shared,
        *hiddens,
        *squares,
        *shared_grad,
        after=(early_token,),
        plain=plain,
        token=True,
        limit=12,
    )
    channel_sum = lax.psum_scatter(channel_term, "seq", scatter_dimension=0, tiled=True)
    carry_back = carry_end(carry_parts, length, False, plain, (channel_token, early_token))
    grad_key, grad_value, first_term = run_backward(
        keep, key_tiles, value_tiles, scanned, to_tiles(share), rates, carry_back
    )

    def lower(key, value):
        return (jnp.stack([key.astype(LOW), value.astype(LOW)]),)

    (grad_late,) = fuse(
        lower,
        [((2, length, width), LOW)],
        *lax.optimization_barrier((from_tiles(grad_key, width), from_tiles(grad_value, width))),
        plain=plain,
    )

    def unmix_one(grads, grad_three, first_all, recept_all, vectors, statics, difference, order):
        lines = vectors[16:]
        grad_key = dot_back(grads[0], first_all[0])
        grad_value = dot_back(grads[1], first_all[1])
        grad_recept = dot_back(grad_three[1], recept_all)
        m_key, m_value, m_recept = lines[4:5], lines[5:6], lines[6:7]
        passed = (
            grad_key * (1.0 - m_key) + grad_value * (1.0 - m_value) + grad_recept * (1.0 - m_recept)
        ) * statics[:, :1]
        return (
            grad_key * m_key + grad_value * m_value + grad_recept * m_recept,
            passed,
            restore(passed[:16], order)[:SUBS],
            stack_rows([column_sum(x * difference) for x in (grad_key, grad_value, grad_recept)]),
        )

    own_one, passed_one, after_one, mix_sums_one = fuse(
        unmix_one,
        [full_act, full_act, edge_row, edge_row],
        grad_late,
        grad_three,
        first_all,
        recept_all,
        vectors,
        statics,
        difference_one,
        order,
        plain=plain,
        limit=24,
    )
    after_one = send_back(after_one)

    def input_back(
        own_part, passed, after, unit, statics, vectors, order, grad_middle, mix_sums, sums_two, first
    ):
        lines, scale = vectors[16:], statics[:, 3 * LANES : 3 * LANES + 1]
        after = jnp.where(row_index((16, width)) == 0, after[0:1], 0.0)
        grad_normed = own_part + up(passed, restore_in(after, order)[0:1], plain)
        part = norm_backward(grad_normed, unit, scale, lines[0:1])
        ordered = stack_rows(
            [
                column_sum(grad_normed * unit),
                column_sum(grad_normed),
                mix_sums[0:1],
                mix_sums[1:2],
                mix_sums[2:3],
            ],
            16,
        )
        ordered = restore(ordered, order)
        total = [ordered[0:1], sums_two[0:1], ordered[1:2], sums_two[1:2]]
        total += [ordered[2:3], ordered[3:4], ordered[4:5], sums_two[2:3], sums_two[3:4]]
        total += [sums_two[4:5], from_lanes(first)]
        return grad_middle + restore(part, order), stack_rows(total, 16)

    input_grad, sums = fuse(
        input_back,
        [full_act, ((16, width), FULL)],
        own_one,
        passed_one,
        after_one,
        unit_one,
        statics,
        vectors,
        order,
        grad_middle,
        mix_sums_one,
        sums_two,
        first_term,
        plain=plain,
        limit=24,
    )
    sums = sums + to_core(sums)
    *early_pieces, early_wide_token = add_batch(early[0], early_got, 3, plain, (sums,))
    early_half = None
    if depth == 4:
        *early_pieces, early_half = halve_depth(early_pieces, plain)

    def late_terms(sides, sides_got, grads, grads_got, sums):
        terms = [paired(sides[i], sides_got[i], grads[i], grads_got[i]) for i in range(2)]
        return cut(terms, *split_parts(sums))

    late = fuse(
        late_terms,
        [((2 * half // rows + 32, width), LOW)] * rows,
        sides,
        sides_got,
        grad_late,
        to_core(grad_late),
        sums,
        after=(early_wide_token,),
        plain=plain,
    )
    late_got = [to_batch(late[k], k) for k in range(1, rows)]
    def own_columns(total):
        b, z, core = places()
        device = b * cols + z * 2 + core
        if plain:
            total = lax.dynamic_slice(total, (0, device * own), (16, own))
        else:
            total = pltpu.roll(total, (width - device * own) & (width - 1), 1)[:, :own]
        return [total[0:2], total[2:4], total[4:9], total[9:10], total[10:11]]

    *late_pieces, _ = add_batch(late[0], late_got, 2, plain, (early_half,), vectors=sums)
    output_grad, recept_grad, gate_grad = add_depth(early_pieces, 3, own, [], None, plain)
    key_grad, value_grad, gains_grad, offsets_grad, mixes_grad, decay_grad, first_grad = add_depth(
        late_pieces,
        2,
        own,
        [((2, own), FULL), ((2, own), FULL), ((5, own), FULL), ((1, own), FULL), ((1, own), FULL)],
        own_columns,
        plain,
    )

    crossed = channel_sum[:cross_rows].reshape(rows, own, part_width)
    crossed = lax.all_to_all(crossed, "batch", 0, 0)

    def assemble(x, crossed):
        return (
            jnp.concatenate([crossed[j].astype(FULL) for j in range(rows)], axis=1),
            x[cross_rows:].astype(FULL),
        )

    channel_key_grad, channel_value_grad = fuse(
        assemble,
        [((own, hidden_width), FULL), (channel_value.shape, FULL)],
        channel_sum,
        crossed,
        plain=plain,
    )
    return (
        block_output[None],
        input_grad[None],
        key_grad,
        value_grad,
        recept_grad,
        output_grad,
        channel_key_grad,
        channel_value_grad,
        gate_grad,
        gains_grad,
        offsets_grad,
        mixes_grad,
        decay_grad[0],
        first_grad[0],
    )


def solution(mesh):
    tokens = P("batch", "seq", None)
    weight = P(BOTH, None)
    lines = P(None, BOTH)
    return jax.shard_map(
        per_device,
        mesh=mesh,
        in_specs=(tokens, P("batch", "seq"), tokens)
        + (weight,) * 7
        + (lines,) * 3
        + (P(BOTH),) * 2,
        out_specs=(tokens, tokens) + (weight,) * 7 + (lines,) * 3 + (P(BOTH),) * 2,
        check_vma=False,
    )
```

```python
import jax
import jax.numpy as jnp
from jax import lax
from jax.experimental import pallas as pl
from jax.experimental.pallas import tpu as pltpu
from jax.sharding import PartitionSpec as P

EPS = 1e-05
BOTH = ("batch", "seq")
LOW = jnp.bfloat16
FULL = jnp.float32
LANES = 128
SUBS = 8
MIB = 1024 * 1024
COST = 2000000
IN_VMEM = pl.BlockSpec(memory_space=pltpu.VMEM)
IN_HBM = pl.BlockSpec(memory_space=pltpu.HBM)


def sizes():
    return lax.axis_size("batch"), lax.axis_size("seq")


def places():
    s = lax.axis_index("seq")
    return lax.axis_index("batch"), s >> 1, s & 1


def send(block, route):
    rows, cols = sizes()
    pairs = []
    for b in range(rows):
        for s in range(cols):
            target = route(b, s)
            if target is not None:
                pairs.append((b * cols + s, target[0] * cols + target[1]))
    return lax.ppermute(block, BOTH, pairs)


def send_next(block):
    cols = lax.axis_size("seq")
    return send(block, lambda b, s: (b, s + 1) if s + 1 < cols else None)


def send_back(block):
    return send(block, lambda b, s: (b, s - 1) if s > 0 else None)


def to_core(block):
    return send(block, lambda b, s: (b, s ^ 1))


def to_batch(block, k):
    return send(block, lambda b, s: (b ^ k, s))


def to_depth(block, k):
    return send(block, lambda b, s: (b, s ^ (2 * k)))


def fuse(body, outs, *args, after=(), limit=16, plain=False, fetch=False, token=False):
    if plain:
        return tuple(body(*args)) + (None,) * token
    after = [x for x in after if x is not None]
    count, held = len(args), len(args) + len(after)
    outs = [*outs, ((SUBS, LANES), FULL)] if token else outs

    def kernel(*refs):
        taken = refs[:count]
        if fetch:
            taken, arrived = refs[held + len(outs) : -1], refs[-1]
            copies = [
                pltpu.make_async_copy(refs[i], taken[i], arrived.at[i]) for i in range(count)
            ]
            for copy in copies:
                copy.start()
            for copy in copies:
                copy.wait()
        results = body(*[ref[...] for ref in taken])
        if token:
            results = [*results, jnp.zeros((SUBS, LANES), FULL)]
        for ref, value in zip(refs[held : held + len(outs)], results, strict=True):
            ref[...] = value


    return pl.pallas_call(
        kernel,
        out_shape=tuple(jax.ShapeDtypeStruct(shape, dtype) for shape, dtype in outs),
        in_specs=[IN_HBM if fetch else IN_VMEM] * count + [IN_VMEM] * len(after),
        out_specs=(IN_VMEM,) * len(outs),
        scratch_shapes=[pltpu.VMEM(x.shape, x.dtype) for x in args]
        + [pltpu.SemaphoreType.DMA((count,))]
        if fetch
        else [],
        compiler_params=pltpu.CompilerParams(vmem_limit_bytes=limit * MIB),
        cost_estimate=pl.CostEstimate(flops=COST, bytes_accessed=COST, transcendentals=0),
    )(*args, *after)


def dot(x, w):
    return lax.dot_general(x, w, (((1,), (0,)), ((), ())), preferred_element_type=FULL)


def dot_back(x, w):
    return lax.dot_general(x, w, (((1,), (1,)), ((), ())), preferred_element_type=FULL)


def dot_rows(x, y):
    return lax.dot_general(x, y, (((0,), (0,)), ((), ())), preferred_element_type=FULL)


def restore(x, order):
    high = x.astype(LOW)
    rest = (x - high.astype(FULL)).astype(LOW)
    return dot_back(high, order) + dot_back(rest, order)


def restore_in(x, order):
    high = x.astype(LOW)
    rest = (x - high.astype(FULL)).astype(LOW)
    return dot(high, order) + dot(rest, order)


def row_index(shape):
    return lax.broadcasted_iota(jnp.int32, shape, 0)


def stack_rows(rows, count=SUBS):
    width = rows[0].shape[1]
    index = row_index((count, width))
    out = jnp.zeros((count, width), FULL)
    for i, row in enumerate(rows):
        out = jnp.where(index == i, row, out)
    return out


def down(x, first, plain):
    rolled = jnp.roll(x, 1, 0) if plain else pltpu.roll(x, 1, 0)
    return jnp.where(row_index(x.shape) == 0, first, rolled)


def up(x, last, plain):
    count = x.shape[0]
    rolled = jnp.roll(x, -1, 0) if plain else pltpu.roll(x, count - 1, 0)
    return jnp.where(row_index(x.shape) == count - 1, last, rolled)


def column_sum(x):
    return jnp.sum(x, axis=0, keepdims=True)


def lane_mean(x):
    return jnp.mean(x, axis=-1, keepdims=True)


def unit_norm(hidden):
    centred = hidden - lane_mean(hidden)
    scale = lax.rsqrt(lane_mean(centred * centred) + EPS)
    return centred * scale, scale


def norm_backward(grad, unit, scale, gain):
    inner = grad * gain
    centred = inner - lane_mean(inner)
    return scale * (centred - unit * lane_mean(inner * unit))


def mixing(normed, prior, coeff):
    return (normed * coeff + prior * (1.0 - coeff)).astype(LOW)


def pick(values, index):
    out = values[0]
    for i in range(1, len(values)):
        out = jnp.where(index == i, values[i], out)
    return out


def log2(n):
    return n.bit_length() - 1


def untile(x, blocks):
    count = x.shape[0] // blocks
    x = x.reshape(count // SUBS, blocks, SUBS, LANES)
    return jnp.concatenate([x[:, i].reshape(count, LANES) for i in range(blocks)], axis=1)


def to_lanes(row):
    return jnp.concatenate(
        [row[:, i * LANES : (i + 1) * LANES] for i in range(row.shape[1] // LANES)], axis=0
    )


def from_lanes(x):
    return jnp.concatenate([x[i : i + 1] for i in range(x.shape[0])], axis=1)


def to_tiles(x):
    count, width = x.shape
    blocks = width // LANES
    x = x.reshape(count // SUBS, SUBS, blocks, LANES).transpose(0, 2, 1, 3)
    return x.reshape(count * blocks, LANES)


def from_tiles(x, width):
    blocks = width // LANES
    count = x.shape[0] // blocks
    x = x.reshape(count // SUBS, blocks, SUBS, LANES).transpose(0, 2, 1, 3)
    return x.reshape(count, width)


def position(i, r, blocks):
    return pl.ds(i * (SUBS * blocks) + r, blocks, stride=SUBS)


def forward_scan(keep_ref, key_ref, value_ref, rates_ref, carry_ref, out_ref):
    blocks = rates_ref.shape[1]
    fade, bonus = rates_ref[0], rates_ref[1]

    def eight(i, state):
        num, den, num_slope, den_slope = state
        for r in range(SUBS):
            at = position(i, r, blocks)
            key, value = key_ref[at, :], value_ref[at, :]
            keep = keep_ref[pl.ds(i * SUBS + r, 1), :]
            num, den, num_slope, den_slope = (
                num * keep,
                den * keep,
                num_slope * keep,
                den_slope * keep,
            )
            reward = jnp.exp(bonus + key)
            weight = jnp.exp(key)
            inverse = 1.0 / (den + reward)
            wkv = (num + reward * value) * inverse
            out_ref[0, at, :] = wkv
            out_ref[1, at, :] = inverse
            out_ref[2, at, :] = (num_slope - wkv * den_slope) * inverse
            num_slope = fade * (num_slope + num)
            den_slope = fade * (den_slope + den)
            num = fade * num + weight * value
            den = fade * den + weight
        return num, den, num_slope, den_slope

    lax.fori_loop(
        0,
        keep_ref.shape[0] // SUBS,
        eight,
        (carry_ref[0], carry_ref[1], carry_ref[2], carry_ref[3]),
    )


def backward_scan(
    keep_ref, key_ref, value_ref, scanned_ref, share_ref, rates_ref, carry_ref, key_out, value_out, first_out
):
    blocks = rates_ref.shape[1]
    fade, bonus = rates_ref[0], rates_ref[1]
    groups = keep_ref.shape[0] // SUBS

    def eight(step, state):
        direct, scaled, first = state
        i = groups - 1 - step
        for r in reversed(range(SUBS)):
            at = position(i, r, blocks)
            key, value = key_ref[at, :], value_ref[at, :]
            wkv, share = scanned_ref[0, at, :], share_ref[at, :]
            keep = keep_ref[pl.ds(i * SUBS + r, 1), :]
            reward = share * jnp.exp(bonus + key)
            weight = jnp.exp(key)
            bonus_part = reward * (value - wkv)
            key_out[at, :] = weight * (direct * value - scaled) + bonus_part
            value_out[at, :] = weight * direct + reward
            first = first + bonus_part
            direct = (share + fade * direct) * keep
            scaled = (share * wkv + fade * scaled) * keep
        return direct, scaled, first

    first_out[...] = lax.fori_loop(
        0, groups, eight, (carry_ref[0], carry_ref[1], jnp.zeros_like(fade))
    )[2]


def run_forward(keep, key, value, rates, carry):
    return pl.pallas_call(
        forward_scan,
        out_shape=jax.ShapeDtypeStruct((3,) + key.shape, FULL),
        in_specs=[IN_VMEM] * 5,
        out_specs=IN_VMEM,
        compiler_params=pltpu.CompilerParams(vmem_limit_bytes=8 * MIB),
        cost_estimate=pl.CostEstimate(
            flops=20 * key.size, bytes_accessed=20 * key.size, transcendentals=3 * key.size
        ),
    )(keep, key, value, rates, carry)


def run_backward(keep, key, value, wkv, share, rates, carry):
    tiles = jax.ShapeDtypeStruct(key.shape, FULL)
    return pl.pallas_call(
        backward_scan,
        out_shape=(tiles, tiles, jax.ShapeDtypeStruct(rates.shape[1:], FULL)),
        in_specs=[IN_VMEM] * 7,
        out_specs=(IN_VMEM,) * 3,
        compiler_params=pltpu.CompilerParams(vmem_limit_bytes=8 * MIB),
        cost_estimate=pl.CostEstimate(
            flops=20 * key.size, bytes_accessed=24 * key.size, transcendentals=2 * key.size
        ),
    )(keep, key, value, wkv, share, rates, carry)


def moved(sums, span, pace):
    fade = jnp.exp(-pace * span)
    if len(sums) == 4:
        num, den, num_slope, den_slope = sums
        return [
            fade * num,
            fade * den,
            fade * (num_slope + span * num),
            fade * (den_slope + span * den),
        ]
    return [fade * x for x in sums]


def split_message(message, count):
    return [message[i : i + 1] for i in range(count)], message[count : count + 1], message[count + 1 : count + 2]


def by_place(message, other):
    core = places()[2]
    return jnp.where(core == 0, message, other), jnp.where(core == 0, other, message)


def chip_sums(count, length, forward):
    def body(message, other, vectors):
        pace = jnp.exp(vectors[9:10])
        first, second = by_place(message, other)
        one, one_last, one_before = split_message(first, count)
        two, two_last, _ = split_message(second, count)
        near, far = (two, one) if forward else (one, two)
        through = (two_last == one_last) if forward else (one_last == one_before)
        far = moved(far, float(length), pace)
        sums = [n + jnp.where(through, f, 0.0) for n, f in zip(near, far, strict=True)]
        return (stack_rows(sums + [two_last, one_before]),)

    return body


def joined_sums(count, length, chips):
    def body(near, far, vectors):
        pace = jnp.exp(vectors[9:10])
        sums, last, before = split_message(near, count)
        more, far_last, far_before = split_message(far, count)
        more = moved(more, 2.0 * length * chips, pace)
        sums = [x + jnp.where(last == before, y, 0.0) for x, y in zip(sums, more, strict=True)]
        ids = [last, far_before] if count == 4 else [far_last, before]
        return (stack_rows(sums + ids),)

    return body


def carried(count, length, forward):
    def body(message, other, vectors, *got):
        core = places()[2]
        pace = jnp.exp(vectors[9:10])
        first, second = by_place(message, other)
        one, one_last, one_before = split_message(first, count)
        two, two_last, _ = split_message(second, count)
        total, last, before = split_message(got[0], count)
        through, chips = last == before, 1
        for i, message in enumerate(got[1:]):
            sums, last, before = split_message(message, count)
            sums = moved(sums, 2.0 * length * chips, pace)
            total = [t + jnp.where(through, x, 0.0) for t, x in zip(total, sums, strict=True)]
            through, chips = through & (last == before), chips + 2 ** (i + 1)
        inner, through = (one, one_last == one_before) if forward else (two, two_last == one_last)
        passed = moved(total, float(length), pace)
        passed = [x + jnp.where(through, y, 0.0) for x, y in zip(inner, passed, strict=True)]
        chosen = core == (1 if forward else 0)
        return (
            jnp.stack(
                [to_lanes(jnp.where(chosen, p, t)) for p, t in zip(passed, total, strict=True)]
            ),
        )

    return body


def carry_chip(values, vectors, length, forward, plain):
    count = 4 if forward else 2
    width = values.shape[1]
    other = to_core(values)
    (chip,) = fuse(
        chip_sums(count, length, forward), [((SUBS, width), FULL)], values, other, vectors, plain=plain
    )
    return other, chip


def carry_steps(chip, vectors, length, forward, plain, after=()):
    cols = lax.axis_size("seq")
    count = 4 if forward else 2
    width = chip.shape[1]

    def route(step):
        def go(b, s):
            target = s + 2 * step * (1 if forward else -1)
            return (b, target) if 0 <= target < cols else None

        return go

    got, sums, step = [], chip, 1
    while step < cols // 2:
        got.append(send(sums, route(step)))
        if 2 * step < cols // 2:
            (sums,) = fuse(
                joined_sums(count, length, step),
                [((SUBS, width), FULL)],
                sums,
                got[-1],
                vectors,
                after=after,
                plain=plain,
            )
        step *= 2
    return got


def carry_end(parts, length, forward, plain, after=()):
    count = 4 if forward else 2
    return fuse(
        carried(count, length, forward),
        [((count, parts[0].shape[1] // LANES, LANES), FULL)],
        *parts,
        after=after,
        plain=plain,
    )[0]


def split_parts(x):
    high = x.astype(LOW)
    return [high, (x - high.astype(FULL)).astype(LOW)]


def add_batch(own, got, count, plain, after=(), vectors=None):
    depth = lax.axis_size("seq") // 2
    height, width = own.shape
    extra = 32 if vectors is not None else 0
    height -= extra
    part = height // (count * depth)
    inputs = [own, *got] + ([vectors] if extra else [])

    def body(own, *got):
        got, sums = (got[:-1], got[-1]) if extra else (got, None)
        got = [x.astype(FULL) for x in got]
        total = sum((x[:height] for x in got), own[:height].astype(FULL))
        blocks = [
            [total[(i * depth + k) * part : (i * depth + k + 1) * part] for i in range(count)]
            for k in range(depth)
        ]
        first, rest = blocks[0], [[x.astype(LOW) for x in block] for block in blocks[1:]]
        if extra:
            sums = sum((x[height : height + 16] + x[height + 16 :] for x in got), sums)
            first, rest = first + [sums], [block + split_parts(sums) for block in rest]
        return [jnp.concatenate(x, axis=0) for x in [first, *rest]]

    return fuse(
        body,
        [((count * part + extra // 2, width), FULL)]
        + [((count * part + extra, width), LOW)] * (depth - 1),
        *inputs,
        after=after,
        plain=plain,
        token=True,
    )


def add_depth(pieces, count, part, outs, last, plain, after=()):
    width = pieces[0].shape[1]
    height = count * part
    got = [to_depth(pieces[k], k) for k in range(1, len(pieces))]

    def body(own, *got):
        got = [x.astype(FULL) for x in got]
        total = sum((x[:height] for x in got), own[:height])
        results = [total[i * part : (i + 1) * part] for i in range(count)]
        if last is not None:
            sums = sum((x[height : height + 16] + x[height + 16 :] for x in got), own[height:])
            results += last(sums)
        return results

    return fuse(
        body, [((part, width), FULL)] * count + outs, pieces[0], *got, after=after, plain=plain
    )


def halve_depth(pieces, plain):
    half = len(pieces) // 2
    height, width = pieces[0].shape
    joined = fuse(
        lambda *x: (jnp.concatenate(x, axis=0),),
        [((half * height, width), LOW)],
        *pieces[half:],
        plain=plain,
    )[0]
    got = to_depth(joined, half)

    def body(own, *rest):
        rest, got = rest[:-1], rest[-1].astype(FULL)
        blocks = [got[i * height : (i + 1) * height] for i in range(half)]
        return [own + blocks[0]] + [
            (x.astype(FULL) + y).astype(LOW) for x, y in zip(rest, blocks[1:], strict=True)
        ]

    return fuse(
        body,
        [((height, width), FULL)] + [((height, width), LOW)] * (half - 1),
        *pieces[:half],
        got,
        plain=plain,
        token=True,
    )


def per_device(
    layer_input,
    segment_ids,
    out_cotangent,
    key_weight,
    value_weight,
    recept_weight,
    output_weight,
    channel_key,
    channel_value,
    channel_recept,
    norm_gains,
    norm_offsets,
    mix_coeffs,
    time_decay,
    time_first,
):
    rows, cols = sizes()
    depth = cols // 2
    length, width = layer_input.shape[1:]
    own = key_weight.shape[0]
    hidden_width = channel_key.shape[1]
    part_width = hidden_width // rows
    half = width // 2
    plain = own % 16 != 0
    low_act, full_act = ((length, width), LOW), ((length, width), FULL)
    narrow = ((length, LANES), FULL)
    square = ((width, width), LOW)
    edge_row = ((SUBS, width), FULL)
    raw, cotangent = layer_input[0], out_cotangent[0]
    mac = 2 * length * width * width

    small = [norm_gains, norm_offsets, mix_coeffs, time_decay[None], time_first[None]]
    n_vectors = sum(x.shape[0] for x in small)

    def prepare(key, value, recept, output, gate, cross, raw, ids, *small):
        b, z, core = places()
        device = b * cols + z * 2 + core
        lane = lax.broadcasted_iota(jnp.int32, (own, width), 1)
        home = (lane == device * own + row_index((own, width))).astype(FULL).astype(LOW)
        placed = jnp.zeros((16, width), FULL)
        at = 0
        for x in small:
            x = dot(x, home)
            for i in range(x.shape[0]):
                placed = jnp.where(row_index(placed.shape) == at, x[i : i + 1], placed)
                at += 1
        blocks = [cross[:, j * part_width : (j + 1) * part_width] for j in range(rows)]
        ids = ids.astype(FULL)
        last = raw[length - 16 :].astype(FULL)[15:16]
        edge = stack_rows([last, jnp.broadcast_to(ids[:, length - 1 :], (1, width))], 16)
        return (
            [
                jnp.concatenate([key, value, placed.astype(LOW)], axis=0),
                jnp.concatenate([recept, output, gate], axis=0),
                edge,
                jnp.broadcast_to(ids, (LANES, length)).T,
            ]
            + [pick(blocks, b ^ k) for k in range(rows)]
        )

    first_pack, second_pack, edge, ids_lanes, *crossing = fuse(
        prepare,
        [((2 * own + 16, width), LOW), ((3 * own, width), LOW), ((16, width), FULL), narrow]
        + [((own, part_width), LOW)] * rows,
        key_weight,
        value_weight,
        recept_weight,
        output_weight,
        channel_recept,
        channel_key,
        raw,
        segment_ids,
        *small,
        plain=plain,
        fetch=True,
        limit=58,
    )
    deep_got = [to_depth(first_pack, k) for k in range(1, depth)]
    cross_got = [to_batch(crossing[k], k) for k in range(1, rows)]
    edge = send_next(edge)

    def begin(raw, edge, ids):
        b, z, core = places()
        place = lax.broadcasted_iota(jnp.int32, (1, width), 1)
        block, row = place >> log2(own), place & (own - 1)
        k_core = block >> log2(rows * depth)
        k_batch = (block >> log2(depth)) & (rows - 1)
        k_depth = block & (depth - 1)
        target = ((k_batch ^ b) << log2(cols)) + ((k_depth ^ z) << 1) + (k_core ^ core)
        feature = (target << log2(own)) + row
        order = jnp.concatenate(
            [
                (row_index((LANES, width)) + i * LANES == feature).astype(FULL).astype(LOW)
                for i in range(width // LANES)
            ],
            axis=0,
        )
        unit, scale = unit_norm(dot(raw, order))
        edge_unit = unit_norm(dot(edge.astype(LOW), order))[0]
        before = jnp.where((z == 0) & (core == 0), -1.0, edge[1:2])
        before_lanes = before[:, :LANES]
        last = ids[length - 1 : length]
        keep = (ids == down(ids, before_lanes, plain)).astype(FULL)
        opened = (ids == before_lanes).astype(FULL)
        closing = (ids == last).astype(FULL)
        last = jnp.broadcast_to(last[:, :1], (1, width))
        scale = jnp.broadcast_to(scale, (length, LANES))
        return (
            order,
            unit,
            keep,
            jnp.concatenate([keep, opened, closing, scale], axis=1),
            stack_rows([edge_unit[0:1], last, before]),
        )

    order, unit_one, keep, statics, edges = fuse(
        begin,
        [square, full_act, narrow, ((length, 4 * LANES), FULL), edge_row],
        raw,
        edge,
        ids_lanes,
        plain=plain,
    )

    def deepen_first(second, *x):
        vectors = sum(y[2 * own :].astype(FULL) for y in x).astype(LOW)
        parts = [y[i * own : (i + 1) * own] for i in range(2) for y in x]
        return jnp.concatenate(parts + [vectors], axis=0), second

    first_deep, second_pack = fuse(
        deepen_first,
        [((2 * depth * own + 16, width), LOW), (second_pack.shape, LOW)],
        second_pack,
        first_pack,
        *deep_got,
        after=(order, *cross_got),
        plain=plain,
    )
    first_wide = [to_batch(first_deep, k) for k in range(1, rows)]
    first_pieces = [first_deep] + first_wide
    first_pieces = first_pieces + [to_core(piece) for piece in first_pieces]
    second_got = [to_depth(second_pack, k) for k in range(1, depth)]

    cross_rows = rows * own * part_width // width
    packed_rows = cross_rows + channel_value.shape[0]

    def deepen(value, *x):
        b = places()[0]
        cross, x = x[:rows], x[rows:]
        cross = jnp.concatenate([pick(cross, j ^ b) for j in range(rows)], axis=0)
        return (
            jnp.stack([y[: 2 * own] for y in x]),
            jnp.stack([y[2 * own :] for y in x]),
            jnp.concatenate([cross.reshape(cross_rows, width), value], axis=0),
        )

    second_deep, third_deep, channel_pack = fuse(
        deepen,
        [
            ((depth, 2 * own, width), LOW),
            ((depth, own, width), LOW),
            ((packed_rows, width), LOW),
        ],
        channel_value,
        crossing[0],
        *cross_got,
        second_pack,
        *second_got,
        after=first_wide,
        plain=plain,
    )
    channel_pack = lax.all_gather(channel_pack, "seq", axis=0, tiled=True)

    def unpack_channel(x):
        x = x.reshape(cols, packed_rows, width)
        key = x[:, :cross_rows].reshape(cols, rows, own, part_width)
        key = jnp.concatenate(
            [key[j, i] for i in range(rows) for j in range(cols)], axis=0
        )
        return key, x[:, cross_rows:].reshape(part_width, width)

    part_key, part_value = fuse(
        unpack_channel,
        [((width, part_width), LOW), ((part_width, width), LOW)],
        channel_pack,
        plain=plain,
    )

    second_wide = [to_batch(second_deep, k) for k in range(1, rows)]
    (third_deep,) = fuse(
        lambda x: (x,), [(third_deep.shape, LOW)], third_deep, after=second_wide, plain=plain
    )
    third_wide = [to_batch(third_deep, k) for k in range(1, rows)]

    def joined(deep, wide, after):
        (mine,) = fuse(
            lambda *x: (jnp.concatenate(x, axis=0),),
            [((rows * depth,) + deep.shape[1:], LOW)],
            deep,
            *wide,
            after=after,
            plain=plain,
        )
        return mine, to_core(mine)


    def gathered(pieces, start):
        return jnp.concatenate(
            [piece[:, start : start + own].reshape(-1, width) for piece in pieces], axis=0
        )

    def front(unit, statics, edges, order, *pieces):
        height = depth * own
        vectors = sum(piece[2 * height :].astype(FULL) for piece in pieces)
        lines = dot(vectors.astype(LOW), order)
        normed = unit * lines[0:1] + lines[2:3]
        edge_normed = edges[0:1] * lines[0:1] + lines[2:3]
        prior = down(normed, edge_normed, plain) * statics[:, :1]
        mix_key = mixing(normed, prior, lines[4:5])
        mix_value = mixing(normed, prior, lines[5:6])
        mix_recept = mixing(normed, prior, lines[6:7])
        key_all = jnp.concatenate([piece[:height] for piece in pieces], axis=0)
        value_all = jnp.concatenate([piece[height : 2 * height] for piece in pieces], axis=0)
        key, value = dot(mix_key, key_all), dot(mix_value, value_all)
        pace = jnp.exp(vectors[9:10])
        left = length - 1.0 - row_index((length, width)).astype(FULL)
        den = jnp.where(statics[:, 2 * LANES : 2 * LANES + 1] > 0.5, jnp.exp(key - pace * left), 0.0)
        num = den * value
        message = stack_rows(
            [column_sum(num), column_sum(den), column_sum(num * left), column_sum(den * left)]
            + [edges[1:2], edges[2:3]]
        )
        return (
            jnp.concatenate([vectors, lines], axis=0),
            normed - prior,
            jnp.stack([mix_key, mix_value, mix_recept]),
            jnp.stack([key_all, value_all]),
            key,
            value,
            message,
            jnp.stack([to_lanes(jnp.exp(-pace)), to_lanes(vectors[10:11])]),
        )

    (
        vectors,
        difference_one,
        mixes,
        first_all,
        key_act,
        value_act,
        message,
        rates,
    ) = fuse(
        front,
        [
            ((32, width), FULL),
            full_act,
            ((3, length, width), LOW),
            ((2, width, width), LOW),
            full_act,
            full_act,
            edge_row,
            ((2, width // LANES, LANES), FULL),
        ],
        unit_one,
        statics,
        edges,
        order,
        *first_pieces,
        plain=plain,
        limit=32,
    )
    other, chip = carry_chip(message, vectors, length, True, plain)
    got = carry_steps(chip, vectors, length, True, plain)
    carry = carry_end([message, other, vectors] + got, length, True, plain)

    def receptance(mixes, *pieces):
        recept_all = gathered(pieces, 0)
        return jax.nn.sigmoid(dot(mixes[2], recept_all)), recept_all, gathered(pieces, own)

    recept_act, recept_all, output_all = fuse(
        receptance,
        [full_act, square, square],
        mixes,
        *joined(second_deep, second_wide, (carry,)),
        plain=plain,
        limit=32,
    )
    key_tiles, value_tiles = to_tiles(key_act), to_tiles(value_act)
    scanned = run_forward(keep, key_tiles, value_tiles, rates, carry)

    def attend(scanned, recept, order, output_all, raw, vectors):
        gated = dot((recept * untile(scanned[0], width // LANES)).astype(LOW), order).astype(LOW)
        middle = raw.astype(FULL) + dot(gated, output_all)
        unit, scale = unit_norm(middle)
        normed = unit * vectors[1:2] + vectors[3:4]
        return (
            gated,
            middle,
            jnp.concatenate([unit, jnp.broadcast_to(scale, (length, LANES))], axis=1),
            stack_rows([normed[length - 1 :]]),
        )

    gated, middle, unit_two, edge_two = fuse(
        attend,
        [low_act, full_act, ((length, width + LANES), FULL), edge_row],
        scanned,
        recept_act,
        order,
        output_all,
        raw,
        vectors,
        plain=plain,
    )
    edge_two = send_next(edge_two)

    def mix_two(unit, edge, statics, vectors):
        normed = unit[:, :width] * vectors[1:2] + vectors[3:4]
        prior = down(normed, edge[0:1], plain) * statics[:, :1]
        return (
            mixing(normed, prior, vectors[7:8]),
            mixing(normed, prior, vectors[8:9]),
            normed - prior,
        )

    mix_hidden, mix_gate, difference_two, mixed_token = fuse(
        mix_two, [low_act, low_act, full_act], unit_two, edge_two, statics, vectors, plain=plain, token=True
    )
    shared = [mix_hidden] + [to_batch(mix_hidden, k) for k in range(1, rows)]

    def channel(x, key, value):
        positive = jnp.maximum(dot(x, key), 0.0)
        squared = (positive * positive).astype(LOW)
        return squared, dot(squared, value)

    def channel_low(x, key, value):
        squared, out = channel(x, key, value)
        return squared, out.astype(LOW)

    hidden_act = ((length, part_width), LOW)
    squares, returned = [], []
    for k in range(rows):
        squared, out = fuse(
            channel_low if k else channel,
            [hidden_act, low_act if k else full_act],
            shared[k],
            part_key,
            part_value,
            plain=plain,
        )
        squares.append(squared)
        returned.append(to_batch(out, k) if k else out)

    def gating(mix, order, gated, mixes, *pieces):
        gate_all = gathered(pieces, 0)
        mix = dot(mix, order).astype(LOW)
        sides = jnp.stack([mixes[0], mixes[1], mixes[2], gated, mix])
        return jax.nn.sigmoid(dot(mix, gate_all)), sides, gate_all

    gate, sides, gate_all = fuse(
        gating,
        [full_act, ((5, length, width), LOW), square],
        mix_gate,
        order,
        gated,
        mixes,
        *joined(third_deep, third_wide, (mixed_token,)),
        plain=plain,
    )

    def finish(own_part, gate, middle, grad_out, *got):
        out = sum((x.astype(FULL) for x in got), own_part)
        grad_out = grad_out.astype(FULL)
        return (
            (middle + gate * out).astype(LOW),
            (grad_out * gate).astype(LOW),
            (grad_out * out * gate * (1.0 - gate)).astype(LOW),
        )

    block_output, grad_values, grad_gate = fuse(
        finish,
        [low_act, low_act, low_act],
        returned[0],
        gate,
        middle,
        cotangent,
        *returned[1:],
        plain=plain,
    )

    shared_grad = [grad_values] + [to_batch(grad_values, k) for k in range(1, rows)]

    def channel_back(grad, squared, key, value):
        positive = jnp.sqrt(squared.astype(FULL))
        hidden = (dot_back(grad, value) * 2.0 * positive).astype(LOW)
        return hidden, dot_back(hidden, key)

    def channel_back_low(grad, squared, key, value):
        hidden, out = channel_back(grad, squared, key, value)
        return hidden, out.astype(LOW)

    def channel_back_own(grad, squared, key, value, grad_gate, gate_all, order):
        hidden, out = channel_back(grad, squared, key, value)
        return hidden, out, restore(dot_back(grad_gate, gate_all), order)

    hidden, out, grad_mix_gate = fuse(
        channel_back_own,
        [hidden_act, full_act, full_act],
        shared_grad[0],
        squares[0],
        part_key,
        part_value,
        grad_gate,
        gate_all,
        order,
        plain=plain,
    )
    hiddens, returned = [hidden], [out]
    for k in range(1, rows):
        hidden, out = fuse(
            channel_back_low,
            [hidden_act, low_act],
            shared_grad[k],
            squares[k],
            part_key,
            part_value,
            plain=plain,
        )
        hiddens.append(hidden)
        returned.append(to_batch(out, k))

    def paired(active, active_got, grad, grad_got):
        return dot_rows(
            jnp.concatenate([active[:, :half], active_got[:, half:]], axis=0),
            jnp.concatenate([grad, grad_got], axis=0),
        ).astype(LOW)

    def cut(terms, *more):
        part = half // rows
        return [
            jnp.concatenate([term[k * part : (k + 1) * part] for term in terms] + list(more), axis=0)
            for k in range(rows)
        ]

    def early_terms(sides, sides_got, grads, grads_got):
        return cut(
            [
                paired(sides[side], sides_got[side], grads[i], grads_got[i])
                for i, side in enumerate((3, 2, 4))
            ]
        )

    sides_got = to_core(sides)

    def unmix_two(own_part, grad_gate, difference, statics, vectors, *got):
        grad_hidden = sum((x.astype(FULL) for x in got), own_part)
        mix_h, mix_g = vectors[7:8], vectors[8:9]
        passed = (grad_hidden * (1.0 - mix_h) + grad_gate * (1.0 - mix_g)) * statics[:, :1]
        return (
            grad_hidden * mix_h + grad_gate * mix_g,
            passed,
            stack_rows([passed[0:1]]),
            stack_rows([column_sum(grad_hidden * difference), column_sum(grad_gate * difference)]),
        )

    own_two, passed_two, after_two, mix_sums_two = fuse(
        unmix_two,
        [full_act, full_act, edge_row, edge_row],
        returned[0],
        grad_mix_gate,
        difference_two,
        statics,
        vectors,
        *returned[1:],
        plain=plain,
    )
    after_two = send_back(after_two)

    def middle_back(
        own_part, passed, after, unit, grad_out, vectors, mix_sums, recept, scanned,
        output_all, order, statics, edges, grad_gate,
    ):
        wkv, inverse, slope = (untile(scanned[i], width // LANES) for i in range(3))
        unit, scale = unit[:, :width], unit[:, width : width + 1]
        grad_normed = own_part + up(passed, after[0:1], plain)
        part = norm_backward(grad_normed, unit, scale, vectors[1:2])
        grad_middle = grad_out.astype(FULL) + part
        grad_low = grad_middle.astype(LOW)
        grad_gated = restore(dot_back(grad_low, output_all), order)
        grad_wkv = grad_gated * recept
        grad_recept = (grad_wkv * wkv * (1.0 - recept)).astype(LOW)
        share = grad_wkv * inverse
        pace = jnp.exp(vectors[9:10])
        step = row_index((length, width)).astype(FULL)
        head = jnp.where(statics[:, LANES : LANES + 1] > 0.5, share * jnp.exp(-pace * step), 0.0)
        return (
            grad_middle,
            jnp.stack([grad_low, grad_recept, grad_gate]),
            share,
            stack_rows([column_sum(head), column_sum(head * wkv), edges[1:2], edges[2:3]]),
            stack_rows(
                [
                    column_sum(grad_normed * unit),
                    column_sum(grad_normed),
                    mix_sums[0:1],
                    mix_sums[1:2],
                    -pace * column_sum(grad_wkv * slope),
                ]
            ),
        )

    grad_middle, grad_three, share, message, sums_two = fuse(
        middle_back,
        [full_act, ((3, length, width), LOW), full_act, edge_row, edge_row],
        own_two,
        passed_two,
        after_two,
        unit_two,
        cotangent,
        vectors,
        mix_sums_two,
        recept_act,
        scanned,
        output_all,
        order,
        statics,
        edges,
        grad_gate,
        plain=plain,
        limit=24,
    )

    other, chip_back = carry_chip(message, vectors, length, False, plain)

    *early, early_token = fuse(
        early_terms,
        [((3 * half // rows, width), LOW)] * rows,
        sides,
        sides_got,
        grad_three,
        to_core(grad_three),
        after=(chip_back,),
        plain=plain,
        token=True,
    )
    carry_parts = [message, other, vectors] + carry_steps(
        chip_back, vectors, length, False, plain, (early_token,)
    )
    early_got = [to_batch(early[k], k) for k in range(1, rows)]
    def channel_terms(*x):
        shared, hiddens, squares, grads = (
            jnp.concatenate(x[i * rows : (i + 1) * rows], axis=0) for i in range(4)
        )
        key = dot_rows(shared, hiddens).astype(LOW)
        value = dot_rows(squares, grads).astype(LOW)
        key = key.reshape(rows, cols, own, part_width)
        value_rows = part_width // cols
        parts = []
        for j in range(cols):
            block = jnp.concatenate([key[i, j] for i in range(rows)], axis=0)
            parts += [
                block.reshape(cross_rows, width),
                value[j * value_rows : (j + 1) * value_rows],
            ]
        return (jnp.concatenate(parts, axis=0),)

    channel_term, channel_token = fuse(
        channel_terms,
        [((cols * packed_rows, width), LOW)],
        *shared,
        *hiddens,
        *squares,
        *shared_grad,
        after=(early_token,),
        plain=plain,
        token=True,
        limit=12,
    )
    channel_sum = lax.psum_scatter(channel_term, "seq", scatter_dimension=0, tiled=True)
    carry_back = carry_end(carry_parts, length, False, plain, (channel_token, early_token))
    grad_key, grad_value, first_term = run_backward(
        keep, key_tiles, value_tiles, scanned, to_tiles(share), rates, carry_back
    )

    def lower(key, value):
        return (jnp.stack([key.astype(LOW), value.astype(LOW)]),)

    (grad_late,) = fuse(
        lower,
        [((2, length, width), LOW)],
        *lax.optimization_barrier((from_tiles(grad_key, width), from_tiles(grad_value, width))),
        plain=plain,
    )

    def unmix_one(grads, grad_three, first_all, recept_all, vectors, statics, difference, order):
        lines = vectors[16:]
        grad_key = dot_back(grads[0], first_all[0])
        grad_value = dot_back(grads[1], first_all[1])
        grad_recept = dot_back(grad_three[1], recept_all)
        m_key, m_value, m_recept = lines[4:5], lines[5:6], lines[6:7]
        passed = (
            grad_key * (1.0 - m_key) + grad_value * (1.0 - m_value) + grad_recept * (1.0 - m_recept)
        ) * statics[:, :1]
        return (
            grad_key * m_key + grad_value * m_value + grad_recept * m_recept,
            passed,
            restore(passed[:16], order)[:SUBS],
            stack_rows([column_sum(x * difference) for x in (grad_key, grad_value, grad_recept)]),
        )

    own_one, passed_one, after_one, mix_sums_one = fuse(
        unmix_one,
        [full_act, full_act, edge_row, edge_row],
        grad_late,
        grad_three,
        first_all,
        recept_all,
        vectors,
        statics,
        difference_one,
        order,
        plain=plain,
        limit=24,
    )
    after_one = send_back(after_one)

    def input_back(
        own_part, passed, after, unit, statics, vectors, order, grad_middle, mix_sums, sums_two, first
    ):
        lines, scale = vectors[16:], statics[:, 3 * LANES : 3 * LANES + 1]
        after = jnp.where(row_index((16, width)) == 0, after[0:1], 0.0)
        grad_normed = own_part + up(passed, restore_in(after, order)[0:1], plain)
        part = norm_backward(grad_normed, unit, scale, lines[0:1])
        ordered = stack_rows(
            [
                column_sum(grad_normed * unit),
                column_sum(grad_normed),
                mix_sums[0:1],
                mix_sums[1:2],
                mix_sums[2:3],
            ],
            16,
        )
        ordered = restore(ordered, order)
        total = [ordered[0:1], sums_two[0:1], ordered[1:2], sums_two[1:2]]
        total += [ordered[2:3], ordered[3:4], ordered[4:5], sums_two[2:3], sums_two[3:4]]
        total += [sums_two[4:5], from_lanes(first)]
        return grad_middle + restore(part, order), stack_rows(total, 16)

    input_grad, sums = fuse(
        input_back,
        [full_act, ((16, width), FULL)],
        own_one,
        passed_one,
        after_one,
        unit_one,
        statics,
        vectors,
        order,
        grad_middle,
        mix_sums_one,
        sums_two,
        first_term,
        plain=plain,
        limit=24,
    )
    sums = sums + to_core(sums)
    *early_pieces, early_wide_token = add_batch(early[0], early_got, 3, plain, (sums,))
    early_half = None
    if depth == 4:
        *early_pieces, early_half = halve_depth(early_pieces, plain)

    def late_terms(sides, sides_got, grads, grads_got, sums):
        terms = [paired(sides[i], sides_got[i], grads[i], grads_got[i]) for i in range(2)]
        return cut(terms, *split_parts(sums))

    late = fuse(
        late_terms,
        [((2 * half // rows + 32, width), LOW)] * rows,
        sides,
        sides_got,
        grad_late,
        to_core(grad_late),
        sums,
        after=(early_wide_token,),
        plain=plain,
    )
    late_got = [to_batch(late[k], k) for k in range(1, rows)]
    def own_columns(total):
        b, z, core = places()
        device = b * cols + z * 2 + core
        if plain:
            total = lax.dynamic_slice(total, (0, device * own), (16, own))
        else:
            total = pltpu.roll(total, (width - device * own) & (width - 1), 1)[:, :own]
        return [total[0:2], total[2:4], total[4:9], total[9:10], total[10:11]]

    *late_pieces, late_token = add_batch(late[0], late_got, 2, plain, (early_half,), vectors=sums)
    output_grad, recept_grad, gate_grad = add_depth(early_pieces, 3, own, [], None, plain)
    key_grad, value_grad, gains_grad, offsets_grad, mixes_grad, decay_grad, first_grad = add_depth(
        late_pieces,
        2,
        own,
        [((2, own), FULL), ((2, own), FULL), ((5, own), FULL), ((1, own), FULL), ((1, own), FULL)],
        own_columns,
        plain,
    )

    (crossed,) = fuse(
        lambda x: (x[:cross_rows].reshape(rows, own, part_width),),
        [((rows, own, part_width), LOW)],
        channel_sum,
        after=(late_token,),
        plain=plain,
    )
    crossed = lax.all_to_all(crossed, "batch", 0, 0)

    def assemble(x, crossed):
        return (
            jnp.concatenate([crossed[j].astype(FULL) for j in range(rows)], axis=1),
            x[cross_rows:].astype(FULL),
        )

    channel_key_grad, channel_value_grad = fuse(
        assemble,
        [((own, hidden_width), FULL), (channel_value.shape, FULL)],
        channel_sum,
        crossed,
        plain=plain,
    )
    return (
        block_output[None],
        input_grad[None],
        key_grad,
        value_grad,
        recept_grad,
        output_grad,
        channel_key_grad,
        channel_value_grad,
        gate_grad,
        gains_grad,
        offsets_grad,
        mixes_grad,
        decay_grad[0],
        first_grad[0],
    )


def solution(mesh):
    tokens = P("batch", "seq", None)
    weight = P(BOTH, None)
    lines = P(None, BOTH)
    return jax.shard_map(
        per_device,
        mesh=mesh,
        in_specs=(tokens, P("batch", "seq"), tokens)
        + (weight,) * 7
        + (lines,) * 3
        + (P(BOTH),) * 2,
        out_specs=(tokens, tokens) + (weight,) * 7 + (lines,) * 3 + (P(BOTH),) * 2,
        check_vma=False,
    )
```

```python
import jax
import jax.numpy as jnp
from jax import lax
from jax.experimental import pallas as pl
from jax.experimental.pallas import tpu as pltpu
from jax.sharding import PartitionSpec as P

EPS = 1e-05
BOTH = ("batch", "seq")
LOW = jnp.bfloat16
FULL = jnp.float32
LANES = 128
SUBS = 8
MIB = 1024 * 1024
COST = 2000000
IN_VMEM = pl.BlockSpec(memory_space=pltpu.VMEM)
IN_HBM = pl.BlockSpec(memory_space=pltpu.HBM)


def sizes():
    return lax.axis_size("batch"), lax.axis_size("seq")


def places():
    s = lax.axis_index("seq")
    return lax.axis_index("batch"), s >> 1, s & 1


def send(block, route):
    rows, cols = sizes()
    pairs = []
    for b in range(rows):
        for s in range(cols):
            target = route(b, s)
            if target is not None:
                pairs.append((b * cols + s, target[0] * cols + target[1]))
    return lax.ppermute(block, BOTH, pairs)


def send_next(block):
    cols = lax.axis_size("seq")
    return send(block, lambda b, s: (b, s + 1) if s + 1 < cols else None)


def send_back(block):
    return send(block, lambda b, s: (b, s - 1) if s > 0 else None)


def to_core(block):
    return send(block, lambda b, s: (b, s ^ 1))


def to_batch(block, k):
    return send(block, lambda b, s: (b ^ k, s))


def to_depth(block, k):
    return send(block, lambda b, s: (b, s ^ (2 * k)))


def fuse(body, outs, *args, after=(), limit=16, plain=False, fetch=False, token=False):
    if plain:
        return tuple(body(*args)) + (None,) * token
    after = [x for x in after if x is not None]
    count, held = len(args), len(args) + len(after)
    outs = [*outs, ((SUBS, LANES), FULL)] if token else outs

    def kernel(*refs):
        taken = refs[:count]
        if fetch:
            taken, arrived = refs[held + len(outs) : -1], refs[-1]
            copies = [
                pltpu.make_async_copy(refs[i], taken[i], arrived.at[i]) for i in range(count)
            ]
            for copy in copies:
                copy.start()
            for copy in copies:
                copy.wait()
        results = body(*[ref[...] for ref in taken])
        if token:
            results = [*results, jnp.zeros((SUBS, LANES), FULL)]
        for ref, value in zip(refs[held : held + len(outs)], results, strict=True):
            ref[...] = value


    return pl.pallas_call(
        kernel,
        out_shape=tuple(jax.ShapeDtypeStruct(shape, dtype) for shape, dtype in outs),
        in_specs=[IN_HBM if fetch else IN_VMEM] * count + [IN_VMEM] * len(after),
        out_specs=(IN_VMEM,) * len(outs),
        scratch_shapes=[pltpu.VMEM(x.shape, x.dtype) for x in args]
        + [pltpu.SemaphoreType.DMA((count,))]
        if fetch
        else [],
        compiler_params=pltpu.CompilerParams(vmem_limit_bytes=limit * MIB),
        cost_estimate=pl.CostEstimate(flops=COST, bytes_accessed=COST, transcendentals=0),
    )(*args, *after)


def dot(x, w):
    return lax.dot_general(x, w, (((1,), (0,)), ((), ())), preferred_element_type=FULL)


def dot_back(x, w):
    return lax.dot_general(x, w, (((1,), (1,)), ((), ())), preferred_element_type=FULL)


def dot_rows(x, y):
    return lax.dot_general(x, y, (((0,), (0,)), ((), ())), preferred_element_type=FULL)


def restore(x, order):
    high = x.astype(LOW)
    rest = (x - high.astype(FULL)).astype(LOW)
    return dot_back(high, order) + dot_back(rest, order)


def restore_in(x, order):
    high = x.astype(LOW)
    rest = (x - high.astype(FULL)).astype(LOW)
    return dot(high, order) + dot(rest, order)


def row_index(shape):
    return lax.broadcasted_iota(jnp.int32, shape, 0)


def stack_rows(rows, count=SUBS):
    width = rows[0].shape[1]
    index = row_index((count, width))
    out = jnp.zeros((count, width), FULL)
    for i, row in enumerate(rows):
        out = jnp.where(index == i, row, out)
    return out


def down(x, first, plain):
    rolled = jnp.roll(x, 1, 0) if plain else pltpu.roll(x, 1, 0)
    return jnp.where(row_index(x.shape) == 0, first, rolled)


def up(x, last, plain):
    count = x.shape[0]
    rolled = jnp.roll(x, -1, 0) if plain else pltpu.roll(x, count - 1, 0)
    return jnp.where(row_index(x.shape) == count - 1, last, rolled)


def column_sum(x):
    return jnp.sum(x, axis=0, keepdims=True)


def lane_mean(x):
    return jnp.mean(x, axis=-1, keepdims=True)


def unit_norm(hidden):
    centred = hidden - lane_mean(hidden)
    scale = lax.rsqrt(lane_mean(centred * centred) + EPS)
    return centred * scale, scale


def norm_backward(grad, unit, scale, gain):
    inner = grad * gain
    centred = inner - lane_mean(inner)
    return scale * (centred - unit * lane_mean(inner * unit))


def mixing(normed, prior, coeff):
    return (normed * coeff + prior * (1.0 - coeff)).astype(LOW)


def pick(values, index):
    out = values[0]
    for i in range(1, len(values)):
        out = jnp.where(index == i, values[i], out)
    return out


def log2(n):
    return n.bit_length() - 1


def untile(x, blocks):
    count = x.shape[0] // blocks
    x = x.reshape(count // SUBS, blocks, SUBS, LANES)
    return jnp.concatenate([x[:, i].reshape(count, LANES) for i in range(blocks)], axis=1)


def to_lanes(row):
    return jnp.concatenate(
        [row[:, i * LANES : (i + 1) * LANES] for i in range(row.shape[1] // LANES)], axis=0
    )


def from_lanes(x):
    return jnp.concatenate([x[i : i + 1] for i in range(x.shape[0])], axis=1)


def to_tiles(x):
    count, width = x.shape
    blocks = width // LANES
    x = x.reshape(count // SUBS, SUBS, blocks, LANES).transpose(0, 2, 1, 3)
    return x.reshape(count * blocks, LANES)


def from_tiles(x, width):
    blocks = width // LANES
    count = x.shape[0] // blocks
    x = x.reshape(count // SUBS, blocks, SUBS, LANES).transpose(0, 2, 1, 3)
    return x.reshape(count, width)


def position(i, r, blocks):
    return pl.ds(i * (SUBS * blocks) + r, blocks, stride=SUBS)


def forward_scan(keep_ref, key_ref, value_ref, rates_ref, carry_ref, out_ref):
    blocks = rates_ref.shape[1]
    fade, bonus = rates_ref[0], rates_ref[1]

    def eight(i, state):
        num, den, num_slope, den_slope = state
        for r in range(SUBS):
            at = position(i, r, blocks)
            key, value = key_ref[at, :], value_ref[at, :]
            keep = keep_ref[pl.ds(i * SUBS + r, 1), :]
            num, den, num_slope, den_slope = (
                num * keep,
                den * keep,
                num_slope * keep,
                den_slope * keep,
            )
            reward = jnp.exp(bonus + key)
            weight = jnp.exp(key)
            inverse = 1.0 / (den + reward)
            wkv = (num + reward * value) * inverse
            out_ref[0, at, :] = wkv
            out_ref[1, at, :] = inverse
            out_ref[2, at, :] = (num_slope - wkv * den_slope) * inverse
            num_slope = fade * (num_slope + num)
            den_slope = fade * (den_slope + den)
            num = fade * num + weight * value
            den = fade * den + weight
        return num, den, num_slope, den_slope

    lax.fori_loop(
        0,
        keep_ref.shape[0] // SUBS,
        eight,
        (carry_ref[0], carry_ref[1], carry_ref[2], carry_ref[3]),
    )


def backward_scan(
    keep_ref, key_ref, value_ref, scanned_ref, share_ref, rates_ref, carry_ref, key_out, value_out, first_out
):
    blocks = rates_ref.shape[1]
    fade, bonus = rates_ref[0], rates_ref[1]
    groups = keep_ref.shape[0] // SUBS

    def eight(step, state):
        direct, scaled, first = state
        i = groups - 1 - step
        for r in reversed(range(SUBS)):
            at = position(i, r, blocks)
            key, value = key_ref[at, :], value_ref[at, :]
            wkv, share = scanned_ref[0, at, :], share_ref[at, :]
            keep = keep_ref[pl.ds(i * SUBS + r, 1), :]
            reward = share * jnp.exp(bonus + key)
            weight = jnp.exp(key)
            bonus_part = reward * (value - wkv)
            key_out[at, :] = weight * (direct * value - scaled) + bonus_part
            value_out[at, :] = weight * direct + reward
            first = first + bonus_part
            direct = (share + fade * direct) * keep
            scaled = (share * wkv + fade * scaled) * keep
        return direct, scaled, first

    first_out[...] = lax.fori_loop(
        0, groups, eight, (carry_ref[0], carry_ref[1], jnp.zeros_like(fade))
    )[2]


def run_forward(keep, key, value, rates, carry):
    return pl.pallas_call(
        forward_scan,
        out_shape=jax.ShapeDtypeStruct((3,) + key.shape, FULL),
        in_specs=[IN_VMEM] * 5,
        out_specs=IN_VMEM,
        compiler_params=pltpu.CompilerParams(vmem_limit_bytes=8 * MIB),
        cost_estimate=pl.CostEstimate(
            flops=20 * key.size, bytes_accessed=20 * key.size, transcendentals=3 * key.size
        ),
    )(keep, key, value, rates, carry)


def run_backward(keep, key, value, wkv, share, rates, carry):
    tiles = jax.ShapeDtypeStruct(key.shape, FULL)
    return pl.pallas_call(
        backward_scan,
        out_shape=(tiles, tiles, jax.ShapeDtypeStruct(rates.shape[1:], FULL)),
        in_specs=[IN_VMEM] * 7,
        out_specs=(IN_VMEM,) * 3,
        compiler_params=pltpu.CompilerParams(vmem_limit_bytes=8 * MIB),
        cost_estimate=pl.CostEstimate(
            flops=20 * key.size, bytes_accessed=24 * key.size, transcendentals=2 * key.size
        ),
    )(keep, key, value, wkv, share, rates, carry)


def moved(sums, span, pace):
    fade = jnp.exp(-pace * span)
    if len(sums) == 4:
        num, den, num_slope, den_slope = sums
        return [
            fade * num,
            fade * den,
            fade * (num_slope + span * num),
            fade * (den_slope + span * den),
        ]
    return [fade * x for x in sums]


def split_message(message, count):
    return [message[i : i + 1] for i in range(count)], message[count : count + 1], message[count + 1 : count + 2]


def by_place(message, other):
    core = places()[2]
    return jnp.where(core == 0, message, other), jnp.where(core == 0, other, message)


def chip_sums(count, length, forward):
    def body(message, other, vectors):
        pace = jnp.exp(vectors[9:10])
        first, second = by_place(message, other)
        one, one_last, one_before = split_message(first, count)
        two, two_last, _ = split_message(second, count)
        near, far = (two, one) if forward else (one, two)
        through = (two_last == one_last) if forward else (one_last == one_before)
        far = moved(far, float(length), pace)
        sums = [n + jnp.where(through, f, 0.0) for n, f in zip(near, far, strict=True)]
        return (stack_rows(sums + [two_last, one_before]),)

    return body


def joined_sums(count, length, chips):
    def body(near, far, vectors):
        pace = jnp.exp(vectors[9:10])
        sums, last, before = split_message(near, count)
        more, far_last, far_before = split_message(far, count)
        more = moved(more, 2.0 * length * chips, pace)
        sums = [x + jnp.where(last == before, y, 0.0) for x, y in zip(sums, more, strict=True)]
        ids = [last, far_before] if count == 4 else [far_last, before]
        return (stack_rows(sums + ids),)

    return body


def carried(count, length, forward):
    def body(message, other, vectors, *got):
        core = places()[2]
        pace = jnp.exp(vectors[9:10])
        first, second = by_place(message, other)
        one, one_last, one_before = split_message(first, count)
        two, two_last, _ = split_message(second, count)
        total, last, before = split_message(got[0], count)
        through, chips = last == before, 1
        for i, message in enumerate(got[1:]):
            sums, last, before = split_message(message, count)
            sums = moved(sums, 2.0 * length * chips, pace)
            total = [t + jnp.where(through, x, 0.0) for t, x in zip(total, sums, strict=True)]
            through, chips = through & (last == before), chips + 2 ** (i + 1)
        inner, through = (one, one_last == one_before) if forward else (two, two_last == one_last)
        passed = moved(total, float(length), pace)
        passed = [x + jnp.where(through, y, 0.0) for x, y in zip(inner, passed, strict=True)]
        chosen = core == (1 if forward else 0)
        return (
            jnp.stack(
                [to_lanes(jnp.where(chosen, p, t)) for p, t in zip(passed, total, strict=True)]
            ),
        )

    return body


def carry_chip(values, vectors, length, forward, plain):
    count = 4 if forward else 2
    width = values.shape[1]
    other = to_core(values)
    (chip,) = fuse(
        chip_sums(count, length, forward), [((SUBS, width), FULL)], values, other, vectors, plain=plain
    )
    return other, chip


def carry_steps(chip, vectors, length, forward, plain, after=()):
    cols = lax.axis_size("seq")
    count = 4 if forward else 2
    width = chip.shape[1]

    def route(step):
        def go(b, s):
            target = s + 2 * step * (1 if forward else -1)
            return (b, target) if 0 <= target < cols else None

        return go

    got, sums, step = [], chip, 1
    while step < cols // 2:
        got.append(send(sums, route(step)))
        if 2 * step < cols // 2:
            (sums,) = fuse(
                joined_sums(count, length, step),
                [((SUBS, width), FULL)],
                sums,
                got[-1],
                vectors,
                after=after,
                plain=plain,
            )
        step *= 2
    return got


def carry_end(parts, length, forward, plain, after=()):
    count = 4 if forward else 2
    return fuse(
        carried(count, length, forward),
        [((count, parts[0].shape[1] // LANES, LANES), FULL)],
        *parts,
        after=after,
        plain=plain,
    )[0]


def columns_at(x, start, count, plain):
    width = x.shape[1]
    if plain:
        return jnp.roll(x, -start, 1)[:, :count]
    return pltpu.roll(x, (width - start) & (width - 1), 1)[:, :count]


def pack_vectors(x, width):
    count = width // x.shape[1]
    high = x.astype(LOW).astype(FULL)
    rows = [
        jnp.concatenate([part[i + j : i + j + 1] for j in range(count)], axis=1)
        for part in (high, x - high)
        for i in range(0, 16, count)
    ]
    return stack_rows(rows, 16).astype(LOW)


def unpack_vectors(x, columns):
    x = x.astype(FULL)
    count = x.shape[1] // columns
    height = 16 // count
    x = x[:height] + x[height : 2 * height]
    return stack_rows(
        [
            x[i // count : i // count + 1, i % count * columns : (i % count + 1) * columns]
            for i in range(16)
        ],
        16,
    )


def add_batch(own, got, count, plain, after=(), vectors=None):
    batch, cols = sizes()
    depth = cols // 2
    width = own.shape[1]
    extra = 16 if vectors is not None else 0
    height = own.shape[0] - extra
    part = height // (count * depth)
    columns = width // batch
    few = min(LANES, columns)
    each = columns // cols
    inputs = [own, *got] + ([vectors] if extra else [])

    def body(own, *got):
        got, sums = (got[:-1], got[-1]) if extra else (got, None)
        total = sum((x[:height].astype(FULL) for x in got), own[:height].astype(FULL))
        blocks = [
            [total[(i * depth + k) * part : (i * depth + k + 1) * part] for i in range(count)]
            for k in range(depth)
        ]
        first, rest = blocks[0], [[x.astype(LOW) for x in block] for block in blocks[1:]]
        results = [jnp.concatenate(first, axis=0)]
        if extra:
            b, z, core = places()
            sums = columns_at(sums, b * columns, columns, plain)
            sums = sum((unpack_vectors(x[height:], columns) for x in got), sums)
            cuts = [
                columns_at(sums, ((z ^ k) * 2 + core) * each, few, plain) for k in range(depth)
            ]
            rest = [block + [pack_vectors(x, width)] for block, x in zip(rest, cuts[1:], strict=True)]
            results.append(cuts[0])
        return results + [jnp.concatenate(x, axis=0) for x in rest]

    return fuse(
        body,
        [((count * part, width), FULL)]
        + [((16, few), FULL)] * (extra > 0)
        + [((count * part + extra, width), LOW)] * (depth - 1),
        *inputs,
        after=after,
        plain=plain,
        token=True,
    )


def add_depth(own, pieces, count, part, plain, vectors=None, outs=(), last=None):
    height = count * part
    got = [to_depth(piece, k + 1) for k, piece in enumerate(pieces)]

    def body(own, *got):
        sums = None
        if last is not None:
            sums, got = got[0], got[1:]
        total = sum((x[:height].astype(FULL) for x in got), own)
        results = [total[i * part : (i + 1) * part] for i in range(count)]
        if last is not None:
            results += last(sum((unpack_vectors(x[height:], sums.shape[1]) for x in got), sums))
        return results

    return fuse(
        body,
        [((part, own.shape[1]), FULL)] * count + list(outs),
        own,
        *([vectors] if last is not None else []),
        *got,
        plain=plain,
    )


def halve_depth(pieces, plain):
    half = len(pieces) // 2
    height, width = pieces[0].shape
    joined = fuse(
        lambda *x: (jnp.concatenate(x, axis=0),),
        [((half * height, width), LOW)],
        *pieces[half:],
        plain=plain,
    )[0]
    got = to_depth(joined, half)

    def body(own, *rest):
        rest, got = rest[:-1], rest[-1].astype(FULL)
        blocks = [got[i * height : (i + 1) * height] for i in range(half)]
        return [own + blocks[0]] + [
            (x.astype(FULL) + y).astype(LOW) for x, y in zip(rest, blocks[1:], strict=True)
        ]

    return fuse(
        body,
        [((height, width), FULL)] + [((height, width), LOW)] * (half - 1),
        *pieces[:half],
        got,
        plain=plain,
        token=True,
    )


def per_device(
    layer_input,
    segment_ids,
    out_cotangent,
    key_weight,
    value_weight,
    recept_weight,
    output_weight,
    channel_key,
    channel_value,
    channel_recept,
    norm_gains,
    norm_offsets,
    mix_coeffs,
    time_decay,
    time_first,
):
    rows, cols = sizes()
    depth = cols // 2
    length, width = layer_input.shape[1:]
    own = key_weight.shape[0]
    hidden_width = channel_key.shape[1]
    part_width = hidden_width // rows
    half = width // 2
    plain = own % 16 != 0
    low_act, full_act = ((length, width), LOW), ((length, width), FULL)
    narrow = ((length, LANES), FULL)
    square = ((width, width), LOW)
    edge_row = ((SUBS, width), FULL)
    raw, cotangent = layer_input[0], out_cotangent[0]
    mac = 2 * length * width * width

    small = [norm_gains, norm_offsets, mix_coeffs, time_decay[None], time_first[None]]
    n_vectors = sum(x.shape[0] for x in small)

    def prepare(key, value, recept, output, gate, cross, raw, ids, *small):
        b, z, core = places()
        device = b * cols + z * 2 + core
        lane = lax.broadcasted_iota(jnp.int32, (own, width), 1)
        home = (lane == device * own + row_index((own, width))).astype(FULL).astype(LOW)
        placed = jnp.zeros((16, width), FULL)
        at = 0
        for x in small:
            x = dot(x, home)
            for i in range(x.shape[0]):
                placed = jnp.where(row_index(placed.shape) == at, x[i : i + 1], placed)
                at += 1
        blocks = [cross[:, j * part_width : (j + 1) * part_width] for j in range(rows)]
        ids = ids.astype(FULL)
        last = raw[length - 16 :].astype(FULL)[15:16]
        edge = stack_rows([last, jnp.broadcast_to(ids[:, length - 1 :], (1, width))], 16)
        return (
            [
                jnp.concatenate([key, value, placed.astype(LOW)], axis=0),
                jnp.concatenate([recept, output, gate], axis=0),
                edge,
                jnp.broadcast_to(ids, (LANES, length)).T,
            ]
            + [pick(blocks, b ^ k) for k in range(rows)]
        )

    first_pack, second_pack, edge, ids_lanes, *crossing = fuse(
        prepare,
        [((2 * own + 16, width), LOW), ((3 * own, width), LOW), ((16, width), FULL), narrow]
        + [((own, part_width), LOW)] * rows,
        key_weight,
        value_weight,
        recept_weight,
        output_weight,
        channel_recept,
        channel_key,
        raw,
        segment_ids,
        *small,
        plain=plain,
        fetch=True,
        limit=58,
    )
    deep_got = [to_depth(first_pack, k) for k in range(1, depth)]
    cross_got = [to_batch(crossing[k], k) for k in range(1, rows)]
    edge = send_next(edge)

    def begin(raw, edge, ids):
        b, z, core = places()
        place = lax.broadcasted_iota(jnp.int32, (1, width), 1)
        block, row = place >> log2(own), place & (own - 1)
        k_core = block >> log2(rows * depth)
        k_batch = (block >> log2(depth)) & (rows - 1)
        k_depth = block & (depth - 1)
        target = ((k_batch ^ b) << log2(cols)) + ((k_depth ^ z) << 1) + (k_core ^ core)
        feature = (target << log2(own)) + row
        order = jnp.concatenate(
            [
                (row_index((LANES, width)) + i * LANES == feature).astype(FULL).astype(LOW)
                for i in range(width // LANES)
            ],
            axis=0,
        )
        unit, scale = unit_norm(dot(raw, order))
        edge_unit = unit_norm(dot(edge.astype(LOW), order))[0]
        before = jnp.where((z == 0) & (core == 0), -1.0, edge[1:2])
        before_lanes = before[:, :LANES]
        last = ids[length - 1 : length]
        keep = (ids == down(ids, before_lanes, plain)).astype(FULL)
        opened = (ids == before_lanes).astype(FULL)
        closing = (ids == last).astype(FULL)
        last = jnp.broadcast_to(last[:, :1], (1, width))
        scale = jnp.broadcast_to(scale, (length, LANES))
        return (
            order,
            unit,
            keep,
            jnp.concatenate([keep, opened, closing, scale], axis=1),
            stack_rows([edge_unit[0:1], last, before]),
        )

    order, unit_one, keep, statics, edges = fuse(
        begin,
        [square, full_act, narrow, ((length, 4 * LANES), FULL), edge_row],
        raw,
        edge,
        ids_lanes,
        plain=plain,
    )

    def deepen_first(second, *x):
        vectors = sum(y[2 * own :].astype(FULL) for y in x).astype(LOW)
        parts = [y[i * own : (i + 1) * own] for i in range(2) for y in x]
        return jnp.concatenate(parts + [vectors], axis=0), second

    first_deep, second_pack = fuse(
        deepen_first,
        [((2 * depth * own + 16, width), LOW), (second_pack.shape, LOW)],
        second_pack,
        first_pack,
        *deep_got,
        after=(order, *cross_got),
        plain=plain,
    )
    first_wide = [to_batch(first_deep, k) for k in range(1, rows)]
    first_pieces = [first_deep] + first_wide
    first_pieces = first_pieces + [to_core(piece) for piece in first_pieces]
    second_got = [to_depth(second_pack, k) for k in range(1, depth)]

    cross_rows = rows * own * part_width // width
    packed_rows = cross_rows + channel_value.shape[0]

    def deepen(value, *x):
        b = places()[0]
        cross, x = x[:rows], x[rows:]
        cross = jnp.concatenate([pick(cross, j ^ b) for j in range(rows)], axis=0)
        return (
            jnp.stack([y[: 2 * own] for y in x]),
            jnp.stack([y[2 * own :] for y in x]),
            jnp.concatenate([cross.reshape(cross_rows, width), value], axis=0),
        )

    second_deep, third_deep, channel_pack = fuse(
        deepen,
        [
            ((depth, 2 * own, width), LOW),
            ((depth, own, width), LOW),
            ((packed_rows, width), LOW),
        ],
        channel_value,
        crossing[0],
        *cross_got,
        second_pack,
        *second_got,
        after=first_wide,
        plain=plain,
    )
    channel_pack = lax.all_gather(channel_pack, "seq", axis=0, tiled=True)

    def unpack_channel(x):
        x = x.reshape(cols, packed_rows, width)
        key = x[:, :cross_rows].reshape(cols, rows, own, part_width)
        key = jnp.concatenate(
            [key[j, i] for i in range(rows) for j in range(cols)], axis=0
        )
        return key, x[:, cross_rows:].reshape(part_width, width)

    part_key, part_value = fuse(
        unpack_channel,
        [((width, part_width), LOW), ((part_width, width), LOW)],
        channel_pack,
        plain=plain,
    )

    second_wide = [to_batch(second_deep, k) for k in range(1, rows)]
    (third_deep,) = fuse(
        lambda x: (x,), [(third_deep.shape, LOW)], third_deep, after=second_wide, plain=plain
    )
    third_wide = [to_batch(third_deep, k) for k in range(1, rows)]

    def joined(deep, wide, after):
        (mine,) = fuse(
            lambda *x: (jnp.concatenate(x, axis=0),),
            [((rows * depth,) + deep.shape[1:], LOW)],
            deep,
            *wide,
            after=after,
            plain=plain,
        )
        return mine, to_core(mine)


    def gathered(pieces, start):
        return jnp.concatenate(
            [piece[:, start : start + own].reshape(-1, width) for piece in pieces], axis=0
        )

    def front(unit, statics, edges, order, *pieces):
        height = depth * own
        vectors = sum(piece[2 * height :].astype(FULL) for piece in pieces)
        lines = dot(vectors.astype(LOW), order)
        normed = unit * lines[0:1] + lines[2:3]
        edge_normed = edges[0:1] * lines[0:1] + lines[2:3]
        prior = down(normed, edge_normed, plain) * statics[:, :1]
        mix_key = mixing(normed, prior, lines[4:5])
        mix_value = mixing(normed, prior, lines[5:6])
        mix_recept = mixing(normed, prior, lines[6:7])
        key_all = jnp.concatenate([piece[:height] for piece in pieces], axis=0)
        value_all = jnp.concatenate([piece[height : 2 * height] for piece in pieces], axis=0)
        key, value = dot(mix_key, key_all), dot(mix_value, value_all)
        pace = jnp.exp(vectors[9:10])
        left = length - 1.0 - row_index((length, width)).astype(FULL)
        den = jnp.where(statics[:, 2 * LANES : 2 * LANES + 1] > 0.5, jnp.exp(key - pace * left), 0.0)
        num = den * value
        message = stack_rows(
            [column_sum(num), column_sum(den), column_sum(num * left), column_sum(den * left)]
            + [edges[1:2], edges[2:3]]
        )
        return (
            jnp.concatenate([vectors, lines], axis=0),
            normed - prior,
            jnp.stack([mix_key, mix_value, mix_recept]),
            jnp.stack([key_all, value_all]),
            key,
            value,
            message,
            jnp.stack([to_lanes(jnp.exp(-pace)), to_lanes(vectors[10:11])]),
        )

    (
        vectors,
        difference_one,
        mixes,
        first_all,
        key_act,
        value_act,
        message,
        rates,
    ) = fuse(
        front,
        [
            ((32, width), FULL),
            full_act,
            ((3, length, width), LOW),
            ((2, width, width), LOW),
            full_act,
            full_act,
            edge_row,
            ((2, width // LANES, LANES), FULL),
        ],
        unit_one,
        statics,
        edges,
        order,
        *first_pieces,
        plain=plain,
        limit=32,
    )
    other, chip = carry_chip(message, vectors, length, True, plain)
    got = carry_steps(chip, vectors, length, True, plain)
    carry = carry_end([message, other, vectors] + got, length, True, plain)

    def receptance(mixes, *pieces):
        recept_all = gathered(pieces, 0)
        return jax.nn.sigmoid(dot(mixes[2], recept_all)), recept_all, gathered(pieces, own)

    recept_act, recept_all, output_all = fuse(
        receptance,
        [full_act, square, square],
        mixes,
        *joined(second_deep, second_wide, (carry,)),
        plain=plain,
        limit=32,
    )
    key_tiles, value_tiles = to_tiles(key_act), to_tiles(value_act)
    scanned = run_forward(keep, key_tiles, value_tiles, rates, carry)

    def attend(scanned, recept, order, output_all, raw, vectors):
        gated = dot((recept * untile(scanned[0], width // LANES)).astype(LOW), order).astype(LOW)
        middle = raw.astype(FULL) + dot(gated, output_all)
        unit, scale = unit_norm(middle)
        normed = unit * vectors[1:2] + vectors[3:4]
        return (
            gated,
            middle,
            jnp.concatenate([unit, jnp.broadcast_to(scale, (length, LANES))], axis=1),
            stack_rows([normed[length - 1 :]]),
        )

    gated, middle, unit_two, edge_two = fuse(
        attend,
        [low_act, full_act, ((length, width + LANES), FULL), edge_row],
        scanned,
        recept_act,
        order,
        output_all,
        raw,
        vectors,
        plain=plain,
    )
    edge_two = send_next(edge_two)

    def mix_two(unit, edge, statics, vectors):
        normed = unit[:, :width] * vectors[1:2] + vectors[3:4]
        prior = down(normed, edge[0:1], plain) * statics[:, :1]
        return (
            mixing(normed, prior, vectors[7:8]),
            mixing(normed, prior, vectors[8:9]),
            normed - prior,
        )

    mix_hidden, mix_gate, difference_two, mixed_token = fuse(
        mix_two, [low_act, low_act, full_act], unit_two, edge_two, statics, vectors, plain=plain, token=True
    )
    shared = [mix_hidden] + [to_batch(mix_hidden, k) for k in range(1, rows)]

    def channel(x, key, value):
        positive = jnp.maximum(dot(x, key), 0.0)
        squared = (positive * positive).astype(LOW)
        return squared, dot(squared, value)

    def channel_low(x, key, value):
        squared, out = channel(x, key, value)
        return squared, out.astype(LOW)

    hidden_act = ((length, part_width), LOW)
    squares, returned = [], []
    for k in range(rows):
        squared, out = fuse(
            channel_low if k else channel,
            [hidden_act, low_act if k else full_act],
            shared[k],
            part_key,
            part_value,
            plain=plain,
        )
        squares.append(squared)
        returned.append(to_batch(out, k) if k else out)

    def gating(mix, order, gated, mixes, *pieces):
        gate_all = gathered(pieces, 0)
        mix = dot(mix, order).astype(LOW)
        sides = jnp.stack([mixes[0], mixes[1], mixes[2], gated, mix])
        return jax.nn.sigmoid(dot(mix, gate_all)), sides, gate_all

    gate, sides, gate_all = fuse(
        gating,
        [full_act, ((5, length, width), LOW), square],
        mix_gate,
        order,
        gated,
        mixes,
        *joined(third_deep, third_wide, (mixed_token,)),
        plain=plain,
    )

    def finish(own_part, gate, middle, grad_out, *got):
        out = sum((x.astype(FULL) for x in got), own_part)
        grad_out = grad_out.astype(FULL)
        return (
            (middle + gate * out).astype(LOW),
            (grad_out * gate).astype(LOW),
            (grad_out * out * gate * (1.0 - gate)).astype(LOW),
        )

    block_output, grad_values, grad_gate = fuse(
        finish,
        [low_act, low_act, low_act],
        returned[0],
        gate,
        middle,
        cotangent,
        *returned[1:],
        plain=plain,
    )

    shared_grad = [grad_values] + [to_batch(grad_values, k) for k in range(1, rows)]

    def channel_back(grad, squared, key, value):
        positive = jnp.sqrt(squared.astype(FULL))
        hidden = (dot_back(grad, value) * 2.0 * positive).astype(LOW)
        return hidden, dot_back(hidden, key)

    def channel_back_low(grad, squared, key, value):
        hidden, out = channel_back(grad, squared, key, value)
        return hidden, out.astype(LOW)

    def channel_back_own(grad, squared, key, value, grad_gate, gate_all, order):
        hidden, out = channel_back(grad, squared, key, value)
        return hidden, out, restore(dot_back(grad_gate, gate_all), order)

    hidden, out, grad_mix_gate = fuse(
        channel_back_own,
        [hidden_act, full_act, full_act],
        shared_grad[0],
        squares[0],
        part_key,
        part_value,
        grad_gate,
        gate_all,
        order,
        plain=plain,
    )
    hiddens, returned = [hidden], [out]
    for k in range(1, rows):
        hidden, out = fuse(
            channel_back_low,
            [hidden_act, low_act],
            shared_grad[k],
            squares[k],
            part_key,
            part_value,
            plain=plain,
        )
        hiddens.append(hidden)
        returned.append(to_batch(out, k))

    def paired(active, active_got, grad, grad_got):
        return dot_rows(
            jnp.concatenate([active[:, :half], active_got[:, half:]], axis=0),
            jnp.concatenate([grad, grad_got], axis=0),
        ).astype(LOW)

    def cut(terms):
        part = half // rows
        return [
            jnp.concatenate([term[k * part : (k + 1) * part] for term in terms], axis=0)
            for k in range(rows)
        ]

    def early_terms(sides, sides_got, grads, grads_got):
        return cut(
            [
                paired(sides[side], sides_got[side], grads[i], grads_got[i])
                for i, side in enumerate((3, 2, 4))
            ]
        )

    sides_got = to_core(sides)

    def unmix_two(own_part, grad_gate, difference, statics, vectors, *got):
        grad_hidden = sum((x.astype(FULL) for x in got), own_part)
        mix_h, mix_g = vectors[7:8], vectors[8:9]
        passed = (grad_hidden * (1.0 - mix_h) + grad_gate * (1.0 - mix_g)) * statics[:, :1]
        return (
            grad_hidden * mix_h + grad_gate * mix_g,
            passed,
            stack_rows([passed[0:1]]),
            stack_rows([column_sum(grad_hidden * difference), column_sum(grad_gate * difference)]),
        )

    own_two, passed_two, after_two, mix_sums_two = fuse(
        unmix_two,
        [full_act, full_act, edge_row, edge_row],
        returned[0],
        grad_mix_gate,
        difference_two,
        statics,
        vectors,
        *returned[1:],
        plain=plain,
    )
    after_two = send_back(after_two)

    def middle_back(
        own_part, passed, after, unit, grad_out, vectors, mix_sums, recept, scanned,
        output_all, order, statics, edges, grad_gate,
    ):
        wkv, inverse, slope = (untile(scanned[i], width // LANES) for i in range(3))
        unit, scale = unit[:, :width], unit[:, width : width + 1]
        grad_normed = own_part + up(passed, after[0:1], plain)
        part = norm_backward(grad_normed, unit, scale, vectors[1:2])
        grad_middle = grad_out.astype(FULL) + part
        grad_low = grad_middle.astype(LOW)
        grad_gated = restore(dot_back(grad_low, output_all), order)
        grad_wkv = grad_gated * recept
        grad_recept = (grad_wkv * wkv * (1.0 - recept)).astype(LOW)
        share = grad_wkv * inverse
        pace = jnp.exp(vectors[9:10])
        step = row_index((length, width)).astype(FULL)
        head = jnp.where(statics[:, LANES : LANES + 1] > 0.5, share * jnp.exp(-pace * step), 0.0)
        return (
            grad_middle,
            jnp.stack([grad_low, grad_recept, grad_gate]),
            share,
            stack_rows([column_sum(head), column_sum(head * wkv), edges[1:2], edges[2:3]]),
            stack_rows(
                [
                    column_sum(grad_normed * unit),
                    column_sum(grad_normed),
                    mix_sums[0:1],
                    mix_sums[1:2],
                    -pace * column_sum(grad_wkv * slope),
                ]
            ),
        )

    grad_middle, grad_three, share, message, sums_two = fuse(
        middle_back,
        [full_act, ((3, length, width), LOW), full_act, edge_row, edge_row],
        own_two,
        passed_two,
        after_two,
        unit_two,
        cotangent,
        vectors,
        mix_sums_two,
        recept_act,
        scanned,
        output_all,
        order,
        statics,
        edges,
        grad_gate,
        plain=plain,
        limit=24,
    )

    other, chip_back = carry_chip(message, vectors, length, False, plain)

    *early, early_token = fuse(
        early_terms,
        [((3 * half // rows, width), LOW)] * rows,
        sides,
        sides_got,
        grad_three,
        to_core(grad_three),
        after=(chip_back,),
        plain=plain,
        token=True,
    )
    carry_parts = [message, other, vectors] + carry_steps(
        chip_back, vectors, length, False, plain, (early_token,)
    )
    early_got = [to_batch(early[k], k) for k in range(1, rows)]
    def channel_terms(*x):
        shared, hiddens, squares, grads = (
            jnp.concatenate(x[i * rows : (i + 1) * rows], axis=0) for i in range(4)
        )
        key = dot_rows(shared, hiddens).astype(LOW)
        value = dot_rows(squares, grads).astype(LOW)
        key = key.reshape(rows, cols, own, part_width)
        value_rows = part_width // cols
        parts = []
        for j in range(cols):
            block = jnp.concatenate([key[i, j] for i in range(rows)], axis=0)
            parts += [
                block.reshape(cross_rows, width),
                value[j * value_rows : (j + 1) * value_rows],
            ]
        return (jnp.concatenate(parts, axis=0),)

    channel_term, channel_token = fuse(
        channel_terms,
        [((cols * packed_rows, width), LOW)],
        *shared,
        *hiddens,
        *squares,
        *shared_grad,
        after=(early_token,),
        plain=plain,
        token=True,
        limit=12,
    )
    channel_sum = lax.psum_scatter(channel_term, "seq", scatter_dimension=0, tiled=True)
    carry_back = carry_end(carry_parts, length, False, plain, (channel_token, early_token))
    grad_key, grad_value, first_term = run_backward(
        keep, key_tiles, value_tiles, scanned, to_tiles(share), rates, carry_back
    )

    def lower(key, value):
        return (jnp.stack([key.astype(LOW), value.astype(LOW)]),)

    (grad_late,) = fuse(
        lower,
        [((2, length, width), LOW)],
        *lax.optimization_barrier((from_tiles(grad_key, width), from_tiles(grad_value, width))),
        plain=plain,
    )

    def unmix_one(grads, grad_three, first_all, recept_all, vectors, statics, difference, order):
        lines = vectors[16:]
        grad_key = dot_back(grads[0], first_all[0])
        grad_value = dot_back(grads[1], first_all[1])
        grad_recept = dot_back(grad_three[1], recept_all)
        m_key, m_value, m_recept = lines[4:5], lines[5:6], lines[6:7]
        passed = (
            grad_key * (1.0 - m_key) + grad_value * (1.0 - m_value) + grad_recept * (1.0 - m_recept)
        ) * statics[:, :1]
        return (
            grad_key * m_key + grad_value * m_value + grad_recept * m_recept,
            passed,
            restore(passed[:16], order)[:SUBS],
            stack_rows([column_sum(x * difference) for x in (grad_key, grad_value, grad_recept)]),
        )

    own_one, passed_one, after_one, mix_sums_one = fuse(
        unmix_one,
        [full_act, full_act, edge_row, edge_row],
        grad_late,
        grad_three,
        first_all,
        recept_all,
        vectors,
        statics,
        difference_one,
        order,
        plain=plain,
        limit=24,
    )
    after_one = send_back(after_one)

    def input_back(
        own_part, passed, after, unit, statics, vectors, order, grad_middle, mix_sums, sums_two, first
    ):
        lines, scale = vectors[16:], statics[:, 3 * LANES : 3 * LANES + 1]
        after = jnp.where(row_index((16, width)) == 0, after[0:1], 0.0)
        grad_normed = own_part + up(passed, restore_in(after, order)[0:1], plain)
        part = norm_backward(grad_normed, unit, scale, lines[0:1])
        ordered = stack_rows(
            [
                column_sum(grad_normed * unit),
                column_sum(grad_normed),
                mix_sums[0:1],
                mix_sums[1:2],
                mix_sums[2:3],
            ],
            16,
        )
        ordered = restore(ordered, order)
        total = [ordered[0:1], sums_two[0:1], ordered[1:2], sums_two[1:2]]
        total += [ordered[2:3], ordered[3:4], ordered[4:5], sums_two[2:3], sums_two[3:4]]
        total += [sums_two[4:5], from_lanes(first)]
        return grad_middle + restore(part, order), stack_rows(total, 16)

    input_grad, sums = fuse(
        input_back,
        [full_act, ((16, width), FULL)],
        own_one,
        passed_one,
        after_one,
        unit_one,
        statics,
        vectors,
        order,
        grad_middle,
        mix_sums_one,
        sums_two,
        first_term,
        plain=plain,
        limit=24,
    )
    sums = sums + to_core(sums)
    *early_pieces, early_wide_token = add_batch(early[0], early_got, 3, plain, (sums,))
    early_half = None
    if depth == 4:
        *early_pieces, early_half = halve_depth(early_pieces, plain)

    def late_terms(sides, sides_got, grads, grads_got, sums):
        b = places()[0]
        terms = [paired(sides[i], sides_got[i], grads[i], grads_got[i]) for i in range(2)]
        columns = width // rows
        return [
            jnp.concatenate(
                [x, pack_vectors(columns_at(sums, (b ^ k) * columns, columns, plain), width)], axis=0
            )
            for k, x in enumerate(cut(terms))
        ]

    late = fuse(
        late_terms,
        [((2 * half // rows + 16, width), LOW)] * rows,
        sides,
        sides_got,
        grad_late,
        to_core(grad_late),
        sums,
        after=(early_wide_token,),
        plain=plain,
    )
    late_got = [to_batch(late[k], k) for k in range(1, rows)]
    def own_columns(x):
        return [x[0:2, :own], x[2:4, :own], x[4:9, :own], x[9:10, :own], x[10:11, :own]]

    late_own, late_sums, *late_pieces, late_token = add_batch(
        late[0], late_got, 2, plain, (early_half,), vectors=sums
    )
    output_grad, recept_grad, gate_grad = add_depth(
        early_pieces[0], early_pieces[1:], 3, own, plain
    )
    key_grad, value_grad, gains_grad, offsets_grad, mixes_grad, decay_grad, first_grad = add_depth(
        late_own,
        late_pieces,
        2,
        own,
        plain,
        late_sums,
        [((2, own), FULL), ((2, own), FULL), ((5, own), FULL), ((1, own), FULL), ((1, own), FULL)],
        own_columns,
    )

    (crossed,) = fuse(
        lambda x: (x[:cross_rows].reshape(rows, own, part_width),),
        [((rows, own, part_width), LOW)],
        channel_sum,
        after=(late_token,),
        plain=plain,
    )
    crossed = lax.all_to_all(crossed, "batch", 0, 0)

    def assemble(x, crossed):
        return (
            jnp.concatenate([crossed[j].astype(FULL) for j in range(rows)], axis=1),
            x[cross_rows:].astype(FULL),
        )

    channel_key_grad, channel_value_grad = fuse(
        assemble,
        [((own, hidden_width), FULL), (channel_value.shape, FULL)],
        channel_sum,
        crossed,
        plain=plain,
    )
    return (
        block_output[None],
        input_grad[None],
        key_grad,
        value_grad,
        recept_grad,
        output_grad,
        channel_key_grad,
        channel_value_grad,
        gate_grad,
        gains_grad,
        offsets_grad,
        mixes_grad,
        decay_grad[0],
        first_grad[0],
    )


def solution(mesh):
    tokens = P("batch", "seq", None)
    weight = P(BOTH, None)
    lines = P(None, BOTH)
    return jax.shard_map(
        per_device,
        mesh=mesh,
        in_specs=(tokens, P("batch", "seq"), tokens)
        + (weight,) * 7
        + (lines,) * 3
        + (P(BOTH),) * 2,
        out_specs=(tokens, tokens) + (weight,) * 7 + (lines,) * 3 + (P(BOTH),) * 2,
        check_vma=False,
    )
```
